128 devices in a mesh: row: 8 (over z, core), leaf: 16 (over y, x).
Axes of the slice: x: 4, y: 4, z: 4, core: 2. Of those that a mesh axis runs over, the one named last changes fastest.
Arguments:
- leaf_update: float32 [16384, 256], P(('leaf', 'row')), may hold values from -6 to 6
- rhs: float32 [3, 16384, 256], P(None, ('leaf', 'row')), may hold values from -6 to 6
- inv_top: bfloat16 [2, 16384, 16, 8, 128], P(None, 'leaf', None, 'row'), may hold values from -0.03125 to 0.03125
- inv_mid: bfloat16 [2, 16384, 8, 8, 128], P(None, 'leaf', None, 'row'), may hold values from -0.046875 to 0.046875
- inv_low: bfloat16 [2, 16384, 4, 8, 128], P(None, 'leaf', None, 'row'), may hold values from -0.0625 to 0.0625
- couple_mid: bfloat16 [2, 16384, 8, 8, 128], P(None, 'leaf', None, 'row'), may hold values from -0.046875 to 0.046875
- couple_low: bfloat16 [2, 16384, 4, 8, 128], P(None, 'leaf', None, 'row'), may hold values from -0.0625 to 0.0625
- block_map: int32 [3, 128], P(None, ('leaf', 'row')), may hold values from 0 to 127, as said below
Outputs:
- solution: float32 [3, 16384, 256], P(None, ('leaf', 'row'))
- leaf_solution: float32 [16384, 256], P(('leaf', 'row'))
The draws below stay inside these ranges and needn't reach their ends.
Inputs may be any that keep to these rules, and one draw needn't show every extreme that they name: Device d of the group of a front holds rows d * 128 to (d + 1) * 128 - 1 of the front's separator part and the same rows of its update part, with d = p * 8 + r for group position p (leaf index modulo the group size) and row index r. block_map[k] is one to one within each parent, and a block held at row index r and group position p of a child lands on a parent block held at row index r and group position p or p + (group size of the parent) / 2. At level 0 every parent block receives one block.
All inputs are finite; a program needn't handle non-finite values.
Results may differ from the reference program's by a relative error of at most 0.012.
Values may be sent and summed in bfloat16 or wider, within the bound.
No kernel may reach another device: no remote copies, remote signals or barrier semaphores. Data moves between devices by JAX's collectives and lax.ppermute only.
A program may use at most 128 MiB of HBM per device.

```python
import jax
import jax.numpy as jnp
from jax import lax

S_TOP = 16384
RHS = 128
BLOCK = 128
SLICE_ROWS = 128
BLOCKS_DEV = 1
SEP_MID = 8192
SEP_LOW = 4096
N_ROW = 8
N_LEAF = 16


def draw_block_map(key, part):
    levels = []
    for level_index in range(3):
        fronts = 2 ** level_index
        group_size = N_LEAF // fronts
        half_group = group_size // 2
        blocks_dev = BLOCKS_DEV
        per_side = blocks_dev * (2 if level_index > 0 else 1)
        pool_size = 2 * per_side
        sep_blocks = group_size * N_ROW * blocks_dev
        scores = jax.random.randint(jax.random.fold_in(key, 17 + level_index), (fronts, half_group, N_ROW, pool_size), 0, 1 << 20)
        scores = scores * pool_size + jnp.arange(pool_size, dtype=jnp.int32)
        picked = jnp.argsort(scores, axis=-1)[..., :2 * blocks_dev]
        side_index = picked // per_side
        remainder = picked % per_side
        kind_index = remainder // blocks_dev
        slot_index = remainder % blocks_dev
        position = jnp.arange(half_group, dtype=jnp.int32)[None, :, None, None]
        row_index = jnp.arange(N_ROW, dtype=jnp.int32)[None, None, :, None]
        holder = (side_index * half_group + position) * N_ROW + row_index
        targets = kind_index * sep_blocks + holder * blocks_dev + slot_index
        targets = targets.reshape(fronts, half_group, N_ROW, 2, blocks_dev).transpose(0, 3, 1, 2, 4)
        levels.append(targets.reshape(-1))
    return jnp.stack(levels).astype(jnp.int32)


def level_of(key, extent, split, low, high):
    def one(dim, blocks):
        draws = jax.random.uniform(jax.random.fold_in(jax.random.fold_in(key, 6), dim), (blocks,), jnp.float32, low / len(split), high / len(split))
        return jnp.repeat(jnp.exp(draws), extent[dim] // blocks).reshape((-1,) + (1,) * (len(extent) - dim - 1))

    level = one(*split[0])
    for cut in split[1:]:
        level = level * one(*cut)
    return level


def scatter_about(rng, dims, width, bound, pieces=(), held_as=jnp.bfloat16):
    array = jax.random.normal(rng, dims, jnp.float32) * width
    if len(pieces) > 0:
        array = level_of(rng, dims, pieces, -0.22, 0.18) * array
    return jnp.clip(array, min=-bound, max=bound).astype(held_as)


def setup_inputs(seed: int = 0) -> dict:
    key_list = jax.random.split(jax.random.key(seed), 9)
    return {
        "leaf_update": scatter_about(key_list[0], (S_TOP, 2 * RHS), 1.0, 6.0, ((0, 128),), jnp.float32),
        "rhs": scatter_about(key_list[1], (3, S_TOP, 2 * RHS), 1.0, 6.0, ((1, 128),), jnp.float32),
        "inv_top": scatter_about(key_list[2], (2, S_TOP, N_LEAF, N_ROW, SLICE_ROWS), (2 * S_TOP) ** -0.5, 0.03125, ((1, 16), (3, 8))),
        "inv_mid": scatter_about(key_list[3], (2, S_TOP, N_LEAF // 2, N_ROW, SLICE_ROWS), (2 * SEP_MID) ** -0.5, 0.046875, ((1, 16), (3, 8))),
        "inv_low": scatter_about(key_list[4], (2, S_TOP, N_LEAF // 4, N_ROW, SLICE_ROWS), (2 * SEP_LOW) ** -0.5, 0.0625, ((1, 16), (3, 8))),
        "couple_mid": scatter_about(key_list[5], (2, S_TOP, N_LEAF // 2, N_ROW, SLICE_ROWS), (2 * SEP_MID) ** -0.5, 0.046875, ((1, 16), (3, 8))),
        "couple_low": scatter_about(key_list[6], (2, S_TOP, N_LEAF // 4, N_ROW, SLICE_ROWS), (2 * SEP_LOW) ** -0.5, 0.0625, ((1, 16), (3, 8))),
        "block_map": draw_block_map(jax.random.fold_in(key_list[8], 71), 0),
    }


def complex_apply(real_part, imag_part, vector, transpose):
    half_cols = vector.shape[1] // 2
    right_side = vector.astype(jnp.bfloat16)
    if transpose:
        dim_numbers = (((0,), (0,)), ((), ()))
    else:
        dim_numbers = (((1,), (0,)), ((), ()))
    product_real = lax.dot_general(real_part, right_side, dim_numbers, preferred_element_type=jnp.float32)
    product_imag = lax.dot_general(imag_part, right_side, dim_numbers, preferred_element_type=jnp.float32)
    return jnp.concatenate([product_real[:, :half_cols] - product_imag[:, half_cols:], product_real[:, half_cols:] + product_imag[:, :half_cols]], axis=1)


def parent_index(targets, level_index, front_blocks):
    fronts = 2 ** level_index
    per_child = targets.shape[0] // (2 * fronts)
    parent_of = (jnp.arange(targets.shape[0], dtype=jnp.int32) // per_child) // 2
    return parent_of * front_blocks + targets


def reference(leaf_update, rhs, inv_top, inv_mid, inv_low, couple_mid, couple_low, block_map):
    columns = rhs.shape[2]
    inverses = [inv_top, inv_mid, inv_low]
    couplings = [None, couple_mid, couple_low]
    children = leaf_update
    saved_y = [None, None, None]
    for level_index in [2, 1, 0]:
        fronts = 2 ** level_index
        sep_rows = S_TOP // fronts
        has_update = level_index > 0
        front_blocks = (2 if has_update else 1) * (sep_rows // BLOCK)
        child_blocks = children.reshape(-1, BLOCK, columns)
        placed = parent_index(block_map[level_index], level_index, front_blocks)
        front_vec = jnp.zeros((fronts * front_blocks, BLOCK, columns), jnp.float32).at[placed].add(child_blocks)
        front_vec = front_vec.reshape(fronts, front_blocks * BLOCK, columns)
        sep_part = front_vec[:, :sep_rows] + rhs[level_index].reshape(fronts, sep_rows, columns)
        inverse = inverses[level_index].reshape(2, fronts, sep_rows, sep_rows)
        outputs_y = []
        updates = []
        for front_idx in range(fronts):
            solved = complex_apply(inverse[0, front_idx], inverse[1, front_idx], sep_part[front_idx], False)
            outputs_y.append(solved)
            if has_update:
                coupling = couplings[level_index].reshape(2, fronts, sep_rows, sep_rows)
                updates.append(front_vec[front_idx, sep_rows:] - complex_apply(coupling[0, front_idx], coupling[1, front_idx], solved, False))
        saved_y[level_index] = outputs_y
        if has_update:
            children = jnp.concatenate(updates, axis=0)
    solutions = []
    parent_flat = None
    for level_index in [0, 1, 2]:
        fronts = 2 ** level_index
        sep_rows = S_TOP // fronts
        inverse = inverses[level_index].reshape(2, fronts, sep_rows, sep_rows)
        if level_index > 0:
            parent_blocks = parent_flat.shape[0] // (2 ** (level_index - 1))
            taken_rows = parent_flat[parent_index(block_map[level_index - 1], level_index - 1, parent_blocks)]
            x_update = taken_rows.reshape(fronts, sep_rows, columns)
            coupling = couplings[level_index].reshape(2, fronts, sep_rows, sep_rows)
        level_x = []
        front_vectors = []
        for front_idx in range(fronts):
            reduced = saved_y[level_index][front_idx]
            if level_index > 0:
                reduced = reduced - complex_apply(coupling[0, front_idx], coupling[1, front_idx], x_update[front_idx], True)
            solved = complex_apply(inverse[0, front_idx], inverse[1, front_idx], reduced, True)
            level_x.append(solved)
            if level_index > 0:
                front_vectors.append(jnp.concatenate([solved, x_update[front_idx]], axis=0))
            else:
                front_vectors.append(solved)
        solutions.append(jnp.concatenate(level_x, axis=0))
        parent_flat = jnp.concatenate(front_vectors, axis=0).reshape(-1, BLOCK, columns)
    leaf_blocks = parent_flat[parent_index(block_map[2], 2, parent_flat.shape[0] // 4)]
    return jnp.stack(solutions), leaf_blocks.reshape(S_TOP, columns)
```

```python
import jax
import jax.numpy as jnp
from jax import lax
from jax.sharding import PartitionSpec as P

BF = jnp.bfloat16
F32 = jnp.float32
BLOCK = 128


def swap(value, axis, mask):
    count = lax.axis_size(axis)
    return lax.ppermute(value, axis, [(i, i ^ mask) for i in range(count)])


def pick(blocks, index):
    return lax.dynamic_index_in_dim(blocks, index, 0, keepdims=False)


def in_order(pieces, index_of):
    count = len(pieces)
    out = jnp.zeros((count,) + next(iter(pieces.values())).shape, BF)
    for key, piece in pieces.items():
        out = lax.dynamic_update_index_in_dim(out, piece, index_of(key), 0)
    return out


def panel(weights):
    return weights.reshape(2 * weights.shape[1], weights.shape[2], BLOCK)


def forward(weights, vector):
    rows = weights.shape[1]
    half = vector.shape[-1] // 2
    prod = lax.dot_general(
        panel(weights), vector, (((1, 2), (0, 1)), ((), ())), preferred_element_type=F32
    )
    real, imag = prod[:rows], prod[rows:]
    out = jnp.concatenate(
        [real[:, :half] - imag[:, half:], real[:, half:] + imag[:, :half]], axis=1
    )
    return out.reshape(rows // BLOCK, BLOCK, 2 * half)


def transposed(weights, vector):
    rows = weights.shape[1]
    half = vector.shape[-1] // 2
    flat = vector.reshape(rows, 2 * half)
    turned = jnp.concatenate([-flat[:, half:], flat[:, :half]], axis=1)
    both = jnp.concatenate([flat, turned], axis=0)
    return lax.dot_general(
        panel(weights), both, (((0,), (0,)), ((), ())), preferred_element_type=F32
    )


def shards(leaf_update, rhs, inv_top, inv_mid, inv_low, couple_mid, couple_low, block_map):
    leaf = lax.axis_index("leaf")
    row = lax.axis_index("row")
    core, z = row & 1, row >> 1
    x, y = leaf & 3, leaf >> 2

    def reduce_row(blocks):
        total = None
        for step in (1, 3, 2, 0):
            slot = 2 * (z ^ step)
            other = swap(pick(blocks, slot + 1 - core).astype(BF), "row", 1)
            part = pick(blocks, slot + core) + other.astype(F32)
            if step:
                part = swap(part.astype(BF), "row", 2 * step).astype(F32)
            total = part if total is None else total + part
        return total

    def gather_row(own):
        pieces = {(0, 0): own}
        for step in (1, 3, 2):
            pieces[(step, 0)] = swap(own, "row", 2 * step)
        for step in (0, 1, 3, 2):
            pieces[(step, 1)] = swap(pieces[(step, 0)], "row", 1)
        return in_order(pieces, lambda key: 2 * (z ^ key[0]) + (core ^ key[1]))

    def gather_x(value):
        out = {0: value}
        for step in (1, 3, 2):
            out[step] = swap(value, "leaf", step)
        return out

    def flag(target, slot):
        return (target == slot.astype(F32)).astype(F32)

    tags = block_map.astype(F32)

    def tag_rows(level):
        return jnp.broadcast_to(tags[level].reshape(1, 1).astype(BF), (16, 2 * BLOCK))

    sent = jnp.concatenate([leaf_update.astype(BF), rhs[2].astype(BF), tag_rows(2)], axis=0)
    got = gather_x(sent)
    rhs_y1 = swap(jnp.concatenate([rhs[1].astype(BF), rhs[0].astype(BF), tag_rows(1), tag_rows(0)], 0), "leaf", 4)
    rhs_y3 = swap(jnp.concatenate([rhs[0].astype(BF), tag_rows(0)], 0), "leaf", 12)
    rhs_y2 = swap(jnp.concatenate([rhs[0].astype(BF), tag_rows(0)], 0), "leaf", 8)
    child = {k: got[k][:BLOCK].astype(F32) for k in got}
    goal = {k: got[k][2 * BLOCK, 0].astype(F32) for k in got}
    seps = {}
    for k in got:
        slot = (x ^ k) * 8 + row
        seps[k] = (
            got[k][BLOCK : 2 * BLOCK].astype(F32)
            + flag(goal[k], slot) * child[k]
            + flag(goal[k ^ 2], slot) * child[k ^ 2]
        ).astype(BF)
    slot = x * 8 + row + 32
    update = flag(goal[0], slot) * leaf_update + flag(goal[2], slot) * child[2]
    y_low = reduce_row(forward(inv_low, in_order(seps, lambda k: x ^ k)))
    pieces = gather_x(y_low.astype(BF))
    children = update - reduce_row(forward(couple_low, in_order(pieces, lambda k: x ^ k)))

    y0 = y & 1
    mine = children.astype(BF)
    theirs = swap(mine, "leaf", 4).astype(F32)
    goal_own, goal_other = tags[1, 0], rhs_y1[2 * BLOCK, 0].astype(F32)

    def level_one(base, slot):
        return base + flag(goal_own, slot) * children + flag(goal_other, slot) * theirs

    own_slot = (y0 * 4 + x) * 8 + row
    other_slot = ((y0 ^ 1) * 4 + x) * 8 + row
    sep_own = level_one(rhs[1], own_slot).astype(BF)
    sep_other = level_one(rhs_y1[:BLOCK].astype(F32), other_slot).astype(BF)
    update = level_one(jnp.zeros_like(children), own_slot + 64)

    def gather_eight(own, other):
        pair = jnp.stack([jnp.where(y0 == 0, own, other), jnp.where(y0 == 0, other, own)])
        got = in_order(gather_x(pair), lambda k: x ^ k)
        return jnp.moveaxis(got, 0, 1).reshape(8, BLOCK, 2 * BLOCK)

    y_mid = reduce_row(forward(inv_mid, gather_eight(sep_own, sep_other)))
    own = y_mid.astype(BF)
    vector = gather_eight(own, swap(own, "leaf", 4))
    children = update - reduce_row(forward(couple_mid, vector))

    mine = children.astype(BF)
    stack = {0: children}
    for step in (1, 3, 2):
        stack[step] = swap(mine, "leaf", 4 * step).astype(F32)
    goal = {
        0: tags[0, 0],
        1: rhs_y1[2 * BLOCK + 16, 0].astype(F32),
        3: rhs_y3[BLOCK, 0].astype(F32),
        2: rhs_y2[BLOCK, 0].astype(F32),
    }
    base = {
        0: rhs[0],
        1: rhs_y1[BLOCK : 2 * BLOCK].astype(F32),
        3: rhs_y3[:BLOCK].astype(F32),
        2: rhs_y2[:BLOCK].astype(F32),
    }
    column = {}
    for k in stack:
        slot = ((y ^ k) * 4 + x) * 8 + row
        column[k] = (
            base[k] + flag(goal[k], slot) * stack[k] + flag(goal[k ^ 2], slot) * stack[k ^ 2]
        ).astype(BF)
    column = in_order(column, lambda k: y ^ k)
    vector = in_order(gather_x(column), lambda k: x ^ k)
    vector = jnp.moveaxis(vector, 0, 1).reshape(16, BLOCK, 2 * BLOCK)
    y_top = reduce_row(forward(inv_top, vector))
    partial = transposed(inv_top, gather_row(y_top.astype(BF)))

    blocks = jnp.moveaxis(partial.reshape(4, 4, BLOCK, 2 * BLOCK), 1, 0)
    total = pick(blocks, x)
    for step in (1, 3, 2):
        total = total + swap(pick(blocks, x ^ step).astype(BF), "leaf", step).astype(F32)
    x_own, x_other = pick(total, y), pick(total, y ^ 2)
    for step in (1, 3, 2):
        sent = jnp.concatenate([pick(total, y ^ step), pick(total, y ^ step ^ 2)], 0).astype(BF)
        part = swap(sent, "leaf", 4 * step).astype(F32)
        x_own, x_other = x_own + part[:BLOCK], x_other + part[BLOCK:]
    x_top = x_own
    down_mid = jnp.where(block_map[0, 0] == leaf * 8 + row, x_own, x_other)

    def reduce_x(partial_blocks):
        blocks = jnp.moveaxis(partial_blocks, 1, 0)
        total = pick(blocks, x)
        for step in (1, 3, 2):
            total = total + swap(pick(blocks, x ^ step).astype(BF), "leaf", step).astype(F32)
        return total

    down_own = down_mid.astype(BF)
    partial = transposed(couple_mid, gather_row(down_own)).reshape(2, 4, BLOCK, 2 * BLOCK)
    total = reduce_x(partial)
    coupled = pick(total, y0) + swap(pick(total, y0 ^ 1).astype(BF), "leaf", 4).astype(F32)
    reduced = y_mid - coupled
    partial = transposed(inv_mid, gather_row(reduced.astype(BF))).reshape(2, 4, BLOCK, 2 * BLOCK)
    total = reduce_x(partial)
    x_own, x_other = pick(total, y0), pick(total, y0 ^ 1)
    sent = jnp.concatenate([x_other.astype(BF), x_own.astype(BF), down_own], 0)
    part = swap(sent, "leaf", 4).astype(F32)
    x_mid = x_own + part[:BLOCK]
    x_other = x_other + part[BLOCK : 2 * BLOCK]
    down_other = part[2 * BLOCK :]
    target = block_map[1, 0]
    own_slot = (y0 * 4 + x) * 8 + row
    other_slot = ((y0 ^ 1) * 4 + x) * 8 + row
    down_low = jnp.where(
        target == own_slot,
        x_mid,
        jnp.where(target == own_slot + 64, down_mid, jnp.where(target == other_slot, x_other, down_other)),
    )

    down_own = down_low.astype(BF)
    partial = transposed(couple_low, gather_row(down_own)).reshape(4, BLOCK, 2 * BLOCK)
    coupled = pick(partial, x)
    for step in (1, 3, 2):
        coupled = coupled + swap(pick(partial, x ^ step).astype(BF), "leaf", step).astype(F32)
    reduced = y_low - coupled
    partial = transposed(inv_low, gather_row(reduced.astype(BF))).reshape(4, BLOCK, 2 * BLOCK)
    x_own, x_other = pick(partial, x), pick(partial, x ^ 2)
    for step in (1, 3, 2):
        sent = [pick(partial, x ^ step).astype(BF), pick(partial, x ^ step ^ 2).astype(BF)]
        if step == 2:
            sent.append(down_own)
        part = swap(jnp.concatenate(sent, 0), "leaf", step).astype(F32)
        x_own, x_other = x_own + part[:BLOCK], x_other + part[BLOCK : 2 * BLOCK]
        if step == 2:
            down_other = part[2 * BLOCK :]
    target = block_map[2, 0]
    own_slot = x * 8 + row
    other_slot = (x ^ 2) * 8 + row
    leaf_solution = jnp.where(
        target == own_slot,
        x_own,
        jnp.where(target == own_slot + 32, down_low, jnp.where(target == other_slot, x_other, down_other)),
    )
    return (jnp.stack([x_top, x_mid, x_own]), leaf_solution)


def solution(mesh):
    return jax.shard_map(
        shards,
        mesh=mesh,
        in_specs=(
            P(("leaf", "row"), None),
            P(None, ("leaf", "row"), None),
            P(None, "leaf", None, "row", None),
            P(None, "leaf", None, "row", None),
            P(None, "leaf", None, "row", None),
            P(None, "leaf", None, "row", None),
            P(None, "leaf", None, "row", None),
            P(None, ("leaf", "row")),
        ),
        out_specs=(P(None, ("leaf", "row"), None), P(("leaf", "row"), None)),
        check_vma=False,
    )
```

```python
import functools

import jax
import jax.numpy as jnp
from jax import lax
from jax.experimental import pallas as pl
from jax.experimental.pallas import tpu as pltpu
from jax.sharding import PartitionSpec as P

BF = jnp.bfloat16
F32 = jnp.float32
B = 128
C = 256
STEPS = (1, 3, 2)
X, Y, Z, CORE, ROW, T0, T1, T2 = range(8)
SMALL = 8 << 20
LARGE = 28 << 20


def swap(value, axis, mask):
    count = lax.axis_size(axis)
    return lax.ppermute(value, axis, [(i, i ^ mask) for i in range(count)])


def small(body, outs, scal, *ins):
    return pl.pallas_call(
        body,
        out_shape=[jax.ShapeDtypeStruct(*o) for o in outs],
        in_specs=[pl.BlockSpec(memory_space=pltpu.SMEM)]
        + [pl.BlockSpec(memory_space=pltpu.VMEM)] * len(ins),
        out_specs=[pl.BlockSpec(memory_space=pltpu.VMEM)] * len(outs),
        compiler_params=pltpu.CompilerParams(vmem_limit_bytes=SMALL),
        cost_estimate=pl.CostEstimate(flops=1 << 18, bytes_accessed=1 << 19, transcendentals=0),
    )(scal, *ins)


def relay_body(groups, real_ref, imag_ref, out_ref):
    span = C // groups
    shift = span.bit_length() - 1
    target = lax.broadcasted_iota(jnp.int32, (C, C), 0)
    source = lax.broadcasted_iota(jnp.int32, (C, C), 1)
    place = (source == (target & span - 1) * groups + (target >> shift)).astype(BF)
    for chunk in range(B * groups // C):
        rows = slice(chunk * C, (chunk + 1) * C)
        both = jnp.concatenate([real_ref[rows, :], imag_ref[rows, :]], axis=1)
        moved = jnp.dot(place, both, preferred_element_type=F32).astype(BF)
        for p in range(groups):
            out_ref[chunk * span : (chunk + 1) * span, p * C : (p + 1) * C] = moved[
                p * span : (p + 1) * span
            ]


def relay(weights):
    _, rows, groups, _, width = weights.shape
    flat = weights.reshape(2 * rows * groups, width)
    tiles = rows // B
    return pl.pallas_call(
        functools.partial(relay_body, groups),
        grid=(tiles,),
        out_shape=jax.ShapeDtypeStruct((rows, groups * C), BF),
        in_specs=[
            pl.BlockSpec((B * groups, B), lambda t: (t, 0)),
            pl.BlockSpec((B * groups, B), lambda t: (t + tiles, 0)),
        ],
        out_specs=pl.BlockSpec((B, groups * C), lambda t: (t, 0)),
        compiler_params=pltpu.CompilerParams(vmem_limit_bytes=LARGE),
        cost_estimate=pl.CostEstimate(
            flops=4 * rows * groups * C * B, bytes_accessed=8 * rows * groups * B, transcendentals=0
        ),
    )(flat, flat)


def forward(weights, scal, ins, gather, extras=()):
    rows, depth = weights.shape
    tiles = rows // C
    count = len(ins)

    def body(s, w_ref, *refs):
        in_refs, own_ref, other_ref = refs[:count], refs[count], refs[count + 1]
        extra_refs = refs[count + 2 : -2]
        vec, acc = refs[-2:]

        @pl.when(pl.program_id(0) == 0)
        def _():
            for index, block in gather(s, in_refs, extra_refs):
                start = pl.multiple_of(index * C, C)
                block = block.astype(F32)
                vec[pl.ds(start, B), :] = block.astype(BF)
                vec[pl.ds(start + B, B), :] = jnp.concatenate(
                    [-block[:, B:], block[:, :B]], axis=1
                ).astype(BF)

        prod = jnp.dot(w_ref[...], vec[...], preferred_element_type=F32)
        acc[0] = prod[:B]
        acc[1] = prod[B:]
        own_ref[0] = acc[s[CORE]]
        other_ref[0] = acc[1 - s[CORE]].astype(BF)

    def whole(shape):
        return pl.BlockSpec(shape, lambda t, s: (0,) * len(shape))

    spread = pl.BlockSpec((1, B, C), lambda t, s: (t ^ s[Z], 0, 0))
    return pl.pallas_call(
        body,
        grid_spec=pltpu.PrefetchScalarGridSpec(
            num_scalar_prefetch=1,
            grid=(tiles,),
            in_specs=[pl.BlockSpec((C, depth), lambda t, s: (t, 0))] + [whole(i.shape) for i in ins],
            out_specs=[spread, spread] + [whole(e) for e in extras],
            scratch_shapes=[pltpu.VMEM((depth, C), BF), pltpu.VMEM((2, B, C), F32)],
        ),
        out_shape=[
            jax.ShapeDtypeStruct((tiles, B, C), F32),
            jax.ShapeDtypeStruct((tiles, B, C), BF),
        ]
        + [jax.ShapeDtypeStruct(e, F32) for e in extras],
        compiler_params=pltpu.CompilerParams(vmem_limit_bytes=LARGE),
        cost_estimate=pl.CostEstimate(
            flops=2 * rows * depth * C, bytes_accessed=2 * rows * depth, transcendentals=0
        ),
    )(scal, weights, *ins)


def transposed(weights, scal, pieces, paired=None):
    rows, depth = weights.shape
    tiles = depth // (4 * C)
    ins = list(pieces.values()) + ([] if paired is None else [paired])
    keys = list(pieces)
    count = len(ins)
    planes = {k: 1 if paired is None else 3 if k == 2 else 2 for k in range(4)}

    def body(s, w_ref, *refs):
        in_refs, out_refs, (vec, acc) = refs[:count], refs[count : count + 4], refs[-2:]

        @pl.when(pl.program_id(0) == 0)
        def _():
            for (zz, j), ref in zip(keys, in_refs):
                slot = 2 * (s[Z] ^ zz) + (s[CORE] ^ j)
                vec[:, pl.ds(pl.multiple_of(slot * B, B), B)] = ref[...]

        prod = jnp.dot(vec[...], w_ref[...], preferred_element_type=F32)
        for p in range(4):
            part = prod[:, p * C : (p + 1) * C]
            acc[p, :B] = part[:B, :B] - part[B:, B:]
            acc[p, B:] = part[B:, :B] + part[:B, B:]
        for k in range(4):
            kind = out_refs[k].dtype
            out_refs[k][0] = acc[s[X] ^ k].astype(kind)
            if paired is not None:
                out_refs[k][1] = acc[s[X] ^ k ^ 2].astype(kind)
                if k == 2:
                    out_refs[k][2] = in_refs[-1][...]

    def out_spec(k):
        if paired is None:
            mask = {4: 3, 2: 1, 1: 0}[tiles]
            return pl.BlockSpec((1, C, B), lambda t, s: (t ^ s[Y] & mask, 0, 0))
        return pl.BlockSpec((planes[k], C, B), lambda t, s: (0, 0, 0))

    return pl.pallas_call(
        body,
        grid_spec=pltpu.PrefetchScalarGridSpec(
            num_scalar_prefetch=1,
            grid=(tiles,),
            in_specs=[pl.BlockSpec((rows, 4 * C), lambda t, s: (0, t))]
            + [pl.BlockSpec((C, B), lambda t, s: (0, 0))] * count,
            out_specs=[out_spec(k) for k in range(4)],
            scratch_shapes=[pltpu.VMEM((C, rows), BF), pltpu.VMEM((4, C, B), F32)],
        ),
        out_shape=[
            jax.ShapeDtypeStruct((tiles * planes[k], C, B), BF if k else F32) for k in range(4)
        ],
        compiler_params=pltpu.CompilerParams(vmem_limit_bytes=LARGE),
        cost_estimate=pl.CostEstimate(
            flops=2 * rows * depth * C, bytes_accessed=2 * rows * depth, transcendentals=0
        ),
    )(scal, weights, *ins)


def same(goal, slot):
    return (goal == slot.astype(F32)).astype(F32)


def shards(leaf_update, rhs, inv_top, inv_mid, inv_low, couple_mid, couple_low, block_map):
    leaf = lax.axis_index("leaf")
    row = lax.axis_index("row")
    scal = jnp.concatenate(
        [jnp.stack([leaf & 3, leaf >> 2, row >> 1, row & 1, row]).astype(jnp.int32), block_map[:, 0]]
    )

    def reduce_row(own, other, tail, outs, *ins):
        other = swap(other, "row", 1)

        def split(s, own_ref, other_ref, *out_refs):
            for k, ref in enumerate(out_refs):
                ref[...] = (own_ref[k] + other_ref[k].astype(F32)).astype(ref.dtype)

        parts = small(
            split, [((B, C), F32)] + [((B, C), BF)] * 3, scal, own, other
        )
        got = [swap(parts[k], "row", 2 * k) for k in STEPS]

        def body(s, *refs):
            total = refs[0][...]
            for ref in refs[1:4]:
                total = total + ref[...].astype(F32)
            tail(s, total, *refs[4:])

        return small(body, outs, scal, parts[0], *got, *ins)

    def gather_row(own):
        pieces = {(0, 0): own}
        for k in STEPS:
            pieces[(k, 0)] = swap(own, "row", 2 * k)
        for k in (0,) + STEPS:
            pieces[(k, 1)] = swap(pieces[(k, 0)], "row", 1)
        return pieces

    def gather_x(value):
        return [value] + [swap(value, "leaf", k) for k in (1, 2, 3)]

    def send(s, leaf_ref, rhs_ref, low_ref, y1_ref, y3_ref):
        def tag(level):
            return jnp.full((16, C), s[T0 + level].astype(F32), F32).astype(BF)

        low_ref[:B] = leaf_ref[...].astype(BF)
        low_ref[B : 2 * B] = rhs_ref[2].astype(BF)
        low_ref[2 * B :] = tag(2)
        y1_ref[:B] = rhs_ref[1].astype(BF)
        y1_ref[B : 2 * B] = rhs_ref[0].astype(BF)
        y1_ref[2 * B : 2 * B + 16] = tag(1)
        y1_ref[2 * B + 16 :] = tag(0)
        y3_ref[:B] = rhs_ref[0].astype(BF)
        y3_ref[B:] = tag(0)

    low, to_y1, to_y3 = small(
        send,
        [((2 * B + 16, C), BF), ((2 * B + 32, C), BF), ((B + 16, C), BF)],
        scal,
        leaf_update,
        rhs,
    )
    got = gather_x(low)
    from_y1 = swap(to_y1, "leaf", 4)
    from_y3 = swap(to_y3, "leaf", 12)
    from_y2 = swap(to_y3, "leaf", 8)
    w_low, b_low, w_mid, b_mid, w_top = [
        relay(w) for w in (inv_low, couple_low, inv_mid, couple_mid, inv_top)
    ]

    def gather_low(s, refs, extra):
        goal = [r[2 * B : 2 * B + 16, :].astype(F32)[:1] for r in refs]
        child = [r[:B, :].astype(F32) for r in refs]
        slot = (s[X] + 4) * 8 + s[ROW]
        extra[0][...] = same(goal[0], slot) * child[0] + same(goal[2], slot) * child[2]
        for k in range(4):
            slot = (s[X] ^ k) * 8 + s[ROW]
            yield s[X] ^ k, (
                refs[k][B : 2 * B, :].astype(F32)
                + same(goal[k], slot) * child[k]
                + same(goal[k ^ 2], slot) * child[k ^ 2]
            )

    own, other, update = forward(w_low, scal, got, gather_low, [(B, C)])

    def keep(s, total, full_ref, half_ref):
        full_ref[...] = total
        half_ref[...] = total.astype(BF)

    pair_outs = [((B, C), F32), ((B, C), BF)]
    y_low, half = reduce_row(own, other, keep, pair_outs)

    def gather_plain(s, refs, extra):
        for k in range(4):
            yield s[X] ^ k, refs[k][...]

    own, other = forward(b_low, scal, gather_x(half), gather_plain)

    def less(s, total, up_ref, full_ref, half_ref):
        keep(s, up_ref[...] - total, full_ref, half_ref)

    children, half = reduce_row(own, other, less, pair_outs, update)

    theirs = swap(half, "leaf", 4)

    def extend_mid(s, own_ref, other_ref, rhs_ref, y1_ref, pair_ref, up_ref):
        position = (s[Y] & 1) * 4 + s[X]
        goal_own = jnp.full((1, C), s[T1].astype(F32), F32)
        goal_other = y1_ref[2 * B : 2 * B + 16, :].astype(F32)[:1]

        def landed(slot):
            return same(goal_own, slot) * own_ref[...] + same(goal_other, slot) * other_ref[
                ...
            ].astype(F32)

        slot = position * 8 + s[ROW]
        pair_ref[0] = (rhs_ref[1] + landed(slot)).astype(BF)
        up_ref[...] = landed(slot + 64)
        slot = (position ^ 4) * 8 + s[ROW]
        pair_ref[1] = (y1_ref[:B, :].astype(F32) + landed(slot)).astype(BF)

    pair, update = small(
        extend_mid, [((2, B, C), BF), ((B, C), F32)], scal, children, theirs, rhs, from_y1
    )

    def gather_mid(s, refs, extra):
        for k in range(4):
            for j in range(2):
                yield ((s[Y] & 1) ^ j) * 4 + (s[X] ^ k), refs[k][j]

    own, other = forward(w_mid, scal, gather_x(pair), gather_mid)
    y_mid, half = reduce_row(own, other, keep, pair_outs)

    def join(s, a_ref, b_ref, out_ref):
        out_ref[0] = a_ref[...]
        out_ref[1] = b_ref[...]

    (pair,) = small(join, [((2, B, C), BF)], scal, half, swap(half, "leaf", 4))
    own, other = forward(b_mid, scal, gather_x(pair), gather_mid)
    children, half = reduce_row(own, other, less, pair_outs, update)

    moved = [swap(half, "leaf", 4 * k) for k in STEPS]

    def extend_top(s, own_ref, m1, m3, m2, rhs_ref, y1_ref, y3_ref, y2_ref, out_ref):
        child = [own_ref[...], m1[...].astype(F32), m2[...].astype(F32), m3[...].astype(F32)]
        base = [rhs_ref[0], y1_ref[B : 2 * B, :], y2_ref[:B, :], y3_ref[:B, :]]
        goal = [
            jnp.full((1, C), s[T0].astype(F32), F32),
            y1_ref[2 * B + 16 : 2 * B + 32, :].astype(F32)[:1],
            y2_ref[B : B + 16, :].astype(F32)[:1],
            y3_ref[B : B + 16, :].astype(F32)[:1],
        ]
        for k in range(4):
            slot = ((s[Y] ^ k) * 4 + s[X]) * 8 + s[ROW]
            out_ref[k] = (
                base[k].astype(F32)
                + same(goal[k], slot) * child[k]
                + same(goal[k ^ 2], slot) * child[k ^ 2]
            ).astype(BF)

    (column,) = small(
        extend_top, [((4, B, C), BF)], scal, children, *moved, rhs, from_y1, from_y3, from_y2
    )

    def gather_top(s, refs, extra):
        for k in range(4):
            for j in range(4):
                yield (s[Y] ^ j) * 4 + (s[X] ^ k), refs[k][j]

    own, other = forward(w_top, scal, gather_x(column), gather_top)

    def turn(s, total, out_ref):
        out_ref[...] = total.T.astype(BF)

    turned = [((C, B), BF)]
    (half,) = reduce_row(own, other, turn, turned)
    parts = transposed(w_top, scal, gather_row(half))
    got = [swap(parts[k], "leaf", k) for k in STEPS]

    def sum_top(s, own_ref, a, b, c, pair_ref, m1, m3, m2):
        total = [
            own_ref[j] + a[j].astype(F32) + b[j].astype(F32) + c[j].astype(F32) for j in range(4)
        ]
        pair_ref[0] = total[0]
        pair_ref[1] = total[2]
        for k, ref in zip(STEPS, (m1, m3, m2)):
            ref[0] = total[k].astype(BF)
            ref[1] = total[k ^ 2].astype(BF)

    pair, *sent = small(
        sum_top, [((2, C, B), F32)] + [((2, C, B), BF)] * 3, scal, parts[0], *got
    )
    got = [swap(m, "leaf", 4 * k) for k, m in zip(STEPS, sent)]

    def end_top(s, pair_ref, a, b, c, x_ref, down_ref, half_ref):
        own, other = [
            pair_ref[j] + a[j].astype(F32) + b[j].astype(F32) + c[j].astype(F32) for j in range(2)
        ]
        x_ref[...] = own
        position = s[Y] * 4 + s[X]
        hit = same(jnp.full((1, B), s[T0].astype(F32), F32), position * 8 + s[ROW])
        down = own * hit + other * (1.0 - hit)
        down_ref[...] = down
        half_ref[...] = down.astype(BF)

    x_top, down_mid, half = small(
        end_top, [((C, B), F32), ((C, B), F32), ((C, B), BF)], scal, pair, *got
    )

    down_half = half
    parts = transposed(b_mid, scal, gather_row(half))
    got = [swap(parts[k], "leaf", k) for k in STEPS]

    def sum_mid(s, own_ref, a, b, c, full_ref, half_ref):
        total = [
            own_ref[j] + a[j].astype(F32) + b[j].astype(F32) + c[j].astype(F32) for j in range(2)
        ]
        full_ref[...] = total[0]
        half_ref[...] = total[1].astype(BF)

    full, half = small(sum_mid, [((C, B), F32), ((C, B), BF)], scal, parts[0], *got)

    def reduced_mid(s, y_ref, full_ref, got_ref, out_ref):
        out_ref[...] = (y_ref[...].T - (full_ref[...] + got_ref[...].astype(F32))).astype(BF)

    (half,) = small(reduced_mid, turned, scal, y_mid, full, swap(half, "leaf", 4))
    parts = transposed(w_mid, scal, gather_row(half))
    got = [swap(parts[k], "leaf", k) for k in STEPS]

    def pair_mid(s, own_ref, a, b, c, down_ref, full_ref, out_ref):
        for j in range(2):
            total = own_ref[j] + a[j].astype(F32) + b[j].astype(F32) + c[j].astype(F32)
            full_ref[j] = total
            out_ref[1 - j] = total.astype(BF)
        out_ref[2] = down_ref[...]

    full, sent = small(
        pair_mid, [((2, C, B), F32), ((3, C, B), BF)], scal, parts[0], *got, down_half
    )

    def choose(s, target, base, blocks):
        down = None
        goal = jnp.full((1, B), target.astype(F32), F32)
        for slot, block in zip(base, blocks):
            term = block * same(goal, slot)
            down = term if down is None else down + term
        return down

    def end_mid(s, full_ref, got_ref, down_ref, x_ref, out_ref, half_ref):
        own = full_ref[0] + got_ref[0].astype(F32)
        other = full_ref[1] + got_ref[1].astype(F32)
        x_ref[...] = own
        position = (s[Y] & 1) * 4 + s[X]
        slot, far = position * 8 + s[ROW], (position ^ 4) * 8 + s[ROW]
        down = choose(
            s,
            s[T1],
            (slot, slot + 64, far, far + 64),
            (own, down_ref[...], other, got_ref[2].astype(F32)),
        )
        out_ref[...] = down
        half_ref[...] = down.astype(BF)

    x_mid, down_low, half = small(
        end_mid,
        [((C, B), F32), ((C, B), F32), ((C, B), BF)],
        scal,
        full,
        swap(sent, "leaf", 4),
        down_mid,
    )

    down_half = half
    parts = transposed(b_low, scal, gather_row(half))
    got = [swap(parts[k], "leaf", k) for k in STEPS]

    def reduced_low(s, y_ref, own_ref, a, b, c, out_ref):
        total = own_ref[0] + a[0].astype(F32) + b[0].astype(F32) + c[0].astype(F32)
        out_ref[...] = (y_ref[...].T - total).astype(BF)

    (half,) = small(reduced_low, turned, scal, y_low, parts[0], *got)
    parts = transposed(w_low, scal, gather_row(half), down_half)
    got = [swap(parts[k], "leaf", k) for k in STEPS]

    def end_low(s, own_ref, a, b, c, down_ref, top_ref, mid_ref, sol_ref, leaf_ref):
        own, other = [
            own_ref[j] + a[j].astype(F32) + b[j].astype(F32) + c[j].astype(F32) for j in range(2)
        ]
        sol_ref[0] = top_ref[...].T
        sol_ref[1] = mid_ref[...].T
        sol_ref[2] = own.T
        slot, far = s[X] * 8 + s[ROW], (s[X] ^ 2) * 8 + s[ROW]
        leaf_ref[...] = choose(
            s,
            s[T2],
            (slot, slot + 32, far, far + 32),
            (own, down_ref[...], other, c[2].astype(F32)),
        ).T

    solved, leaf_solution = small(
        end_low,
        [((3, B, C), F32), ((B, C), F32)],
        scal,
        parts[0],
        *got,
        down_low,
        x_top,
        x_mid,
    )
    return (solved, leaf_solution)


def solution(mesh):
    return jax.shard_map(
        shards,
        mesh=mesh,
        in_specs=(
            P(("leaf", "row"), None),
            P(None, ("leaf", "row"), None),
            P(None, "leaf", None, "row", None),
            P(None, "leaf", None, "row", None),
            P(None, "leaf", None, "row", None),
            P(None, "leaf", None, "row", None),
            P(None, "leaf", None, "row", None),
            P(None, ("leaf", "row")),
        ),
        out_specs=(P(None, ("leaf", "row"), None), P(("leaf", "row"), None)),
        check_vma=False,
    )
```

```python
import functools

import jax
import jax.numpy as jnp
from jax import lax
from jax.experimental import pallas as pl
from jax.experimental.pallas import tpu as pltpu
from jax.sharding import PartitionSpec as P

BF = jnp.bfloat16
F32 = jnp.float32
B = 128
C = 256
STEPS = (1, 3, 2)
X, Y, Z, CORE, ROW, T0, T1, T2 = range(8)
SMALL = 8 << 20
LARGE = 28 << 20


def swap(value, axis, mask):
    count = lax.axis_size(axis)
    return lax.ppermute(value, axis, [(i, i ^ mask) for i in range(count)])


def small(body, outs, scal, *ins):
    return pl.pallas_call(
        body,
        out_shape=[jax.ShapeDtypeStruct(*o) for o in outs],
        in_specs=[pl.BlockSpec(memory_space=pltpu.SMEM)]
        + [pl.BlockSpec(memory_space=pltpu.VMEM)] * len(ins),
        out_specs=[pl.BlockSpec(memory_space=pltpu.VMEM)] * len(outs),
        compiler_params=pltpu.CompilerParams(vmem_limit_bytes=SMALL),
        cost_estimate=pl.CostEstimate(flops=1 << 18, bytes_accessed=1 << 19, transcendentals=0),
    )(scal, *ins)


def relay_body(groups, real_ref, imag_ref, out_ref):
    span = C // groups
    shift = span.bit_length() - 1
    target = lax.broadcasted_iota(jnp.int32, (C, C), 0)
    source = lax.broadcasted_iota(jnp.int32, (C, C), 1)
    place = (source == (target & span - 1) * groups + (target >> shift)).astype(BF)
    for chunk in range(B * groups // C):
        rows = slice(chunk * C, (chunk + 1) * C)
        both = jnp.concatenate([real_ref[rows, :], imag_ref[rows, :]], axis=1)
        moved = jnp.dot(place, both, preferred_element_type=F32).astype(BF)
        for p in range(groups):
            out_ref[chunk * span : (chunk + 1) * span, p * C : (p + 1) * C] = moved[
                p * span : (p + 1) * span
            ]


def relay(weights):
    _, rows, groups, _, width = weights.shape
    flat = weights.reshape(2 * rows * groups, width)
    tiles = rows // B
    return pl.pallas_call(
        functools.partial(relay_body, groups),
        grid=(tiles,),
        out_shape=jax.ShapeDtypeStruct((rows, groups * C), BF),
        in_specs=[
            pl.BlockSpec((B * groups, B), lambda t: (t, 0)),
            pl.BlockSpec((B * groups, B), lambda t: (t + tiles, 0)),
        ],
        out_specs=pl.BlockSpec((B, groups * C), lambda t: (t, 0)),
        compiler_params=pltpu.CompilerParams(vmem_limit_bytes=LARGE),
        cost_estimate=pl.CostEstimate(
            flops=4 * rows * groups * C * B, bytes_accessed=8 * rows * groups * B, transcendentals=0
        ),
    )(flat, flat)


def call(body, outs, scal, ins, scratch, flops):
    return pl.pallas_call(
        body,
        out_shape=[jax.ShapeDtypeStruct(*o) for o in outs],
        in_specs=[pl.BlockSpec(memory_space=pltpu.SMEM)]
        + [pl.BlockSpec(memory_space=pltpu.VMEM)] * len(ins),
        out_specs=[pl.BlockSpec(memory_space=pltpu.VMEM)] * len(outs),
        scratch_shapes=scratch,
        compiler_params=pltpu.CompilerParams(vmem_limit_bytes=LARGE),
        cost_estimate=pl.CostEstimate(flops=flops, bytes_accessed=1 << 20, transcendentals=0),
    )(scal, *ins)


def forward(weights, scal, ins, gather, natural=False, extras=()):
    rows, depth = weights.shape
    count = len(ins)

    def body(s, w_ref, *refs):
        in_refs, out_refs, vec = refs[:count], refs[count:-1], refs[-1]
        for index, block in gather(s, in_refs, out_refs[5:]):
            start = pl.multiple_of(index * C, C)
            block = block.astype(F32)
            vec[pl.ds(start, B), :] = block.astype(BF)
            vec[pl.ds(start + B, B), :] = jnp.concatenate(
                [-block[:, B:], block[:, :B]], axis=1
            ).astype(BF)
        for k in STEPS + (0,):
            tile = k if natural else s[Z] ^ k
            prod = jnp.dot(
                w_ref[pl.ds(pl.multiple_of(tile * C, C), C), :],
                vec[...],
                preferred_element_type=F32,
            )
            swapped = s[CORE] == 1
            upper, lower = prod[:B], prod[B:]
            out_refs[0][k] = jnp.where(swapped, lower, upper)
            out_refs[1 + k][...] = jnp.where(swapped, upper, lower).astype(BF)

    outs = [((4, B, C), F32)] + [((B, C), BF)] * 4 + list(extras)
    out = call(
        body, outs, scal, [weights, *ins], [pltpu.VMEM((depth, C), BF)], 2 * rows * depth * C
    )
    return out[0], out[1:5], *out[5:]


def transposed(weights, scal, pieces, paired=None, natural=False):
    rows, depth = weights.shape
    tiles = depth // (4 * C)
    ins = list(pieces.values()) + ([] if paired is None else [paired])
    keys = list(pieces)
    count = len(ins)
    mask = tiles - 1

    def body(s, w_ref, *refs):
        in_refs, out_refs, vec = refs[:count], refs[count:-1], refs[-1]
        for (zz, j), ref in zip(keys, in_refs):
            slot = 2 * (s[Z] ^ zz) + (s[CORE] ^ j)
            vec[:, pl.ds(pl.multiple_of(slot * B, B), B)] = ref[...]

        def block(position):
            part = jnp.dot(
                vec[...],
                w_ref[:, pl.ds(pl.multiple_of(position * C, C), C)],
                preferred_element_type=F32,
            )
            return jnp.concatenate(
                [part[:B, :B] - part[B:, B:], part[B:, :B] + part[:B, B:]], axis=0
            )

        if natural:
            for position in range(4 * tiles):
                out_refs[0][position] = block(position).astype(BF)
            return
        for k in STEPS + (0,):
            kind = out_refs[k].dtype
            for j in range(tiles):
                value = block(((s[Y] & mask) ^ j) * 4 + (s[X] ^ k))
                out_refs[k][j] = value.astype(kind)
                if paired is not None:
                    out_refs[k ^ 2][1] = value.astype(out_refs[k ^ 2].dtype)
        if paired is not None:
            out_refs[2][2] = in_refs[-1][...]

    if natural:
        outs = [((4 * tiles, C, B), BF)]
    else:
        planes = [1, 1, 1, 1] if paired is None else [2, 2, 3, 2]
        outs = [((tiles * planes[k], C, B), BF if k else F32) for k in range(4)]
    return call(
        body, outs, scal, [weights, *ins], [pltpu.VMEM((C, rows), BF)], 2 * rows * depth * C
    )


def same(goal, slot):
    return (goal == slot.astype(F32)).astype(F32)


def shards(leaf_update, rhs, inv_top, inv_mid, inv_low, couple_mid, couple_low, block_map):
    leaf = lax.axis_index("leaf")
    row = lax.axis_index("row")
    scal = jnp.concatenate(
        [jnp.stack([leaf & 3, leaf >> 2, row >> 1, row & 1, row]).astype(jnp.int32), block_map[:, 0]]
    )

    def reduce_row(own, others):
        total = None
        for k in STEPS + (0,):
            part = own[k] + swap(others[k], "row", 1).astype(F32)
            if k:
                part = swap(part.astype(BF), "row", 2 * k).astype(F32)
            total = part if total is None else total + part
        return total

    groups = [
        [(2 * z + c) * 16 + (2 * h + y) * 4 + x for z in range(4) for y in range(2)]
        for c in range(2)
        for h in range(2)
        for x in range(4)
    ]

    def exchange_row(own, others):
        sent = [(own[k] + swap(others[k], "row", 1).astype(F32)).astype(BF) for k in range(4)]
        sent = jnp.stack([sent[k // 2] for k in range(8)])
        return lax.all_to_all(
            sent, ("row", "leaf"), 0, 0, axis_index_groups=groups, tiled=True
        )

    def total_of(refs, j):
        return sum(refs[2 * z + j].astype(F32) for z in range(4))

    def gather_row(own):
        pieces = {(0, 0): own}
        for k in STEPS:
            pieces[(k, 0)] = swap(own, "row", 2 * k)
        for k in (0,) + STEPS:
            pieces[(k, 1)] = swap(pieces[(k, 0)], "row", 1)
        return pieces

    def gather_x(value):
        return [value] + [swap(value, "leaf", k) for k in (1, 2, 3)]

    def send(s, leaf_ref, rhs_ref, low_ref, y3_ref):
        def tag(level):
            return jnp.full((16, C), s[T0 + level].astype(F32), F32).astype(BF)

        low_ref[:B] = leaf_ref[...].astype(BF)
        low_ref[B : 2 * B] = rhs_ref[2].astype(BF)
        low_ref[2 * B :] = tag(2)
        y3_ref[:B] = rhs_ref[0].astype(BF)
        y3_ref[B:] = tag(0)

    low, to_y3 = small(
        send,
        [((2 * B + 16, C), BF), ((B + 16, C), BF)],
        scal,
        leaf_update,
        rhs,
    )
    got = gather_x(low)
    from_y3 = swap(to_y3, "leaf", 12)
    from_y2 = swap(to_y3, "leaf", 8)
    w_low, b_low, w_mid, b_mid, w_top = [
        relay(w) for w in (inv_low, couple_low, inv_mid, couple_mid, inv_top)
    ]

    def gather_low(s, refs, extra):
        goal = [r[2 * B : 2 * B + 16, :].astype(F32)[:1] for r in refs[:4]]
        child = [r[:B, :].astype(F32) for r in refs[:4]]
        slot = (s[X] + 4) * 8 + s[ROW]
        update = same(goal[0], slot) * child[0] + same(goal[2], slot) * child[2]
        extra[0][...] = update
        message = extra[1]
        rhs_ref = refs[4]
        message[:B] = rhs_ref[1].astype(BF)
        message[B : 2 * B] = rhs_ref[0].astype(BF)
        message[2 * B : 2 * B + 16] = jnp.full((16, C), s[T1].astype(F32), F32).astype(BF)
        message[2 * B + 16 : 2 * B + 32] = jnp.full((16, C), s[T0].astype(F32), F32).astype(BF)
        message[2 * B + 32 :] = update.astype(BF)
        for k in range(4):
            slot = (s[X] ^ k) * 8 + s[ROW]
            yield s[X] ^ k, (
                refs[k][B : 2 * B, :].astype(F32)
                + same(goal[k], slot) * child[k]
                + same(goal[k ^ 2], slot) * child[k ^ 2]
            )

    own, others, update, to_y1 = forward(
        w_low,
        scal,
        [*got, rhs],
        gather_low,
        extras=[((B, C), F32), ((3 * B + 32, C), BF)],
    )
    from_y1 = swap(to_y1, "leaf", 4)
    y_low = reduce_row(own, others)

    def gather_plain(s, refs, extra):
        for k in range(4):
            yield s[X] ^ k, refs[k][...]

    own, others = forward(b_low, scal, gather_x(y_low.astype(BF)), gather_plain, True)
    arrived = exchange_row(own, others)

    def extend_mid(s, sum_ref, up_in, rhs_ref, y1_ref, pair_ref, up_ref):
        near = s[Y] & 1
        first, second = total_of(sum_ref, 0), total_of(sum_ref, 1)
        flip = near == 1
        child_own = up_in[...] - jnp.where(flip, second, first)
        child_other = y1_ref[2 * B + 32 :, :].astype(F32) - jnp.where(flip, first, second)
        position = near * 4 + s[X]
        goal_own = jnp.full((1, C), s[T1].astype(F32), F32)
        goal_other = y1_ref[2 * B : 2 * B + 16, :].astype(F32)[:1]

        def landed(slot):
            return same(goal_own, slot) * child_own + same(goal_other, slot) * child_other

        slot = position * 8 + s[ROW]
        pair_own = (rhs_ref[1] + landed(slot)).astype(BF)
        up_ref[...] = landed(slot + 64)
        slot = (position ^ 4) * 8 + s[ROW]
        pair_other = (y1_ref[:B, :].astype(F32) + landed(slot)).astype(BF)
        pair_ref[near] = pair_own
        pair_ref[1 - near] = pair_other

    pair, update = small(
        extend_mid, [((2, B, C), BF), ((B, C), F32)], scal, arrived, update, rhs, from_y1
    )

    def gather_mid(s, refs, extra):
        for k in range(4):
            for j in range(2):
                yield j * 4 + (s[X] ^ k), refs[k][j]

    own, others = forward(w_mid, scal, gather_x(pair), gather_mid, True)
    arrived = exchange_row(own, others).reshape(4, 2, B, C)
    y_mid = jnp.sum(arrived.astype(F32), axis=0)
    own, others = forward(b_mid, scal, gather_x(y_mid.astype(BF)), gather_mid)
    children = update - reduce_row(own, others)
    half = children.astype(BF)

    moved = [swap(half, "leaf", 4 * k) for k in STEPS]

    def extend_top(s, own_ref, m1, m3, m2, rhs_ref, y1_ref, y3_ref, y2_ref, out_ref):
        child = [own_ref[...], m1[...].astype(F32), m2[...].astype(F32), m3[...].astype(F32)]
        base = [rhs_ref[0], y1_ref[B : 2 * B, :], y2_ref[:B, :], y3_ref[:B, :]]
        goal = [
            jnp.full((1, C), s[T0].astype(F32), F32),
            y1_ref[2 * B + 16 : 2 * B + 32, :].astype(F32)[:1],
            y2_ref[B : B + 16, :].astype(F32)[:1],
            y3_ref[B : B + 16, :].astype(F32)[:1],
        ]
        for k in range(4):
            slot = ((s[Y] ^ k) * 4 + s[X]) * 8 + s[ROW]
            out_ref[k] = (
                base[k].astype(F32)
                + same(goal[k], slot) * child[k]
                + same(goal[k ^ 2], slot) * child[k ^ 2]
            ).astype(BF)

    (column,) = small(
        extend_top, [((4, B, C), BF)], scal, children, *moved, rhs, from_y1, from_y3, from_y2
    )

    def gather_top(s, refs, extra):
        for k in range(4):
            for j in range(4):
                yield (s[Y] ^ j) * 4 + (s[X] ^ k), refs[k][j]

    own, others = forward(w_top, scal, gather_x(column), gather_top)

    def turn(s, total_ref, out_ref):
        out_ref[...] = total_ref[...].T.astype(BF)

    turned = [((C, B), BF)]
    (half,) = small(turn, turned, scal, reduce_row(own, others))
    parts = transposed(w_top, scal, gather_row(half))
    got = [swap(parts[k], "leaf", k) for k in STEPS]

    def sum_top(s, own_ref, a, b, c, pair_ref, m1, m3, m2):
        total = [
            own_ref[j] + a[j].astype(F32) + b[j].astype(F32) + c[j].astype(F32) for j in range(4)
        ]
        pair_ref[0] = total[0]
        pair_ref[1] = total[2]
        for k, ref in zip(STEPS, (m1, m3, m2)):
            ref[0] = total[k].astype(BF)
            ref[1] = total[k ^ 2].astype(BF)

    pair, *sent = small(
        sum_top, [((2, C, B), F32)] + [((2, C, B), BF)] * 3, scal, parts[0], *got
    )
    got = [swap(m, "leaf", 4 * k) for k, m in zip(STEPS, sent)]

    def end_top(s, pair_ref, a, b, c, x_ref, down_ref, half_ref):
        own, other = [
            pair_ref[j] + a[j].astype(F32) + b[j].astype(F32) + c[j].astype(F32) for j in range(2)
        ]
        x_ref[...] = own
        position = s[Y] * 4 + s[X]
        hit = same(jnp.full((1, B), s[T0].astype(F32), F32), position * 8 + s[ROW])
        down = own * hit + other * (1.0 - hit)
        down_ref[...] = down
        half_ref[...] = down.astype(BF)

    x_top, down_mid, half = small(
        end_top, [((C, B), F32), ((C, B), F32), ((C, B), BF)], scal, pair, *got
    )

    down_half = half
    (parts,) = transposed(b_mid, scal, gather_row(half), natural=True)
    eights = [list(range(8)), list(range(8, 16))]
    arrived = lax.all_to_all(parts, "leaf", 0, 0, axis_index_groups=eights, tiled=True)

    def reduced_mid(s, y_ref, sum_ref, out_ref):
        total = sum(sum_ref[j].astype(F32) for j in range(8))
        out_ref[...] = (y_ref[s[Y] & 1].T - total).astype(BF)

    (half,) = small(reduced_mid, turned, scal, y_mid, arrived)
    parts = transposed(w_mid, scal, gather_row(half))
    got = [swap(parts[k], "leaf", k) for k in STEPS]

    def pair_mid(s, own_ref, a, b, c, down_ref, full_ref, out_ref):
        for j in range(2):
            total = own_ref[j] + a[j].astype(F32) + b[j].astype(F32) + c[j].astype(F32)
            full_ref[j] = total
            out_ref[1 - j] = total.astype(BF)
        out_ref[2] = down_ref[...]

    full, sent = small(
        pair_mid, [((2, C, B), F32), ((3, C, B), BF)], scal, parts[0], *got, down_half
    )

    def choose(s, target, base, blocks):
        down = None
        goal = jnp.full((1, B), target.astype(F32), F32)
        for slot, block in zip(base, blocks):
            term = block * same(goal, slot)
            down = term if down is None else down + term
        return down

    def end_mid(s, full_ref, got_ref, down_ref, x_ref, out_ref, half_ref):
        own = full_ref[0] + got_ref[0].astype(F32)
        other = full_ref[1] + got_ref[1].astype(F32)
        x_ref[...] = own
        position = (s[Y] & 1) * 4 + s[X]
        slot, far = position * 8 + s[ROW], (position ^ 4) * 8 + s[ROW]
        down = choose(
            s,
            s[T1],
            (slot, slot + 64, far, far + 64),
            (own, down_ref[...], other, got_ref[2].astype(F32)),
        )
        out_ref[...] = down
        half_ref[...] = down.astype(BF)

    x_mid, down_low, half = small(
        end_mid,
        [((C, B), F32), ((C, B), F32), ((C, B), BF)],
        scal,
        full,
        swap(sent, "leaf", 4),
        down_mid,
    )

    down_half = half
    parts = transposed(b_low, scal, gather_row(half))
    got = [swap(parts[k], "leaf", k) for k in STEPS]

    def reduced_low(s, y_ref, own_ref, a, b, c, out_ref):
        total = own_ref[0] + a[0].astype(F32) + b[0].astype(F32) + c[0].astype(F32)
        out_ref[...] = (y_ref[...].T - total).astype(BF)

    (half,) = small(reduced_low, turned, scal, y_low, parts[0], *got)
    parts = transposed(w_low, scal, gather_row(half), down_half)
    got = [swap(parts[k], "leaf", k) for k in STEPS]

    def end_low(s, own_ref, a, b, c, down_ref, top_ref, mid_ref, sol_ref, leaf_ref):
        own, other = [
            own_ref[j] + a[j].astype(F32) + b[j].astype(F32) + c[j].astype(F32) for j in range(2)
        ]
        sol_ref[0] = top_ref[...].T
        sol_ref[1] = mid_ref[...].T
        sol_ref[2] = own.T
        slot, far = s[X] * 8 + s[ROW], (s[X] ^ 2) * 8 + s[ROW]
        leaf_ref[...] = choose(
            s,
            s[T2],
            (slot, slot + 32, far, far + 32),
            (own, down_ref[...], other, c[2].astype(F32)),
        ).T

    solved, leaf_solution = small(
        end_low,
        [((3, B, C), F32), ((B, C), F32)],
        scal,
        parts[0],
        *got,
        down_low,
        x_top,
        x_mid,
    )
    return (solved, leaf_solution)


def solution(mesh):
    return jax.shard_map(
        shards,
        mesh=mesh,
        in_specs=(
            P(("leaf", "row"), None),
            P(None, ("leaf", "row"), None),
            P(None, "leaf", None, "row", None),
            P(None, "leaf", None, "row", None),
            P(None, "leaf", None, "row", None),
            P(None, "leaf", None, "row", None),
            P(None, "leaf", None, "row", None),
            P(None, ("leaf", "row")),
        ),
        out_specs=(P(None, ("leaf", "row"), None), P(("leaf", "row"), None)),
        check_vma=False,
    )
```

```python
import functools

import jax
import jax.numpy as jnp
from jax import lax
from jax.experimental import pallas as pl
from jax.experimental.pallas import tpu as pltpu
from jax.sharding import PartitionSpec as P

BF = jnp.bfloat16
F32 = jnp.float32
B = 128
C = 256
STEPS = (1, 3, 2)
X, Y, Z, CORE, ROW, T0, T1, T2 = range(8)
SMALL = 8 << 20
LARGE = 28 << 20


def swap(value, axis, mask):
    count = lax.axis_size(axis)
    return lax.ppermute(value, axis, [(i, i ^ mask) for i in range(count)])


def small(body, outs, scal, *ins):
    return pl.pallas_call(
        body,
        out_shape=[jax.ShapeDtypeStruct(*o) for o in outs],
        in_specs=[pl.BlockSpec(memory_space=pltpu.SMEM)]
        + [pl.BlockSpec(memory_space=pltpu.VMEM)] * len(ins),
        out_specs=[pl.BlockSpec(memory_space=pltpu.VMEM)] * len(outs),
        compiler_params=pltpu.CompilerParams(vmem_limit_bytes=SMALL),
        cost_estimate=pl.CostEstimate(flops=1 << 18, bytes_accessed=1 << 19, transcendentals=0),
    )(scal, *ins)


def relay_body(groups, real_ref, imag_ref, out_ref):
    span = C // groups
    shift = span.bit_length() - 1
    target = lax.broadcasted_iota(jnp.int32, (C, C), 0)
    source = lax.broadcasted_iota(jnp.int32, (C, C), 1)
    place = (source == (target & span - 1) * groups + (target >> shift)).astype(BF)
    for chunk in range(B * groups // C):
        rows = slice(chunk * C, (chunk + 1) * C)
        both = jnp.concatenate([real_ref[rows, :], imag_ref[rows, :]], axis=1)
        moved = jnp.dot(place, both, preferred_element_type=F32).astype(BF)
        for p in range(groups):
            out_ref[chunk * span : (chunk + 1) * span, p * C : (p + 1) * C] = moved[
                p * span : (p + 1) * span
            ]


def relay(weights):
    _, rows, groups, _, width = weights.shape
    flat = weights.reshape(2 * rows * groups, width)
    tiles = rows // B
    return pl.pallas_call(
        functools.partial(relay_body, groups),
        grid=(tiles,),
        out_shape=jax.ShapeDtypeStruct((rows, groups * C), BF),
        in_specs=[
            pl.BlockSpec((B * groups, B), lambda t: (t, 0)),
            pl.BlockSpec((B * groups, B), lambda t: (t + tiles, 0)),
        ],
        out_specs=pl.BlockSpec((B, groups * C), lambda t: (t, 0)),
        compiler_params=pltpu.CompilerParams(vmem_limit_bytes=LARGE),
        cost_estimate=pl.CostEstimate(
            flops=4 * rows * groups * C * B, bytes_accessed=8 * rows * groups * B, transcendentals=0
        ),
    )(flat, flat)


def call(body, outs, scal, ins, scratch, flops):
    return pl.pallas_call(
        body,
        out_shape=[jax.ShapeDtypeStruct(*o) for o in outs],
        in_specs=[pl.BlockSpec(memory_space=pltpu.SMEM)]
        + [pl.BlockSpec(memory_space=pltpu.VMEM)] * len(ins),
        out_specs=[pl.BlockSpec(memory_space=pltpu.VMEM)] * len(outs),
        scratch_shapes=scratch,
        compiler_params=pltpu.CompilerParams(vmem_limit_bytes=LARGE),
        cost_estimate=pl.CostEstimate(flops=flops, bytes_accessed=1 << 20, transcendentals=0),
    )(scal, *ins)


def forward(weights, scal, ins, gather, extras=()):
    rows, depth = weights.shape
    count = len(ins)

    def body(s, w_ref, *refs):
        in_refs, out_refs, vec = refs[:count], refs[count:-1], refs[-1]
        for index, block in gather(s, in_refs, out_refs[4:]):
            start = pl.multiple_of(index * C, C)
            block = block.astype(F32)
            vec[pl.ds(start, B), :] = block.astype(BF)
            vec[pl.ds(start + B, B), :] = jnp.concatenate(
                [-block[:, B:], block[:, :B]], axis=1
            ).astype(BF)
        core = s[CORE]
        swapped = core == 1

        def tile(mask):
            start = pl.multiple_of((s[Z] ^ mask) * C, C)
            prod = jnp.dot(w_ref[pl.ds(start, C), :], vec[...], preferred_element_type=F32)
            upper, lower = prod[:B], prod[B:]
            return jnp.where(swapped, lower, upper), jnp.where(swapped, upper, lower)

        near, near_give, rest, rest_give = out_refs[:4]
        mine, theirs = tile(3 - 2 * core)
        near_give[0] = theirs.astype(BF)
        near_give[1] = mine.astype(BF)
        mine, theirs = tile(1 + 2 * core)
        near[0] = mine
        near[1] = theirs
        for j, mask in enumerate((2, 0)):
            mine, theirs = tile(mask)
            rest[j] = mine
            rest_give[j] = theirs.astype(BF)

    pair = (2, B, C)
    outs = [(pair, F32), (pair, BF), (pair, F32), (pair, BF)] + list(extras)
    out = call(
        body, outs, scal, [weights, *ins], [pltpu.VMEM((depth, C), BF)], 2 * rows * depth * C
    )
    return out[:4], *out[4:]


def transposed(weights, scal, pieces, paired=None, natural=False):
    rows, depth = weights.shape
    tiles = depth // (4 * C)
    ins = list(pieces.values()) + ([] if paired is None else [paired])
    keys = list(pieces)
    count = len(ins)
    mask = tiles - 1

    def body(s, w_ref, *refs):
        in_refs, out_refs, vec = refs[:count], refs[count:-1], refs[-1]
        for (zz, j), ref in zip(keys, in_refs):
            slot = 2 * (s[Z] ^ zz) + (s[CORE] ^ j)
            vec[:, pl.ds(pl.multiple_of(slot * B, B), B)] = ref[...]

        def block(position):
            part = jnp.dot(
                vec[...],
                w_ref[:, pl.ds(pl.multiple_of(position * C, C), C)],
                preferred_element_type=F32,
            )
            return jnp.concatenate(
                [part[:B, :B] - part[B:, B:], part[B:, :B] + part[:B, B:]], axis=0
            )

        if natural:
            for position in range(4 * tiles):
                out_refs[0][position] = block(position).astype(BF)
            return
        for k in STEPS + (0,):
            kind = out_refs[k].dtype
            for j in range(tiles):
                value = block(((s[Y] & mask) ^ j) * 4 + (s[X] ^ k))
                out_refs[k][j] = value.astype(kind)
                if paired is not None:
                    out_refs[k ^ 2][1] = value.astype(out_refs[k ^ 2].dtype)
        if paired is not None:
            out_refs[2][2] = in_refs[-1][...]

    if natural:
        outs = [((4 * tiles, C, B), BF)]
    else:
        planes = [1, 1, 1, 1] if paired is None else [2, 2, 3, 2]
        outs = [((tiles * planes[k], C, B), BF if k else F32) for k in range(4)]
    return call(
        body, outs, scal, [weights, *ins], [pltpu.VMEM((C, rows), BF)], 2 * rows * depth * C
    )


def same(goal, slot):
    return (goal == slot.astype(F32)).astype(F32)


def shards(leaf_update, rhs, inv_top, inv_mid, inv_low, couple_mid, couple_low, block_map):
    leaf = lax.axis_index("leaf")
    row = lax.axis_index("row")
    scal = jnp.concatenate(
        [jnp.stack([leaf & 3, leaf >> 2, row >> 1, row & 1, row]).astype(jnp.int32), block_map[:, 0]]
    )

    def reduce_row(parts):
        near, near_give, rest, rest_give = parts
        near = near + swap(near_give, "row", 1).astype(F32)
        rest = rest + swap(rest_give, "row", 1).astype(F32)
        route = [(r, r ^ (6 if r & 1 else 2)) for r in range(lax.axis_size("row"))]
        near = lax.ppermute(near.astype(BF), "row", route)
        far = swap(rest[0].astype(BF), "row", 4).astype(F32)
        passed = swap(near, "row", 1)
        return rest[1] + far + near[0].astype(F32) + passed[1].astype(F32)

    def gather_row(own):
        pieces = {(0, 0): own}
        for k in STEPS:
            pieces[(k, 0)] = swap(own, "row", 2 * k)
        for k in (0,) + STEPS:
            pieces[(k, 1)] = swap(pieces[(k, 0)], "row", 1)
        return pieces

    def gather_x(value):
        return [value] + [swap(value, "leaf", k) for k in (1, 2, 3)]

    def send(s, leaf_ref, rhs_ref, low_ref, y3_ref):
        def tag(level):
            return jnp.full((16, C), s[T0 + level].astype(F32), F32).astype(BF)

        low_ref[:B] = leaf_ref[...].astype(BF)
        low_ref[B : 2 * B] = rhs_ref[2].astype(BF)
        low_ref[2 * B :] = tag(2)
        y3_ref[:B] = rhs_ref[0].astype(BF)
        y3_ref[B:] = tag(0)

    low, to_y3 = small(
        send,
        [((2 * B + 16, C), BF), ((B + 16, C), BF)],
        scal,
        leaf_update,
        rhs,
    )
    got = gather_x(low)
    from_y3 = swap(to_y3, "leaf", 12)
    from_y2 = swap(to_y3, "leaf", 8)
    w_low, b_low, w_mid, b_mid, w_top = [
        relay(w) for w in (inv_low, couple_low, inv_mid, couple_mid, inv_top)
    ]

    def gather_low(s, refs, extra):
        goal = [r[2 * B : 2 * B + 16, :].astype(F32)[:1] for r in refs[:4]]
        child = [r[:B, :].astype(F32) for r in refs[:4]]
        slot = (s[X] + 4) * 8 + s[ROW]
        update = same(goal[0], slot) * child[0] + same(goal[2], slot) * child[2]
        extra[0][...] = update
        message = extra[1]
        rhs_ref = refs[4]
        message[:B] = rhs_ref[1].astype(BF)
        message[B : 2 * B] = rhs_ref[0].astype(BF)
        message[2 * B : 2 * B + 16] = jnp.full((16, C), s[T1].astype(F32), F32).astype(BF)
        message[2 * B + 16 : 2 * B + 32] = jnp.full((16, C), s[T0].astype(F32), F32).astype(BF)
        for k in range(4):
            slot = (s[X] ^ k) * 8 + s[ROW]
            yield s[X] ^ k, (
                refs[k][B : 2 * B, :].astype(F32)
                + same(goal[k], slot) * child[k]
                + same(goal[k ^ 2], slot) * child[k ^ 2]
            )

    parts, update, to_y1 = forward(
        w_low,
        scal,
        [*got, rhs],
        gather_low,
        extras=[((B, C), F32), ((2 * B + 32, C), BF)],
    )
    from_y1 = swap(to_y1, "leaf", 4)
    y_low = reduce_row(parts)

    def gather_plain(s, refs, extra):
        for k in range(4):
            yield s[X] ^ k, refs[k][...]

    (parts,) = forward(b_low, scal, gather_x(y_low.astype(BF)), gather_plain)
    children = update - reduce_row(parts)

    theirs = swap(children.astype(BF), "leaf", 4)

    def extend_mid(s, own_ref, other_ref, rhs_ref, y1_ref, pair_ref, up_ref):
        position = (s[Y] & 1) * 4 + s[X]
        goal_own = jnp.full((1, C), s[T1].astype(F32), F32)
        goal_other = y1_ref[2 * B : 2 * B + 16, :].astype(F32)[:1]

        def landed(slot):
            return same(goal_own, slot) * own_ref[...] + same(goal_other, slot) * other_ref[
                ...
            ].astype(F32)

        slot = position * 8 + s[ROW]
        pair_ref[0] = (rhs_ref[1] + landed(slot)).astype(BF)
        up_ref[...] = landed(slot + 64)
        slot = (position ^ 4) * 8 + s[ROW]
        pair_ref[1] = (y1_ref[:B, :].astype(F32) + landed(slot)).astype(BF)

    pair, update = small(
        extend_mid, [((2, B, C), BF), ((B, C), F32)], scal, children, theirs, rhs, from_y1
    )

    def gather_mid(s, refs, extra):
        for k in range(4):
            for j in range(2):
                yield ((s[Y] & 1) ^ j) * 4 + (s[X] ^ k), refs[k][j]

    (parts,) = forward(w_mid, scal, gather_x(pair), gather_mid)
    y_mid = reduce_row(parts)
    half = y_mid.astype(BF)

    def join(s, a_ref, b_ref, out_ref):
        out_ref[0] = a_ref[...]
        out_ref[1] = b_ref[...]

    (pair,) = small(join, [((2, B, C), BF)], scal, half, swap(half, "leaf", 4))
    (parts,) = forward(b_mid, scal, gather_x(pair), gather_mid)
    children = update - reduce_row(parts)
    half = children.astype(BF)

    moved = [swap(half, "leaf", 4 * k) for k in STEPS]

    def extend_top(s, own_ref, m1, m3, m2, rhs_ref, y1_ref, y3_ref, y2_ref, out_ref):
        child = [own_ref[...], m1[...].astype(F32), m2[...].astype(F32), m3[...].astype(F32)]
        base = [rhs_ref[0], y1_ref[B : 2 * B, :], y2_ref[:B, :], y3_ref[:B, :]]
        goal = [
            jnp.full((1, C), s[T0].astype(F32), F32),
            y1_ref[2 * B + 16 : 2 * B + 32, :].astype(F32)[:1],
            y2_ref[B : B + 16, :].astype(F32)[:1],
            y3_ref[B : B + 16, :].astype(F32)[:1],
        ]
        for k in range(4):
            slot = ((s[Y] ^ k) * 4 + s[X]) * 8 + s[ROW]
            out_ref[k] = (
                base[k].astype(F32)
                + same(goal[k], slot) * child[k]
                + same(goal[k ^ 2], slot) * child[k ^ 2]
            ).astype(BF)

    (column,) = small(
        extend_top, [((4, B, C), BF)], scal, children, *moved, rhs, from_y1, from_y3, from_y2
    )

    def gather_top(s, refs, extra):
        for k in range(4):
            for j in range(4):
                yield (s[Y] ^ j) * 4 + (s[X] ^ k), refs[k][j]

    (parts,) = forward(w_top, scal, gather_x(column), gather_top)

    def turn(s, total_ref, out_ref):
        out_ref[...] = total_ref[...].T.astype(BF)

    turned = [((C, B), BF)]
    (half,) = small(turn, turned, scal, reduce_row(parts))
    parts = transposed(w_top, scal, gather_row(half))
    got = [swap(parts[k], "leaf", k) for k in STEPS]

    def sum_top(s, own_ref, a, b, c, pair_ref, m1, m3, m2):
        total = [
            own_ref[j] + a[j].astype(F32) + b[j].astype(F32) + c[j].astype(F32) for j in range(4)
        ]
        pair_ref[0] = total[0]
        pair_ref[1] = total[2]
        for k, ref in zip(STEPS, (m1, m3, m2)):
            ref[0] = total[k].astype(BF)
            ref[1] = total[k ^ 2].astype(BF)

    pair, *sent = small(
        sum_top, [((2, C, B), F32)] + [((2, C, B), BF)] * 3, scal, parts[0], *got
    )
    got = [swap(m, "leaf", 4 * k) for k, m in zip(STEPS, sent)]

    def end_top(s, pair_ref, a, b, c, x_ref, down_ref, half_ref):
        own, other = [
            pair_ref[j] + a[j].astype(F32) + b[j].astype(F32) + c[j].astype(F32) for j in range(2)
        ]
        x_ref[...] = own
        position = s[Y] * 4 + s[X]
        hit = same(jnp.full((1, B), s[T0].astype(F32), F32), position * 8 + s[ROW])
        down = own * hit + other * (1.0 - hit)
        down_ref[...] = down
        half_ref[...] = down.astype(BF)

    x_top, down_mid, half = small(
        end_top, [((C, B), F32), ((C, B), F32), ((C, B), BF)], scal, pair, *got
    )

    down_half = half
    (parts,) = transposed(b_mid, scal, gather_row(half), natural=True)
    eights = [list(range(8)), list(range(8, 16))]
    arrived = lax.all_to_all(parts, "leaf", 0, 0, axis_index_groups=eights, tiled=True)

    def reduced_mid(s, y_ref, sum_ref, out_ref):
        total = sum(sum_ref[j].astype(F32) for j in range(8))
        out_ref[...] = (y_ref[...].T - total).astype(BF)

    (half,) = small(reduced_mid, turned, scal, y_mid, arrived)
    parts = transposed(w_mid, scal, gather_row(half))
    got = [swap(parts[k], "leaf", k) for k in STEPS]

    def pair_mid(s, own_ref, a, b, c, down_ref, full_ref, out_ref):
        for j in range(2):
            total = own_ref[j] + a[j].astype(F32) + b[j].astype(F32) + c[j].astype(F32)
            full_ref[j] = total
            out_ref[1 - j] = total.astype(BF)
        out_ref[2] = down_ref[...]

    full, sent = small(
        pair_mid, [((2, C, B), F32), ((3, C, B), BF)], scal, parts[0], *got, down_half
    )

    def choose(s, target, base, blocks):
        down = None
        goal = jnp.full((1, B), target.astype(F32), F32)
        for slot, block in zip(base, blocks):
            term = block * same(goal, slot)
            down = term if down is None else down + term
        return down

    def end_mid(s, full_ref, got_ref, down_ref, x_ref, out_ref, half_ref):
        own = full_ref[0] + got_ref[0].astype(F32)
        other = full_ref[1] + got_ref[1].astype(F32)
        x_ref[...] = own
        position = (s[Y] & 1) * 4 + s[X]
        slot, far = position * 8 + s[ROW], (position ^ 4) * 8 + s[ROW]
        down = choose(
            s,
            s[T1],
            (slot, slot + 64, far, far + 64),
            (own, down_ref[...], other, got_ref[2].astype(F32)),
        )
        out_ref[...] = down
        half_ref[...] = down.astype(BF)

    x_mid, down_low, half = small(
        end_mid,
        [((C, B), F32), ((C, B), F32), ((C, B), BF)],
        scal,
        full,
        swap(sent, "leaf", 4),
        down_mid,
    )

    down_half = half
    parts = transposed(b_low, scal, gather_row(half))
    got = [swap(parts[k], "leaf", k) for k in STEPS]

    def reduced_low(s, y_ref, own_ref, a, b, c, out_ref):
        total = own_ref[0] + a[0].astype(F32) + b[0].astype(F32) + c[0].astype(F32)
        out_ref[...] = (y_ref[...].T - total).astype(BF)

    (half,) = small(reduced_low, turned, scal, y_low, parts[0], *got)
    parts = transposed(w_low, scal, gather_row(half), down_half)
    got = [swap(parts[k], "leaf", k) for k in STEPS]

    def end_low(s, own_ref, a, b, c, down_ref, top_ref, mid_ref, sol_ref, leaf_ref):
        own, other = [
            own_ref[j] + a[j].astype(F32) + b[j].astype(F32) + c[j].astype(F32) for j in range(2)
        ]
        sol_ref[0] = top_ref[...].T
        sol_ref[1] = mid_ref[...].T
        sol_ref[2] = own.T
        slot, far = s[X] * 8 + s[ROW], (s[X] ^ 2) * 8 + s[ROW]
        leaf_ref[...] = choose(
            s,
            s[T2],
            (slot, slot + 32, far, far + 32),
            (own, down_ref[...], other, c[2].astype(F32)),
        ).T

    solved, leaf_solution = small(
        end_low,
        [((3, B, C), F32), ((B, C), F32)],
        scal,
        parts[0],
        *got,
        down_low,
        x_top,
        x_mid,
    )
    return (solved, leaf_solution)


def solution(mesh):
    return jax.shard_map(
        shards,
        mesh=mesh,
        in_specs=(
            P(("leaf", "row"), None),
            P(None, ("leaf", "row"), None),
            P(None, "leaf", None, "row", None),
            P(None, "leaf", None, "row", None),
            P(None, "leaf", None, "row", None),
            P(None, "leaf", None, "row", None),
            P(None, "leaf", None, "row", None),
            P(None, ("leaf", "row")),
        ),
        out_specs=(P(None, ("leaf", "row"), None), P(("leaf", "row"), None)),
        check_vma=False,
    )
```

```python
import functools

import jax
import jax.numpy as jnp
from jax import lax
from jax.experimental import pallas as pl
from jax.experimental.pallas import tpu as pltpu
from jax.sharding import PartitionSpec as P

BF = jnp.bfloat16
F32 = jnp.float32
B = 128
C = 256
STEPS = (1, 3, 2)
X, Y, Z, CORE, ROW, T0, T1, T2 = range(8)
SMALL = 8 << 20
LARGE = 28 << 20


def swap(value, axis, mask):
    count = lax.axis_size(axis)
    return lax.ppermute(value, axis, [(i, i ^ mask) for i in range(count)])


def small(body, outs, scal, *ins):
    return pl.pallas_call(
        body,
        out_shape=[jax.ShapeDtypeStruct(*o) for o in outs],
        in_specs=[pl.BlockSpec(memory_space=pltpu.SMEM)]
        + [pl.BlockSpec(memory_space=pltpu.VMEM)] * len(ins),
        out_specs=[pl.BlockSpec(memory_space=pltpu.VMEM)] * len(outs),
        compiler_params=pltpu.CompilerParams(vmem_limit_bytes=SMALL),
        cost_estimate=pl.CostEstimate(flops=1 << 18, bytes_accessed=1 << 19, transcendentals=0),
    )(scal, *ins)


def relay_body(groups, real_ref, imag_ref, out_ref):
    span = C // groups
    shift = span.bit_length() - 1
    target = lax.broadcasted_iota(jnp.int32, (C, C), 0)
    source = lax.broadcasted_iota(jnp.int32, (C, C), 1)
    place = (source == (target & span - 1) * groups + (target >> shift)).astype(BF)
    for chunk in range(B * groups // C):
        rows = slice(chunk * C, (chunk + 1) * C)
        both = jnp.concatenate([real_ref[rows, :], imag_ref[rows, :]], axis=1)
        moved = jnp.dot(place, both, preferred_element_type=F32).astype(BF)
        for p in range(groups):
            out_ref[chunk * span : (chunk + 1) * span, p * C : (p + 1) * C] = moved[
                p * span : (p + 1) * span
            ]


def relay(weights):
    _, rows, groups, _, width = weights.shape
    flat = weights.reshape(2 * rows * groups, width)
    tiles = rows // B
    return pl.pallas_call(
        functools.partial(relay_body, groups),
        grid=(tiles,),
        out_shape=jax.ShapeDtypeStruct((rows, groups * C), BF),
        in_specs=[
            pl.BlockSpec((B * groups, B), lambda t: (t, 0)),
            pl.BlockSpec((B * groups, B), lambda t: (t + tiles, 0)),
        ],
        out_specs=pl.BlockSpec((B, groups * C), lambda t: (t, 0)),
        compiler_params=pltpu.CompilerParams(vmem_limit_bytes=LARGE),
        cost_estimate=pl.CostEstimate(
            flops=4 * rows * groups * C * B, bytes_accessed=8 * rows * groups * B, transcendentals=0
        ),
    )(flat, flat)


def call(body, outs, scal, ins, scratch, flops):
    return pl.pallas_call(
        body,
        out_shape=[jax.ShapeDtypeStruct(*o) for o in outs],
        in_specs=[pl.BlockSpec(memory_space=pltpu.SMEM)]
        + [pl.BlockSpec(memory_space=pltpu.VMEM)] * len(ins),
        out_specs=[pl.BlockSpec(memory_space=pltpu.VMEM)] * len(outs),
        scratch_shapes=scratch,
        compiler_params=pltpu.CompilerParams(vmem_limit_bytes=LARGE),
        cost_estimate=pl.CostEstimate(flops=flops, bytes_accessed=1 << 20, transcendentals=0),
    )(scal, *ins)


def forward(weights, scal, ins, gather, extras=()):
    rows, depth = weights.shape
    count = len(ins)

    def body(s, w_ref, *refs):
        in_refs, out_refs, vec = refs[:count], refs[count:-1], refs[-1]
        for index, block in gather(s, in_refs, out_refs[5:]):
            start = pl.multiple_of(index * C, C)
            block = block.astype(F32)
            vec[pl.ds(start, B), :] = block.astype(BF)
            vec[pl.ds(start + B, B), :] = jnp.concatenate(
                [-block[:, B:], block[:, :B]], axis=1
            ).astype(BF)
        for k in STEPS + (0,):
            tile = s[Z] ^ k
            prod = jnp.dot(
                w_ref[pl.ds(pl.multiple_of(tile * C, C), C), :],
                vec[...],
                preferred_element_type=F32,
            )
            swapped = s[CORE] == 1
            upper, lower = prod[:B], prod[B:]
            out_refs[0][k] = jnp.where(swapped, lower, upper)
            out_refs[1 + k][...] = jnp.where(swapped, upper, lower).astype(BF)

    outs = [((4, B, C), F32)] + [((B, C), BF)] * 4 + list(extras)
    out = call(
        body, outs, scal, [weights, *ins], [pltpu.VMEM((depth, C), BF)], 2 * rows * depth * C
    )
    return out[0], out[1:5], *out[5:]


def transposed(weights, scal, pieces, paired=None, only=None):
    rows, depth = weights.shape
    tiles = depth // (4 * C)
    ins = list(pieces.values()) + ([] if paired is None else [paired])
    keys = list(pieces)
    count = len(ins)
    mask = tiles - 1

    def body(s, w_ref, *refs):
        in_refs, out_refs, vec = refs[:count], refs[count:-1], refs[-1]
        for (zz, j), ref in zip(keys, in_refs):
            slot = 2 * (s[Z] ^ zz) + (s[CORE] ^ j)
            vec[:, pl.ds(pl.multiple_of(slot * B, B), B)] = ref[...]

        def block(position):
            part = jnp.dot(
                vec[...],
                w_ref[:, pl.ds(pl.multiple_of(position * C, C), C)],
                preferred_element_type=F32,
            )
            return jnp.concatenate(
                [part[:B, :B] - part[B:, B:], part[B:, :B] + part[:B, B:]], axis=0
            )

        if only is not None:
            for plane, j in enumerate((0, 2, 1, 3)):
                value = block((s[Y] ^ j) * 4 + (s[X] ^ only))
                out_refs[0][plane] = value.astype(out_refs[0].dtype)
            return
        for k in STEPS + (0,):
            kind = out_refs[k].dtype
            for j in range(tiles):
                value = block(((s[Y] & mask) ^ j) * 4 + (s[X] ^ k))
                out_refs[k][j] = value.astype(kind)
                if paired is not None:
                    out_refs[k ^ 2][1] = value.astype(out_refs[k ^ 2].dtype)
        if paired is not None:
            out_refs[2][2] = in_refs[-1][...]

    if only is not None:
        outs = [((4, C, B), BF if only else F32)]
    else:
        planes = [1, 1, 1, 1] if paired is None else [2, 2, 3, 2]
        outs = [((tiles * planes[k], C, B), BF if k else F32) for k in range(4)]
    return call(
        body, outs, scal, [weights, *ins], [pltpu.VMEM((C, rows), BF)], 2 * rows * depth * C
    )


def same(goal, slot):
    return (goal == slot.astype(F32)).astype(F32)


def shards(leaf_update, rhs, inv_top, inv_mid, inv_low, couple_mid, couple_low, block_map):
    leaf = lax.axis_index("leaf")
    row = lax.axis_index("row")
    scal = jnp.concatenate(
        [jnp.stack([leaf & 3, leaf >> 2, row >> 1, row & 1, row]).astype(jnp.int32), block_map[:, 0]]
    )

    def reduce_row(own, others):
        total = None
        for k in STEPS + (0,):
            part = own[k] + swap(others[k], "row", 1).astype(F32)
            if k:
                part = swap(part.astype(BF), "row", 2 * k).astype(F32)
            total = part if total is None else total + part
        return total

    def gather_row(own):
        pieces = {(0, 0): own}
        for k in STEPS:
            pieces[(k, 0)] = swap(own, "row", 2 * k)
        for k in (0,) + STEPS:
            pieces[(k, 1)] = swap(pieces[(k, 0)], "row", 1)
        return pieces

    def gather_x(value):
        return [value] + [swap(value, "leaf", k) for k in (1, 2, 3)]

    def send(s, leaf_ref, rhs_ref, low_ref, y3_ref):
        def tag(level):
            return jnp.full((16, C), s[T0 + level].astype(F32), F32).astype(BF)

        low_ref[:B] = leaf_ref[...].astype(BF)
        low_ref[B : 2 * B] = rhs_ref[2].astype(BF)
        low_ref[2 * B :] = tag(2)
        y3_ref[:B] = rhs_ref[0].astype(BF)
        y3_ref[B:] = tag(0)

    low, to_y3 = small(
        send,
        [((2 * B + 16, C), BF), ((B + 16, C), BF)],
        scal,
        leaf_update,
        rhs,
    )
    got = gather_x(low)
    from_y3 = swap(to_y3, "leaf", 12)
    from_y2 = swap(to_y3, "leaf", 8)
    w_low, b_low, w_mid, b_mid, w_top = [
        relay(w) for w in (inv_low, couple_low, inv_mid, couple_mid, inv_top)
    ]

    def gather_low(s, refs, extra):
        goal = [r[2 * B : 2 * B + 16, :].astype(F32)[:1] for r in refs[:4]]
        child = [r[:B, :].astype(F32) for r in refs[:4]]
        slot = (s[X] + 4) * 8 + s[ROW]
        update = same(goal[0], slot) * child[0] + same(goal[2], slot) * child[2]
        extra[0][...] = update
        message = extra[1]
        rhs_ref = refs[4]
        message[:B] = rhs_ref[1].astype(BF)
        message[B : 2 * B] = rhs_ref[0].astype(BF)
        message[2 * B : 2 * B + 16] = jnp.full((16, C), s[T1].astype(F32), F32).astype(BF)
        message[2 * B + 16 : 2 * B + 32] = jnp.full((16, C), s[T0].astype(F32), F32).astype(BF)
        for k in range(4):
            slot = (s[X] ^ k) * 8 + s[ROW]
            yield s[X] ^ k, (
                refs[k][B : 2 * B, :].astype(F32)
                + same(goal[k], slot) * child[k]
                + same(goal[k ^ 2], slot) * child[k ^ 2]
            )

    own, others, update, to_y1 = forward(
        w_low,
        scal,
        [*got, rhs],
        gather_low,
        extras=[((B, C), F32), ((2 * B + 32, C), BF)],
    )
    from_y1 = swap(to_y1, "leaf", 4)
    y_low = reduce_row(own, others)

    def gather_plain(s, refs, extra):
        for k in range(4):
            yield s[X] ^ k, refs[k][...]

    own, others = forward(b_low, scal, gather_x(y_low.astype(BF)), gather_plain)
    children = update - reduce_row(own, others)

    theirs = swap(children.astype(BF), "leaf", 4)

    def extend_mid(s, own_ref, other_ref, rhs_ref, y1_ref, pair_ref, up_ref):
        position = (s[Y] & 1) * 4 + s[X]
        goal_own = jnp.full((1, C), s[T1].astype(F32), F32)
        goal_other = y1_ref[2 * B : 2 * B + 16, :].astype(F32)[:1]

        def landed(slot):
            return same(goal_own, slot) * own_ref[...] + same(goal_other, slot) * other_ref[
                ...
            ].astype(F32)

        slot = position * 8 + s[ROW]
        pair_ref[0] = (rhs_ref[1] + landed(slot)).astype(BF)
        up_ref[...] = landed(slot + 64)
        slot = (position ^ 4) * 8 + s[ROW]
        pair_ref[1] = (y1_ref[:B, :].astype(F32) + landed(slot)).astype(BF)

    pair, update = small(
        extend_mid, [((2, B, C), BF), ((B, C), F32)], scal, children, theirs, rhs, from_y1
    )

    def gather_mid(s, refs, extra):
        for k in range(4):
            for j in range(2):
                yield ((s[Y] & 1) ^ j) * 4 + (s[X] ^ k), refs[k][j]

    own, others = forward(w_mid, scal, gather_x(pair), gather_mid)
    y_mid = reduce_row(own, others)
    half = y_mid.astype(BF)

    def join(s, a_ref, b_ref, out_ref):
        out_ref[0] = a_ref[...]
        out_ref[1] = b_ref[...]

    (pair,) = small(join, [((2, B, C), BF)], scal, half, swap(half, "leaf", 4))
    own, others = forward(b_mid, scal, gather_x(pair), gather_mid)
    children = update - reduce_row(own, others)
    half = children.astype(BF)

    def flip(s, low_ref, mid_ref, low_out, mid_out):
        low_out[...] = low_ref[...].T
        mid_out[...] = mid_ref[...].T

    turned_low, turned_mid = small(flip, [((C, B), F32)] * 2, scal, y_low, y_mid)

    moved = [swap(half, "leaf", 4 * k) for k in STEPS]

    def extend_top(s, own_ref, m1, m3, m2, rhs_ref, y1_ref, y3_ref, y2_ref, out_ref):
        child = [own_ref[...], m1[...].astype(F32), m2[...].astype(F32), m3[...].astype(F32)]
        base = [rhs_ref[0], y1_ref[B : 2 * B, :], y2_ref[:B, :], y3_ref[:B, :]]
        goal = [
            jnp.full((1, C), s[T0].astype(F32), F32),
            y1_ref[2 * B + 16 : 2 * B + 32, :].astype(F32)[:1],
            y2_ref[B : B + 16, :].astype(F32)[:1],
            y3_ref[B : B + 16, :].astype(F32)[:1],
        ]
        for k in range(4):
            slot = ((s[Y] ^ k) * 4 + s[X]) * 8 + s[ROW]
            out_ref[k] = (
                base[k].astype(F32)
                + same(goal[k], slot) * child[k]
                + same(goal[k ^ 2], slot) * child[k ^ 2]
            ).astype(BF)

    (column,) = small(
        extend_top, [((4, B, C), BF)], scal, children, *moved, rhs, from_y1, from_y3, from_y2
    )

    def gather_top(s, refs, extra):
        for k in range(4):
            for j in range(4):
                yield (s[Y] ^ j) * 4 + (s[X] ^ k), refs[k][j]

    own, others = forward(w_top, scal, gather_x(column), gather_top)

    def turn(s, total_ref, out_ref):
        out_ref[...] = total_ref[...].T.astype(BF)

    (half,) = small(turn, [((C, B), BF)], scal, reduce_row(own, others))
    pieces = gather_row(half)
    got = [swap(transposed(w_top, scal, pieces, only=k)[0], "leaf", k) for k in (2, 1, 3)]
    (own,) = transposed(w_top, scal, pieces, only=0)

    def total(planes):
        return own[planes] + sum(g[planes].astype(F32) for g in got)

    pair, cross = total(slice(0, 2)), total(slice(2, 4)).astype(BF)
    from_1, from_3 = swap(cross, "leaf", 4).astype(F32), swap(cross, "leaf", 12).astype(F32)
    from_2 = swap(pair.astype(BF), "leaf", 8).astype(F32)
    x_top = pair[0] + from_2[1] + from_1[0] + from_3[1]
    x_other = pair[1] + from_2[0] + from_1[1] + from_3[0]
    down_mid = jnp.where(block_map[0, 0] == leaf * 8 + row, x_top, x_other)
    half = down_mid.astype(BF)

    down_half = half
    parts = transposed(b_mid, scal, gather_row(half))
    got = [swap(parts[k], "leaf", k) for k in STEPS]
    full, cross = [parts[0][j] + sum(g[j].astype(F32) for g in got) for j in range(2)]
    coupled = full + swap(cross.astype(BF), "leaf", 4).astype(F32)
    half = (turned_mid - coupled).astype(BF)
    parts = transposed(w_mid, scal, gather_row(half))
    got = [swap(parts[k], "leaf", k) for k in STEPS]

    def pair_mid(s, own_ref, a, b, c, down_ref, full_ref, out_ref):
        for j in range(2):
            total = own_ref[j] + a[j].astype(F32) + b[j].astype(F32) + c[j].astype(F32)
            full_ref[j] = total
            out_ref[1 - j] = total.astype(BF)
        out_ref[2] = down_ref[...]

    full, sent = small(
        pair_mid, [((2, C, B), F32), ((3, C, B), BF)], scal, parts[0], *got, down_half
    )

    def choose(s, target, base, blocks):
        down = None
        goal = jnp.full((1, B), target.astype(F32), F32)
        for slot, block in zip(base, blocks):
            term = block * same(goal, slot)
            down = term if down is None else down + term
        return down

    def end_mid(s, full_ref, got_ref, down_ref, x_ref, out_ref, half_ref):
        own = full_ref[0] + got_ref[0].astype(F32)
        other = full_ref[1] + got_ref[1].astype(F32)
        x_ref[...] = own
        position = (s[Y] & 1) * 4 + s[X]
        slot, far = position * 8 + s[ROW], (position ^ 4) * 8 + s[ROW]
        down = choose(
            s,
            s[T1],
            (slot, slot + 64, far, far + 64),
            (own, down_ref[...], other, got_ref[2].astype(F32)),
        )
        out_ref[...] = down
        half_ref[...] = down.astype(BF)

    x_mid, down_low, half = small(
        end_mid,
        [((C, B), F32), ((C, B), F32), ((C, B), BF)],
        scal,
        full,
        swap(sent, "leaf", 4),
        down_mid,
    )

    down_half = half
    parts = transposed(b_low, scal, gather_row(half))
    got = [swap(parts[k], "leaf", k) for k in STEPS]

    coupled = parts[0][0] + sum(g[0].astype(F32) for g in got)
    half = (turned_low - coupled).astype(BF)
    parts = transposed(w_low, scal, gather_row(half), down_half)
    got = [swap(parts[k], "leaf", k) for k in STEPS]

    def end_low(s, own_ref, a, b, c, down_ref, top_ref, mid_ref, sol_ref, leaf_ref):
        own, other = [
            own_ref[j] + a[j].astype(F32) + b[j].astype(F32) + c[j].astype(F32) for j in range(2)
        ]
        sol_ref[0] = top_ref[...].T
        sol_ref[1] = mid_ref[...].T
        sol_ref[2] = own.T
        slot, far = s[X] * 8 + s[ROW], (s[X] ^ 2) * 8 + s[ROW]
        leaf_ref[...] = choose(
            s,
            s[T2],
            (slot, slot + 32, far, far + 32),
            (own, down_ref[...], other, c[2].astype(F32)),
        ).T

    solved, leaf_solution = small(
        end_low,
        [((3, B, C), F32), ((B, C), F32)],
        scal,
        parts[0],
        *got,
        down_low,
        x_top,
        x_mid,
    )
    return (solved, leaf_solution)


def solution(mesh):
    return jax.shard_map(
        shards,
        mesh=mesh,
        in_specs=(
            P(("leaf", "row"), None),
            P(None, ("leaf", "row"), None),
            P(None, "leaf", None, "row", None),
            P(None, "leaf", None, "row", None),
            P(None, "leaf", None, "row", None),
            P(None, "leaf", None, "row", None),
            P(None, "leaf", None, "row", None),
            P(None, ("leaf", "row")),
        ),
        out_specs=(P(None, ("leaf", "row"), None), P(("leaf", "row"), None)),
        check_vma=False,
    )
```

```python
import functools

import jax
import jax.numpy as jnp
from jax import lax
from jax.experimental import pallas as pl
from jax.experimental.pallas import tpu as pltpu
from jax.sharding import PartitionSpec as P

BF = jnp.bfloat16
F32 = jnp.float32
B = 128
C = 256
STEPS = (1, 3, 2)
X, Y, Z, CORE, ROW, T0, T1, T2 = range(8)
SMALL = 8 << 20


def swap(value, axis, mask):
    count = lax.axis_size(axis)
    return lax.ppermute(value, axis, [(i, i ^ mask) for i in range(count)])


def small(body, outs, scal, *ins):
    return pl.pallas_call(
        body,
        out_shape=[jax.ShapeDtypeStruct(*o) for o in outs],
        in_specs=[pl.BlockSpec(memory_space=pltpu.SMEM)]
        + [pl.BlockSpec(memory_space=pltpu.VMEM)] * len(ins),
        out_specs=[pl.BlockSpec(memory_space=pltpu.VMEM)] * len(outs),
        compiler_params=pltpu.CompilerParams(vmem_limit_bytes=SMALL),
        cost_estimate=pl.CostEstimate(flops=1 << 18, bytes_accessed=1 << 19, transcendentals=0),
    )(scal, *ins)


def relay_body(groups, real_ref, imag_ref, out_ref):
    span = C // groups
    shift = span.bit_length() - 1
    target = lax.broadcasted_iota(jnp.int32, (C, C), 0)
    source = lax.broadcasted_iota(jnp.int32, (C, C), 1)
    place = (source == (target & span - 1) * groups + (target >> shift)).astype(BF)

    @pl.loop(0, B * groups // C)
    def _(chunk):
        rows = pl.ds(pl.multiple_of(chunk * C, C), C)
        both = jnp.concatenate([real_ref[rows, :], imag_ref[rows, :]], axis=1)
        moved = jnp.dot(place, both, preferred_element_type=F32).astype(BF)
        for p in range(groups):
            out_ref[pl.ds(pl.multiple_of(chunk * span, span), span), p * C : (p + 1) * C] = moved[
                p * span : (p + 1) * span
            ]


def relay(weights):
    _, rows, groups, _, width = weights.shape
    flat = weights.reshape(2 * rows * groups, width)
    tiles = rows // B
    return pl.pallas_call(
        functools.partial(relay_body, groups),
        grid=(tiles,),
        out_shape=jax.ShapeDtypeStruct((rows, groups * C), BF),
        in_specs=[
            pl.BlockSpec((B * groups, B), lambda t: (t, 0)),
            pl.BlockSpec((B * groups, B), lambda t: (t + tiles, 0)),
        ],
        out_specs=pl.BlockSpec((B, groups * C), lambda t: (t, 0)),
        compiler_params=pltpu.CompilerParams(vmem_limit_bytes=2 * SMALL),
        cost_estimate=pl.CostEstimate(
            flops=4 * rows * groups * C * B, bytes_accessed=8 * rows * groups * B, transcendentals=0
        ),
    )(flat, flat)


def call(body, outs, scal, ins, scratch, flops):
    limit = 2 * ins[0].size + (12 << 20)
    return pl.pallas_call(
        body,
        out_shape=[jax.ShapeDtypeStruct(*o) for o in outs],
        in_specs=[pl.BlockSpec(memory_space=pltpu.SMEM)]
        + [pl.BlockSpec(memory_space=pltpu.VMEM)] * len(ins),
        out_specs=[pl.BlockSpec(memory_space=pltpu.VMEM)] * len(outs),
        scratch_shapes=scratch,
        compiler_params=pltpu.CompilerParams(vmem_limit_bytes=limit),
        cost_estimate=pl.CostEstimate(flops=flops, bytes_accessed=1 << 20, transcendentals=0),
    )(scal, *ins)


def forward(weights, scal, ins, gather, extras=()):
    rows, depth = weights.shape
    count = len(ins)

    def body(s, w_ref, *refs):
        in_refs, out_refs, vec = refs[:count], refs[count:-1], refs[-1]
        for index, block in gather(s, in_refs, out_refs[2:]):
            start = pl.multiple_of(index * C, C)
            block = block.astype(F32)
            vec[pl.ds(start, B), :] = block.astype(BF)
            vec[pl.ds(start + B, B), :] = jnp.concatenate(
                [-block[:, B:], block[:, :B]], axis=1
            ).astype(BF)
        swapped = s[CORE] == 1

        @pl.loop(0, 4)
        def _(k):
            start = pl.multiple_of((s[Z] ^ k) * C, C)
            prod = jnp.dot(w_ref[pl.ds(start, C), :], vec[...], preferred_element_type=F32)
            upper, lower = prod[:B], prod[B:]
            out_refs[0][k] = jnp.where(swapped, lower, upper)
            out_refs[1][k] = jnp.where(swapped, upper, lower).astype(BF)

    outs = [((4, B, C), F32), ((4, B, C), BF)] + list(extras)
    return call(
        body, outs, scal, [weights, *ins], [pltpu.VMEM((depth, C), BF)], 2 * rows * depth * C
    )


def transposed(weights, scal, pieces, paired=None, only=None):
    rows, depth = weights.shape
    tiles = depth // (4 * C)
    ins = list(pieces.values()) + ([] if paired is None else [paired])
    keys = list(pieces)
    count = len(ins)
    mask = tiles - 1
    used = count + (4 if only is None else 1)

    def body(s, w_ref, *refs):
        in_refs, out_refs, scratch = refs[:count], refs[count:used], refs[used:]
        vec = scratch[0]
        for (zz, j), ref in zip(keys, in_refs):
            slot = 2 * (s[Z] ^ zz) + (s[CORE] ^ j)
            vec[:, pl.ds(pl.multiple_of(slot * B, B), B)] = ref[...]

        def block(position):
            part = jnp.dot(
                vec[...],
                w_ref[:, pl.ds(pl.multiple_of(position * C, C), C)],
                preferred_element_type=F32,
            )
            return jnp.concatenate(
                [part[:B, :B] - part[B:, B:], part[B:, :B] + part[:B, B:]], axis=0
            )

        if only is not None:

            @pl.loop(0, 4)
            def _(plane):
                j = (plane & 1) * 2 + (plane >> 1)
                value = block((s[Y] ^ j) * 4 + (s[X] ^ only))
                out_refs[0][plane] = value.astype(out_refs[0].dtype)

            return
        acc = scratch[1]

        @pl.loop(0, 4 * tiles)
        def _(step):
            k, j = step & 3, step >> 2
            acc[k, j] = block(((s[Y] & mask) ^ j) * 4 + (s[X] ^ k))

        for k in range(4):
            kind = out_refs[k].dtype
            out_refs[k][:tiles] = acc[k].astype(kind)
            if paired is not None:
                out_refs[k][1] = acc[k ^ 2, 0].astype(kind)
        if paired is not None:
            out_refs[2][2] = in_refs[-1][...]

    scratch_shapes = [pltpu.VMEM((C, rows), BF)]
    if only is not None:
        outs = [((4, C, B), BF if only else F32)]
    else:
        scratch_shapes.append(pltpu.VMEM((4, tiles, C, B), F32))
        planes = [1, 1, 1, 1] if paired is None else [2, 2, 3, 2]
        outs = [((tiles * planes[k], C, B), BF if k else F32) for k in range(4)]
    return call(
        body, outs, scal, [weights, *ins], scratch_shapes, 2 * rows * depth * C
    )


def same(goal, slot):
    return (goal == slot.astype(F32)).astype(F32)


def shards(leaf_update, rhs, inv_top, inv_mid, inv_low, couple_mid, couple_low, block_map):
    leaf = lax.axis_index("leaf")
    row = lax.axis_index("row")
    scal = jnp.concatenate(
        [jnp.stack([leaf & 3, leaf >> 2, row >> 1, row & 1, row]).astype(jnp.int32), block_map[:, 0]]
    )

    def reduce_row(own, other):
        other = swap(other, "row", 1)
        parts = {k: own[k] + other[k].astype(F32) for k in range(4)}
        total = parts[0]
        for k in STEPS:
            total = total + swap(parts[k].astype(BF), "row", 2 * k).astype(F32)
        return total

    def gather_row(own):
        pieces = {(0, 0): own}
        for k in STEPS:
            pieces[(k, 0)] = swap(own, "row", 2 * k)
        for k in (0,) + STEPS:
            pieces[(k, 1)] = swap(pieces[(k, 0)], "row", 1)
        return pieces

    def gather_x(value):
        return [value] + [swap(value, "leaf", k) for k in (1, 2, 3)]

    def send(map_ref, leaf_ref, rhs_ref, low_ref, leaf_vmem, rhs_vmem, sems):
        first = pltpu.make_async_copy(leaf_ref, leaf_vmem, sems.at[0])
        second = pltpu.make_async_copy(rhs_ref.at[2], rhs_vmem, sems.at[1])
        first.start()
        second.start()
        low_ref[2 * B :] = jnp.full((16, C), map_ref[2, 0].astype(F32), F32).astype(BF)
        first.wait()
        low_ref[:B] = leaf_vmem[...].astype(BF)
        second.wait()
        low_ref[B : 2 * B] = rhs_vmem[...].astype(BF)

    low = pl.pallas_call(
        send,
        out_shape=jax.ShapeDtypeStruct((2 * B + 16, C), BF),
        in_specs=[
            pl.BlockSpec(memory_space=pltpu.SMEM),
            pl.BlockSpec(memory_space=pl.ANY),
            pl.BlockSpec(memory_space=pl.ANY),
        ],
        out_specs=pl.BlockSpec(memory_space=pltpu.VMEM),
        scratch_shapes=[
            pltpu.VMEM((B, C), F32),
            pltpu.VMEM((B, C), F32),
            pltpu.SemaphoreType.DMA((2,)),
        ],
        compiler_params=pltpu.CompilerParams(vmem_limit_bytes=SMALL),
    )(block_map, leaf_update, rhs)
    got = gather_x(low)
    w_low, b_low, w_mid, b_mid, w_top = [
        relay(w) for w in (inv_low, couple_low, inv_mid, couple_mid, inv_top)
    ]

    def gather_low(s, refs, extra):
        goal = [r[2 * B : 2 * B + 16, :].astype(F32)[:1] for r in refs[:4]]
        child = [r[:B, :].astype(F32) for r in refs[:4]]
        slot = (s[X] + 4) * 8 + s[ROW]
        update = same(goal[0], slot) * child[0] + same(goal[2], slot) * child[2]
        extra[0][...] = update
        message = extra[1]
        rhs_ref = refs[4]
        message[:B] = rhs_ref[1].astype(BF)
        message[B : 2 * B] = rhs_ref[0].astype(BF)
        message[2 * B : 2 * B + 16] = jnp.full((16, C), s[T1].astype(F32), F32).astype(BF)
        message[2 * B + 16 : 2 * B + 32] = jnp.full((16, C), s[T0].astype(F32), F32).astype(BF)
        extra[2][:B] = rhs_ref[0].astype(BF)
        extra[2][B:] = jnp.full((16, C), s[T0].astype(F32), F32).astype(BF)
        for k in range(4):
            slot = (s[X] ^ k) * 8 + s[ROW]
            yield s[X] ^ k, (
                refs[k][B : 2 * B, :].astype(F32)
                + same(goal[k], slot) * child[k]
                + same(goal[k ^ 2], slot) * child[k ^ 2]
            )

    own, others, update, to_y1, to_y3 = forward(
        w_low,
        scal,
        [*got, rhs],
        gather_low,
        extras=[((B, C), F32), ((2 * B + 32, C), BF), ((B + 16, C), BF)],
    )
    from_y1 = swap(to_y1, "leaf", 4)
    from_y3 = swap(to_y3, "leaf", 12)
    from_y2 = swap(to_y3, "leaf", 8)
    y_low = reduce_row(own, others)

    def gather_plain(s, refs, extra):
        for k in range(4):
            yield s[X] ^ k, refs[k][...]

    own, others = forward(b_low, scal, gather_x(y_low.astype(BF)), gather_plain)
    children = update - reduce_row(own, others)

    theirs = swap(children.astype(BF), "leaf", 4)

    def extend_mid(s, own_ref, other_ref, rhs_ref, y1_ref, pair_ref, up_ref):
        position = (s[Y] & 1) * 4 + s[X]
        goal_own = jnp.full((1, C), s[T1].astype(F32), F32)
        goal_other = y1_ref[2 * B : 2 * B + 16, :].astype(F32)[:1]

        def landed(slot):
            return same(goal_own, slot) * own_ref[...] + same(goal_other, slot) * other_ref[
                ...
            ].astype(F32)

        slot = position * 8 + s[ROW]
        pair_ref[0] = (rhs_ref[1] + landed(slot)).astype(BF)
        up_ref[...] = landed(slot + 64)
        slot = (position ^ 4) * 8 + s[ROW]
        pair_ref[1] = (y1_ref[:B, :].astype(F32) + landed(slot)).astype(BF)

    pair, update = small(
        extend_mid, [((2, B, C), BF), ((B, C), F32)], scal, children, theirs, rhs, from_y1
    )

    def gather_mid(s, refs, extra):
        for k in range(4):
            for j in range(2):
                yield ((s[Y] & 1) ^ j) * 4 + (s[X] ^ k), refs[k][j]

    own, others = forward(w_mid, scal, gather_x(pair), gather_mid)
    y_mid = reduce_row(own, others)
    half = y_mid.astype(BF)

    def join(s, a_ref, b_ref, out_ref):
        out_ref[0] = a_ref[...]
        out_ref[1] = b_ref[...]

    (pair,) = small(join, [((2, B, C), BF)], scal, half, swap(half, "leaf", 4))
    own, others = forward(b_mid, scal, gather_x(pair), gather_mid)
    children = update - reduce_row(own, others)
    half = children.astype(BF)

    def flip(s, low_ref, mid_ref, low_out, mid_out):
        low_out[...] = low_ref[...].T
        mid_out[...] = mid_ref[...].T

    turned_low, turned_mid = small(flip, [((C, B), F32)] * 2, scal, y_low, y_mid)

    moved = [swap(half, "leaf", 4 * k) for k in STEPS]

    def extend_top(s, own_ref, m1, m3, m2, rhs_ref, y1_ref, y3_ref, y2_ref, out_ref):
        child = [own_ref[...], m1[...].astype(F32), m2[...].astype(F32), m3[...].astype(F32)]
        base = [rhs_ref[0], y1_ref[B : 2 * B, :], y2_ref[:B, :], y3_ref[:B, :]]
        goal = [
            jnp.full((1, C), s[T0].astype(F32), F32),
            y1_ref[2 * B + 16 : 2 * B + 32, :].astype(F32)[:1],
            y2_ref[B : B + 16, :].astype(F32)[:1],
            y3_ref[B : B + 16, :].astype(F32)[:1],
        ]
        for k in range(4):
            slot = ((s[Y] ^ k) * 4 + s[X]) * 8 + s[ROW]
            out_ref[k] = (
                base[k].astype(F32)
                + same(goal[k], slot) * child[k]
                + same(goal[k ^ 2], slot) * child[k ^ 2]
            ).astype(BF)

    (column,) = small(
        extend_top, [((4, B, C), BF)], scal, children, *moved, rhs, from_y1, from_y3, from_y2
    )

    def gather_top(s, refs, extra):
        for k in range(4):
            for j in range(4):
                yield (s[Y] ^ j) * 4 + (s[X] ^ k), refs[k][j]

    own, others = forward(w_top, scal, gather_x(column), gather_top)

    def turn(s, total_ref, out_ref):
        out_ref[...] = total_ref[...].T.astype(BF)

    (half,) = small(turn, [((C, B), BF)], scal, reduce_row(own, others))
    pieces = gather_row(half)
    got = [swap(transposed(w_top, scal, pieces, only=k)[0], "leaf", k) for k in (2, 1, 3)]
    (own,) = transposed(w_top, scal, pieces, only=0)

    def total(planes):
        return own[planes] + sum(g[planes].astype(F32) for g in got)

    pair, cross = total(slice(0, 2)), total(slice(2, 4)).astype(BF)
    from_1, from_3 = swap(cross, "leaf", 4).astype(F32), swap(cross, "leaf", 12).astype(F32)
    from_2 = swap(pair.astype(BF), "leaf", 8).astype(F32)
    x_top = pair[0] + from_2[1] + from_1[0] + from_3[1]
    x_other = pair[1] + from_2[0] + from_1[1] + from_3[0]
    down_mid = jnp.where(block_map[0, 0] == leaf * 8 + row, x_top, x_other)
    half = down_mid.astype(BF)

    down_half = half
    parts = transposed(b_mid, scal, gather_row(half))
    got = [swap(parts[k], "leaf", k) for k in STEPS]
    full, cross = [parts[0][j] + sum(g[j].astype(F32) for g in got) for j in range(2)]
    coupled = full + swap(cross.astype(BF), "leaf", 4).astype(F32)
    half = (turned_mid - coupled).astype(BF)
    parts = transposed(w_mid, scal, gather_row(half))
    got = [swap(parts[k], "leaf", k) for k in STEPS]

    def pair_mid(s, own_ref, a, b, c, down_ref, full_ref, out_ref):
        for j in range(2):
            total = own_ref[j] + a[j].astype(F32) + b[j].astype(F32) + c[j].astype(F32)
            full_ref[j] = total
            out_ref[1 - j] = total.astype(BF)
        out_ref[2] = down_ref[...]

    full, sent = small(
        pair_mid, [((2, C, B), F32), ((3, C, B), BF)], scal, parts[0], *got, down_half
    )

    def choose(s, target, base, blocks):
        down = None
        goal = jnp.full((1, B), target.astype(F32), F32)
        for slot, block in zip(base, blocks):
            term = block * same(goal, slot)
            down = term if down is None else down + term
        return down

    def end_mid(s, full_ref, got_ref, down_ref, x_ref, out_ref, half_ref):
        own = full_ref[0] + got_ref[0].astype(F32)
        other = full_ref[1] + got_ref[1].astype(F32)
        x_ref[...] = own
        position = (s[Y] & 1) * 4 + s[X]
        slot, far = position * 8 + s[ROW], (position ^ 4) * 8 + s[ROW]
        down = choose(
            s,
            s[T1],
            (slot, slot + 64, far, far + 64),
            (own, down_ref[...], other, got_ref[2].astype(F32)),
        )
        out_ref[...] = down
        half_ref[...] = down.astype(BF)

    x_mid, down_low, half = small(
        end_mid,
        [((C, B), F32), ((C, B), F32), ((C, B), BF)],
        scal,
        full,
        swap(sent, "leaf", 4),
        down_mid,
    )

    down_half = half
    parts = transposed(b_low, scal, gather_row(half))
    got = [swap(parts[k], "leaf", k) for k in STEPS]

    coupled = parts[0][0] + sum(g[0].astype(F32) for g in got)
    half = (turned_low - coupled).astype(BF)
    parts = transposed(w_low, scal, gather_row(half), down_half)
    got = [swap(parts[k], "leaf", k) for k in STEPS]

    def end_low(s, own_ref, a, b, c, down_ref, top_ref, mid_ref, sol_ref, leaf_ref):
        own, other = [
            own_ref[j] + a[j].astype(F32) + b[j].astype(F32) + c[j].astype(F32) for j in range(2)
        ]
        sol_ref[0] = top_ref[...].T
        sol_ref[1] = mid_ref[...].T
        sol_ref[2] = own.T
        slot, far = s[X] * 8 + s[ROW], (s[X] ^ 2) * 8 + s[ROW]
        leaf_ref[...] = choose(
            s,
            s[T2],
            (slot, slot + 32, far, far + 32),
            (own, down_ref[...], other, c[2].astype(F32)),
        ).T

    solved, leaf_solution = small(
        end_low,
        [((3, B, C), F32), ((B, C), F32)],
        scal,
        parts[0],
        *got,
        down_low,
        x_top,
        x_mid,
    )
    return (solved, leaf_solution)


def solution(mesh):
    return jax.shard_map(
        shards,
        mesh=mesh,
        in_specs=(
            P(("leaf", "row"), None),
            P(None, ("leaf", "row"), None),
            P(None, "leaf", None, "row", None),
            P(None, "leaf", None, "row", None),
            P(None, "leaf", None, "row", None),
            P(None, "leaf", None, "row", None),
            P(None, "leaf", None, "row", None),
            P(None, ("leaf", "row")),
        ),
        out_specs=(P(None, ("leaf", "row"), None), P(("leaf", "row"), None)),
        check_vma=False,
    )
```

```python
import functools

import jax
import jax.numpy as jnp
from jax import lax
from jax.experimental import pallas as pl
from jax.experimental.pallas import tpu as pltpu
from jax.sharding import PartitionSpec as P

BF = jnp.bfloat16
F32 = jnp.float32
B = 128
C = 256
STEPS = (1, 3, 2)
X, Y, Z, CORE, ROW, T0, T1, T2 = range(8)
SMALL = 8 << 20


def swap(value, axis, mask):
    count = lax.axis_size(axis)
    return lax.ppermute(value, axis, [(i, i ^ mask) for i in range(count)])


def small(body, outs, scal, *ins):
    return pl.pallas_call(
        body,
        out_shape=[jax.ShapeDtypeStruct(*o) for o in outs],
        in_specs=[pl.BlockSpec(memory_space=pltpu.SMEM)]
        + [pl.BlockSpec(memory_space=pltpu.VMEM)] * len(ins),
        out_specs=[pl.BlockSpec(memory_space=pltpu.VMEM)] * len(outs),
        compiler_params=pltpu.CompilerParams(vmem_limit_bytes=SMALL),
        cost_estimate=pl.CostEstimate(flops=1 << 18, bytes_accessed=1 << 19, transcendentals=0),
    )(scal, *ins)


def relay_body(groups, real_ref, imag_ref, out_ref):
    span = C // groups
    shift = span.bit_length() - 1
    target = lax.broadcasted_iota(jnp.int32, (C, C), 0)
    source = lax.broadcasted_iota(jnp.int32, (C, C), 1)
    place = (source == (target & span - 1) * groups + (target >> shift)).astype(BF)

    for chunk in range(B * groups // C):
        rows = slice(chunk * C, (chunk + 1) * C)
        both = jnp.concatenate([real_ref[rows, :], imag_ref[rows, :]], axis=1)
        moved = jnp.dot(place, both, preferred_element_type=F32).astype(BF)
        for p in range(groups):
            out_ref[chunk * span : (chunk + 1) * span, p * C : (p + 1) * C] = moved[
                p * span : (p + 1) * span
            ]


def relay(weights):
    _, rows, groups, _, width = weights.shape
    flat = weights.reshape(2 * rows * groups, width)
    tiles = rows // B
    return pl.pallas_call(
        functools.partial(relay_body, groups),
        grid=(tiles,),
        out_shape=jax.ShapeDtypeStruct((rows, groups * C), BF),
        in_specs=[
            pl.BlockSpec((B * groups, B), lambda t: (t, 0)),
            pl.BlockSpec((B * groups, B), lambda t: (t + tiles, 0)),
        ],
        out_specs=pl.BlockSpec((B, groups * C), lambda t: (t, 0)),
        compiler_params=pltpu.CompilerParams(vmem_limit_bytes=2 * SMALL),
        cost_estimate=pl.CostEstimate(
            flops=4 * rows * groups * C * B, bytes_accessed=8 * rows * groups * B, transcendentals=0
        ),
    )(flat, flat)


def call(body, outs, scal, ins, scratch, flops):
    limit = 2 * ins[0].size + (12 << 20)
    return pl.pallas_call(
        body,
        out_shape=[jax.ShapeDtypeStruct(*o) for o in outs],
        in_specs=[pl.BlockSpec(memory_space=pltpu.SMEM)]
        + [pl.BlockSpec(memory_space=pltpu.VMEM)] * len(ins),
        out_specs=[pl.BlockSpec(memory_space=pltpu.VMEM)] * len(outs),
        scratch_shapes=scratch,
        compiler_params=pltpu.CompilerParams(vmem_limit_bytes=limit),
        cost_estimate=pl.CostEstimate(flops=flops, bytes_accessed=1 << 20, transcendentals=0),
    )(scal, *ins)


def forward(weights, scal, ins, gather, extras=()):
    rows, depth = weights.shape
    count = len(ins)

    def body(s, w_ref, *refs):
        in_refs, out_refs, vec = refs[:count], refs[count:-1], refs[-1]
        for index, block in gather(s, in_refs, out_refs[2:]):
            start = pl.multiple_of(index * C, C)
            block = block.astype(F32)
            vec[pl.ds(start, B), :] = block.astype(BF)
            vec[pl.ds(start + B, B), :] = jnp.concatenate(
                [-block[:, B:], block[:, :B]], axis=1
            ).astype(BF)
        swapped = s[CORE] == 1

        @pl.loop(0, 4)
        def _(k):
            start = pl.multiple_of((s[Z] ^ k) * C, C)
            prod = jnp.dot(w_ref[pl.ds(start, C), :], vec[...], preferred_element_type=F32)
            upper, lower = prod[:B], prod[B:]
            out_refs[0][k] = jnp.where(swapped, lower, upper)
            out_refs[1][k] = jnp.where(swapped, upper, lower).astype(BF)

    outs = [((4, B, C), F32), ((4, B, C), BF)] + list(extras)
    return call(
        body, outs, scal, [weights, *ins], [pltpu.VMEM((depth, C), BF)], 2 * rows * depth * C
    )


def transposed(weights, scal, pieces, paired=None, only=None):
    rows, depth = weights.shape
    tiles = depth // (4 * C)
    ins = list(pieces.values()) + ([] if paired is None else [paired])
    keys = list(pieces)
    count = len(ins)
    mask = tiles - 1
    used = count + (4 if only is None else 1)

    def body(s, w_ref, *refs):
        in_refs, out_refs, scratch = refs[:count], refs[count:used], refs[used:]
        vec = scratch[0]
        for (zz, j), ref in zip(keys, in_refs):
            slot = 2 * (s[Z] ^ zz) + (s[CORE] ^ j)
            vec[:, pl.ds(pl.multiple_of(slot * B, B), B)] = ref[...]

        def block(position):
            part = jnp.dot(
                vec[...],
                w_ref[:, pl.ds(pl.multiple_of(position * C, C), C)],
                preferred_element_type=F32,
            )
            return jnp.concatenate(
                [part[:B, :B] - part[B:, B:], part[B:, :B] + part[:B, B:]], axis=0
            )

        if only is not None:

            @pl.loop(0, 4)
            def _(plane):
                j = (plane & 1) * 2 + (plane >> 1)
                value = block((s[Y] ^ j) * 4 + (s[X] ^ only))
                out_refs[0][plane] = value.astype(out_refs[0].dtype)

            return
        acc = scratch[1]

        @pl.loop(0, 4 * tiles, unroll=2)
        def _(step):
            k, j = step & 3, step >> 2
            acc[k, j] = block(((s[Y] & mask) ^ j) * 4 + (s[X] ^ k))

        for k in range(4):
            kind = out_refs[k].dtype
            out_refs[k][:tiles] = acc[k].astype(kind)
            if paired is not None:
                out_refs[k][1] = acc[k ^ 2, 0].astype(kind)
        if paired is not None:
            out_refs[2][2] = in_refs[-1][...]

    scratch_shapes = [pltpu.VMEM((C, rows), BF)]
    if only is not None:
        outs = [((4, C, B), BF if only else F32)]
    else:
        scratch_shapes.append(pltpu.VMEM((4, tiles, C, B), F32))
        planes = [1, 1, 1, 1] if paired is None else [2, 2, 3, 2]
        outs = [((tiles * planes[k], C, B), BF if k else F32) for k in range(4)]
    return call(
        body, outs, scal, [weights, *ins], scratch_shapes, 2 * rows * depth * C
    )


def same(goal, slot):
    return (goal == slot.astype(F32)).astype(F32)


def shards(leaf_update, rhs, inv_top, inv_mid, inv_low, couple_mid, couple_low, block_map):
    leaf = lax.axis_index("leaf")
    row = lax.axis_index("row")
    scal = jnp.concatenate(
        [jnp.stack([leaf & 3, leaf >> 2, row >> 1, row & 1, row]).astype(jnp.int32), block_map[:, 0]]
    )

    def reduce_row(own, other):
        other = swap(other, "row", 1)
        parts = {k: own[k] + other[k].astype(F32) for k in range(4)}
        total = parts[0]
        for k in STEPS:
            total = total + swap(parts[k].astype(BF), "row", 2 * k).astype(F32)
        return total

    def gather_row(own):
        pieces = {(0, 0): own}
        for k in STEPS:
            pieces[(k, 0)] = swap(own, "row", 2 * k)
        for k in (0,) + STEPS:
            pieces[(k, 1)] = swap(pieces[(k, 0)], "row", 1)
        return pieces

    def gather_x(value):
        return [value] + [swap(value, "leaf", k) for k in (1, 2, 3)]

    def send(map_ref, leaf_ref, rhs_ref, low_ref, leaf_vmem, rhs_vmem, sems):
        first = pltpu.make_async_copy(leaf_ref, leaf_vmem, sems.at[0])
        second = pltpu.make_async_copy(rhs_ref.at[2], rhs_vmem, sems.at[1])
        first.start()
        second.start()
        low_ref[2 * B :] = jnp.full((16, C), map_ref[2, 0].astype(F32), F32).astype(BF)
        first.wait()
        low_ref[:B] = leaf_vmem[...].astype(BF)
        second.wait()
        low_ref[B : 2 * B] = rhs_vmem[...].astype(BF)

    low = pl.pallas_call(
        send,
        out_shape=jax.ShapeDtypeStruct((2 * B + 16, C), BF),
        in_specs=[
            pl.BlockSpec(memory_space=pltpu.SMEM),
            pl.BlockSpec(memory_space=pl.ANY),
            pl.BlockSpec(memory_space=pl.ANY),
        ],
        out_specs=pl.BlockSpec(memory_space=pltpu.VMEM),
        scratch_shapes=[
            pltpu.VMEM((B, C), F32),
            pltpu.VMEM((B, C), F32),
            pltpu.SemaphoreType.DMA((2,)),
        ],
        compiler_params=pltpu.CompilerParams(vmem_limit_bytes=SMALL),
    )(block_map, leaf_update, rhs)
    got = gather_x(low)
    w_low, b_low, w_mid, b_mid, w_top = [
        relay(w) for w in (inv_low, couple_low, inv_mid, couple_mid, inv_top)
    ]

    def gather_low(s, refs, extra):
        goal = [r[2 * B : 2 * B + 16, :].astype(F32)[:1] for r in refs[:4]]
        child = [r[:B, :].astype(F32) for r in refs[:4]]
        slot = (s[X] + 4) * 8 + s[ROW]
        update = same(goal[0], slot) * child[0] + same(goal[2], slot) * child[2]
        extra[0][...] = update
        message = extra[1]
        rhs_ref = refs[4]
        message[:B] = rhs_ref[1].astype(BF)
        message[B : 2 * B] = rhs_ref[0].astype(BF)
        message[2 * B : 2 * B + 16] = jnp.full((16, C), s[T1].astype(F32), F32).astype(BF)
        message[2 * B + 16 : 2 * B + 32] = jnp.full((16, C), s[T0].astype(F32), F32).astype(BF)
        extra[2][:B] = rhs_ref[0].astype(BF)
        extra[2][B:] = jnp.full((16, C), s[T0].astype(F32), F32).astype(BF)
        for k in range(4):
            slot = (s[X] ^ k) * 8 + s[ROW]
            yield s[X] ^ k, (
                refs[k][B : 2 * B, :].astype(F32)
                + same(goal[k], slot) * child[k]
                + same(goal[k ^ 2], slot) * child[k ^ 2]
            )

    own, others, update, to_y1, to_y3 = forward(
        w_low,
        scal,
        [*got, rhs],
        gather_low,
        extras=[((B, C), F32), ((2 * B + 32, C), BF), ((B + 16, C), BF)],
    )
    from_y1 = swap(to_y1, "leaf", 4)
    from_y3 = swap(to_y3, "leaf", 12)
    from_y2 = swap(to_y3, "leaf", 8)
    y_low = reduce_row(own, others)

    def gather_plain(s, refs, extra):
        for k in range(4):
            yield s[X] ^ k, refs[k][...]

    own, others = forward(b_low, scal, gather_x(y_low.astype(BF)), gather_plain)
    children = update - reduce_row(own, others)

    theirs = swap(children.astype(BF), "leaf", 4)

    def extend_mid(s, own_ref, other_ref, rhs_ref, y1_ref, pair_ref, up_ref):
        position = (s[Y] & 1) * 4 + s[X]
        goal_own = jnp.full((1, C), s[T1].astype(F32), F32)
        goal_other = y1_ref[2 * B : 2 * B + 16, :].astype(F32)[:1]

        def landed(slot):
            return same(goal_own, slot) * own_ref[...] + same(goal_other, slot) * other_ref[
                ...
            ].astype(F32)

        slot = position * 8 + s[ROW]
        pair_ref[0] = (rhs_ref[1] + landed(slot)).astype(BF)
        up_ref[...] = landed(slot + 64)
        slot = (position ^ 4) * 8 + s[ROW]
        pair_ref[1] = (y1_ref[:B, :].astype(F32) + landed(slot)).astype(BF)

    pair, update = small(
        extend_mid, [((2, B, C), BF), ((B, C), F32)], scal, children, theirs, rhs, from_y1
    )

    def gather_mid(s, refs, extra):
        for k in range(4):
            for j in range(2):
                yield ((s[Y] & 1) ^ j) * 4 + (s[X] ^ k), refs[k][j]

    own, others = forward(w_mid, scal, gather_x(pair), gather_mid)
    y_mid = reduce_row(own, others)
    half = y_mid.astype(BF)

    def join(s, a_ref, b_ref, out_ref):
        out_ref[0] = a_ref[...]
        out_ref[1] = b_ref[...]

    (pair,) = small(join, [((2, B, C), BF)], scal, half, swap(half, "leaf", 4))
    own, others = forward(b_mid, scal, gather_x(pair), gather_mid)
    children = update - reduce_row(own, others)
    half = children.astype(BF)

    def flip(s, low_ref, mid_ref, low_out, mid_out):
        low_out[...] = low_ref[...].T
        mid_out[...] = mid_ref[...].T

    turned_low, turned_mid = small(flip, [((C, B), F32)] * 2, scal, y_low, y_mid)

    moved = [swap(half, "leaf", 4 * k) for k in STEPS]

    def extend_top(s, own_ref, m1, m3, m2, rhs_ref, y1_ref, y3_ref, y2_ref, out_ref):
        child = [own_ref[...], m1[...].astype(F32), m2[...].astype(F32), m3[...].astype(F32)]
        base = [rhs_ref[0], y1_ref[B : 2 * B, :], y2_ref[:B, :], y3_ref[:B, :]]
        goal = [
            jnp.full((1, C), s[T0].astype(F32), F32),
            y1_ref[2 * B + 16 : 2 * B + 32, :].astype(F32)[:1],
            y2_ref[B : B + 16, :].astype(F32)[:1],
            y3_ref[B : B + 16, :].astype(F32)[:1],
        ]
        for k in range(4):
            slot = ((s[Y] ^ k) * 4 + s[X]) * 8 + s[ROW]
            out_ref[k] = (
                base[k].astype(F32)
                + same(goal[k], slot) * child[k]
                + same(goal[k ^ 2], slot) * child[k ^ 2]
            ).astype(BF)

    (column,) = small(
        extend_top, [((4, B, C), BF)], scal, children, *moved, rhs, from_y1, from_y3, from_y2
    )

    def gather_top(s, refs, extra):
        for k in range(4):
            for j in range(4):
                yield (s[Y] ^ j) * 4 + (s[X] ^ k), refs[k][j]

    own, others = forward(w_top, scal, gather_x(column), gather_top)

    def turn(s, total_ref, out_ref):
        out_ref[...] = total_ref[...].T.astype(BF)

    (half,) = small(turn, [((C, B), BF)], scal, reduce_row(own, others))
    pieces = gather_row(half)
    got = [swap(transposed(w_top, scal, pieces, only=k)[0], "leaf", k) for k in (2, 1, 3)]
    (own,) = transposed(w_top, scal, pieces, only=0)

    def total(planes):
        return own[planes] + sum(g[planes].astype(F32) for g in got)

    pair, cross = total(slice(0, 2)), total(slice(2, 4)).astype(BF)
    from_1, from_3 = swap(cross, "leaf", 4).astype(F32), swap(cross, "leaf", 12).astype(F32)
    from_2 = swap(pair.astype(BF), "leaf", 8).astype(F32)
    x_top = pair[0] + from_2[1] + from_1[0] + from_3[1]
    x_other = pair[1] + from_2[0] + from_1[1] + from_3[0]
    down_mid = jnp.where(block_map[0, 0] == leaf * 8 + row, x_top, x_other)
    half = down_mid.astype(BF)

    down_half = half
    parts = transposed(b_mid, scal, gather_row(half))
    got = [swap(parts[k], "leaf", k) for k in STEPS]
    full, cross = [parts[0][j] + sum(g[j].astype(F32) for g in got) for j in range(2)]
    coupled = full + swap(cross.astype(BF), "leaf", 4).astype(F32)
    half = (turned_mid - coupled).astype(BF)
    parts = transposed(w_mid, scal, gather_row(half))
    got = [swap(parts[k], "leaf", k) for k in STEPS]

    def pair_mid(s, own_ref, a, b, c, down_ref, full_ref, out_ref):
        for j in range(2):
            total = own_ref[j] + a[j].astype(F32) + b[j].astype(F32) + c[j].astype(F32)
            full_ref[j] = total
            out_ref[1 - j] = total.astype(BF)
        out_ref[2] = down_ref[...]

    full, sent = small(
        pair_mid, [((2, C, B), F32), ((3, C, B), BF)], scal, parts[0], *got, down_half
    )

    def choose(s, target, base, blocks):
        down = None
        goal = jnp.full((1, B), target.astype(F32), F32)
        for slot, block in zip(base, blocks):
            term = block * same(goal, slot)
            down = term if down is None else down + term
        return down

    def end_mid(s, full_ref, got_ref, down_ref, x_ref, out_ref, half_ref):
        own = full_ref[0] + got_ref[0].astype(F32)
        other = full_ref[1] + got_ref[1].astype(F32)
        x_ref[...] = own
        position = (s[Y] & 1) * 4 + s[X]
        slot, far = position * 8 + s[ROW], (position ^ 4) * 8 + s[ROW]
        down = choose(
            s,
            s[T1],
            (slot, slot + 64, far, far + 64),
            (own, down_ref[...], other, got_ref[2].astype(F32)),
        )
        out_ref[...] = down
        half_ref[...] = down.astype(BF)

    x_mid, down_low, half = small(
        end_mid,
        [((C, B), F32), ((C, B), F32), ((C, B), BF)],
        scal,
        full,
        swap(sent, "leaf", 4),
        down_mid,
    )

    down_half = half
    parts = transposed(b_low, scal, gather_row(half))
    got = [swap(parts[k], "leaf", k) for k in STEPS]

    coupled = parts[0][0] + sum(g[0].astype(F32) for g in got)
    half = (turned_low - coupled).astype(BF)
    parts = transposed(w_low, scal, gather_row(half), down_half)
    got = [swap(parts[k], "leaf", k) for k in STEPS]

    def end_low(s, own_ref, a, b, c, down_ref, top_ref, mid_ref, sol_ref, leaf_ref):
        own, other = [
            own_ref[j] + a[j].astype(F32) + b[j].astype(F32) + c[j].astype(F32) for j in range(2)
        ]
        sol_ref[0] = top_ref[...].T
        sol_ref[1] = mid_ref[...].T
        sol_ref[2] = own.T
        slot, far = s[X] * 8 + s[ROW], (s[X] ^ 2) * 8 + s[ROW]
        leaf_ref[...] = choose(
            s,
            s[T2],
            (slot, slot + 32, far, far + 32),
            (own, down_ref[...], other, c[2].astype(F32)),
        ).T

    solved, leaf_solution = small(
        end_low,
        [((3, B, C), F32), ((B, C), F32)],
        scal,
        parts[0],
        *got,
        down_low,
        x_top,
        x_mid,
    )
    return (solved, leaf_solution)


def solution(mesh):
    return jax.shard_map(
        shards,
        mesh=mesh,
        in_specs=(
            P(("leaf", "row"), None),
            P(None, ("leaf", "row"), None),
            P(None, "leaf", None, "row", None),
            P(None, "leaf", None, "row", None),
            P(None, "leaf", None, "row", None),
            P(None, "leaf", None, "row", None),
            P(None, "leaf", None, "row", None),
            P(None, ("leaf", "row")),
        ),
        out_specs=(P(None, ("leaf", "row"), None), P(("leaf", "row"), None)),
        check_vma=False,
    )
```

```python
import functools

import jax
import jax.numpy as jnp
from jax import lax
from jax.experimental import pallas as pl
from jax.experimental.pallas import tpu as pltpu
from jax.sharding import PartitionSpec as P

BF = jnp.bfloat16
F32 = jnp.float32
B = 128
C = 256
STEPS = (1, 3, 2)
X, Y, Z, CORE, ROW, T0, T1, T2 = range(8)
SMALL = 8 << 20


def swap(value, axis, mask):
    count = lax.axis_size(axis)
    return lax.ppermute(value, axis, [(i, i ^ mask) for i in range(count)])


def small(body, outs, scal, *ins):
    return pl.pallas_call(
        body,
        out_shape=[jax.ShapeDtypeStruct(*o) for o in outs],
        in_specs=[pl.BlockSpec(memory_space=pltpu.SMEM)]
        + [pl.BlockSpec(memory_space=pltpu.VMEM)] * len(ins),
        out_specs=[pl.BlockSpec(memory_space=pltpu.VMEM)] * len(outs),
        compiler_params=pltpu.CompilerParams(vmem_limit_bytes=SMALL),
        cost_estimate=pl.CostEstimate(flops=1 << 18, bytes_accessed=1 << 19, transcendentals=0),
    )(scal, *ins)


def relay_body(groups, real_ref, imag_ref, out_ref):
    span = C // groups
    shift = span.bit_length() - 1
    target = lax.broadcasted_iota(jnp.int32, (C, C), 0)
    source = lax.broadcasted_iota(jnp.int32, (C, C), 1)
    place = (source == (target & span - 1) * groups + (target >> shift)).astype(BF)

    for chunk in range(B * groups // C):
        rows = slice(chunk * C, (chunk + 1) * C)
        both = jnp.concatenate([real_ref[rows, :], imag_ref[rows, :]], axis=1)
        moved = jnp.dot(place, both, preferred_element_type=F32).astype(BF)
        for p in range(groups):
            out_ref[chunk * span : (chunk + 1) * span, p * C : (p + 1) * C] = moved[
                p * span : (p + 1) * span
            ]


def relay(weights):
    _, rows, groups, _, width = weights.shape
    flat = weights.reshape(2 * rows * groups, width)
    tiles = rows // B
    return pl.pallas_call(
        functools.partial(relay_body, groups),
        grid=(tiles,),
        out_shape=jax.ShapeDtypeStruct((rows, groups * C), BF),
        in_specs=[
            pl.BlockSpec((B * groups, B), lambda t: (t, 0)),
            pl.BlockSpec((B * groups, B), lambda t: (t + tiles, 0)),
        ],
        out_specs=pl.BlockSpec((B, groups * C), lambda t: (t, 0)),
        compiler_params=pltpu.CompilerParams(vmem_limit_bytes=2 * SMALL),
        cost_estimate=pl.CostEstimate(
            flops=4 * rows * groups * C * B, bytes_accessed=8 * rows * groups * B, transcendentals=0
        ),
    )(flat, flat)


def call(body, outs, scal, ins, scratch, flops):
    limit = 2 * ins[0].size + (12 << 20)
    return pl.pallas_call(
        body,
        out_shape=[jax.ShapeDtypeStruct(*o) for o in outs],
        in_specs=[pl.BlockSpec(memory_space=pltpu.SMEM)]
        + [pl.BlockSpec(memory_space=pltpu.VMEM)] * len(ins),
        out_specs=[pl.BlockSpec(memory_space=pltpu.VMEM)] * len(outs),
        scratch_shapes=scratch,
        compiler_params=pltpu.CompilerParams(vmem_limit_bytes=limit),
        cost_estimate=pl.CostEstimate(flops=flops, bytes_accessed=1 << 20, transcendentals=0),
    )(scal, *ins)


def forward(weights, scal, ins, gather, extras=()):
    rows, depth = weights.shape
    count = len(ins)

    def body(s, w_ref, *refs):
        in_refs, out_refs, vec = refs[:count], refs[count:-1], refs[-1]
        for index, block in gather(s, in_refs, out_refs[2:]):
            start = pl.multiple_of(index * C, C)
            block = block.astype(F32)
            vec[pl.ds(start, B), :] = block.astype(BF)
            vec[pl.ds(start + B, B), :] = jnp.concatenate(
                [-block[:, B:], block[:, :B]], axis=1
            ).astype(BF)
        swapped = s[CORE] == 1

        @pl.loop(0, 4)
        def _(k):
            start = pl.multiple_of((s[Z] ^ k) * C, C)
            prod = jnp.dot(w_ref[pl.ds(start, C), :], vec[...], preferred_element_type=F32)
            upper, lower = prod[:B], prod[B:]
            out_refs[0][k] = jnp.where(swapped, lower, upper)
            out_refs[1][k] = jnp.where(swapped, upper, lower).astype(BF)

    outs = [((4, B, C), F32), ((4, B, C), BF)] + list(extras)
    return call(
        body, outs, scal, [weights, *ins], [pltpu.VMEM((depth, C), BF)], 2 * rows * depth * C
    )


def transposed(weights, scal, pieces, paired=None, only=None):
    rows, depth = weights.shape
    tiles = depth // (4 * C)
    ins = list(pieces.values()) + ([] if paired is None else [paired])
    keys = list(pieces)
    count = len(ins)
    mask = tiles - 1
    used = count + (4 if only is None else 1)

    def body(s, w_ref, *refs):
        in_refs, out_refs, scratch = refs[:count], refs[count:used], refs[used:]
        vec = scratch[0]
        for (zz, j), ref in zip(keys, in_refs):
            slot = 2 * (s[Z] ^ zz) + (s[CORE] ^ j)
            vec[:, pl.ds(pl.multiple_of(slot * B, B), B)] = ref[...]

        def block(position):
            part = jnp.dot(
                vec[...],
                w_ref[:, pl.ds(pl.multiple_of(position * C, C), C)],
                preferred_element_type=F32,
            )
            return jnp.concatenate(
                [part[:B, :B] - part[B:, B:], part[B:, :B] + part[:B, B:]], axis=0
            )

        if only is not None:

            @pl.loop(0, 4)
            def _(plane):
                j = (plane & 1) * 2 + (plane >> 1)
                value = block((s[Y] ^ j) * 4 + (s[X] ^ only))
                out_refs[0][plane] = value.astype(out_refs[0].dtype)

            return
        acc = scratch[1]

        @pl.loop(0, 4 * tiles, unroll=2)
        def _(step):
            k, j = step & 3, step >> 2
            acc[k, j] = block(((s[Y] & mask) ^ j) * 4 + (s[X] ^ k))

        for k in range(4):
            kind = out_refs[k].dtype
            out_refs[k][:tiles] = acc[k].astype(kind)
            if paired is not None:
                out_refs[k][1] = acc[k ^ 2, 0].astype(kind)
        if paired is not None:
            out_refs[2][2] = in_refs[-1][...]

    scratch_shapes = [pltpu.VMEM((C, rows), BF)]
    if only is not None:
        outs = [((4, C, B), BF if only else F32)]
    else:
        scratch_shapes.append(pltpu.VMEM((4, tiles, C, B), F32))
        planes = [1, 1, 1, 1] if paired is None else [2, 2, 3, 2]
        outs = [((tiles * planes[k], C, B), BF if k else F32) for k in range(4)]
    return call(
        body, outs, scal, [weights, *ins], scratch_shapes, 2 * rows * depth * C
    )


def same(goal, slot):
    return (goal == slot.astype(F32)).astype(F32)


def shards(leaf_update, rhs, inv_top, inv_mid, inv_low, couple_mid, couple_low, block_map):
    leaf = lax.axis_index("leaf")
    row = lax.axis_index("row")
    scal = jnp.concatenate(
        [jnp.stack([leaf & 3, leaf >> 2, row >> 1, row & 1, row]).astype(jnp.int32), block_map[:, 0]]
    )

    def reduce_row(own, other):
        other = swap(other, "row", 1)
        parts = {k: own[k] + other[k].astype(F32) for k in range(4)}
        total = parts[0]
        for k in STEPS:
            total = total + swap(parts[k].astype(BF), "row", 2 * k).astype(F32)
        return total

    def gather_row(own):
        pieces = {(0, 0): own}
        for k in STEPS:
            pieces[(k, 0)] = swap(own, "row", 2 * k)
        for k in (0,) + STEPS:
            pieces[(k, 1)] = swap(pieces[(k, 0)], "row", 1)
        return pieces

    def gather_x(value):
        return [value] + [swap(value, "leaf", k) for k in (1, 2, 3)]

    def send(map_ref, leaf_ref, rhs_ref, low_ref, leaf_vmem, rhs_vmem, sems):
        first = pltpu.make_async_copy(leaf_ref, leaf_vmem, sems.at[0])
        second = pltpu.make_async_copy(rhs_ref.at[2], rhs_vmem, sems.at[1])
        first.start()
        second.start()
        low_ref[2 * B :] = jnp.full((16, C), map_ref[2, 0].astype(F32), F32).astype(BF)
        first.wait()
        low_ref[:B] = leaf_vmem[...].astype(BF)
        second.wait()
        low_ref[B : 2 * B] = rhs_vmem[...].astype(BF)

    low = pl.pallas_call(
        send,
        out_shape=jax.ShapeDtypeStruct((2 * B + 16, C), BF),
        in_specs=[
            pl.BlockSpec(memory_space=pltpu.SMEM),
            pl.BlockSpec(memory_space=pl.ANY),
            pl.BlockSpec(memory_space=pl.ANY),
        ],
        out_specs=pl.BlockSpec(memory_space=pltpu.VMEM),
        scratch_shapes=[
            pltpu.VMEM((B, C), F32),
            pltpu.VMEM((B, C), F32),
            pltpu.SemaphoreType.DMA((2,)),
        ],
        compiler_params=pltpu.CompilerParams(vmem_limit_bytes=SMALL),
    )(block_map, leaf_update, rhs)
    got = gather_x(low)
    w_low, b_low, w_mid, b_mid, w_top = [
        relay(w) for w in (inv_low, couple_low, inv_mid, couple_mid, inv_top)
    ]

    def gather_low(s, refs, extra):
        goal = [r[2 * B : 2 * B + 16, :].astype(F32)[:1] for r in refs[:4]]
        child = [r[:B, :].astype(F32) for r in refs[:4]]
        slot = (s[X] + 4) * 8 + s[ROW]
        update = same(goal[0], slot) * child[0] + same(goal[2], slot) * child[2]
        extra[0][...] = update
        message = extra[1]
        rhs_ref = refs[4]
        message[:B] = rhs_ref[1].astype(BF)
        message[B:] = jnp.full((16, C), s[T1].astype(F32), F32).astype(BF)
        for k in range(4):
            slot = (s[X] ^ k) * 8 + s[ROW]
            yield s[X] ^ k, (
                refs[k][B : 2 * B, :].astype(F32)
                + same(goal[k], slot) * child[k]
                + same(goal[k ^ 2], slot) * child[k ^ 2]
            )

    own, others, update, to_y1 = forward(
        w_low,
        scal,
        [*got, rhs],
        gather_low,
        extras=[((B, C), F32), ((B + 16, C), BF)],
    )
    from_y1 = swap(to_y1, "leaf", 4)
    y_low = reduce_row(own, others)

    def gather_plain(s, refs, extra):
        for k in range(4):
            yield s[X] ^ k, refs[k][...]

    own, others = forward(b_low, scal, gather_x(y_low.astype(BF)), gather_plain)
    children = update - reduce_row(own, others)

    theirs = swap(children.astype(BF), "leaf", 4)

    def extend_mid(s, own_ref, other_ref, rhs_ref, y1_ref, pair_ref, up_ref):
        position = (s[Y] & 1) * 4 + s[X]
        goal_own = jnp.full((1, C), s[T1].astype(F32), F32)
        goal_other = y1_ref[B : B + 16, :].astype(F32)[:1]

        def landed(slot):
            return same(goal_own, slot) * own_ref[...] + same(goal_other, slot) * other_ref[
                ...
            ].astype(F32)

        slot = position * 8 + s[ROW]
        pair_ref[0] = (rhs_ref[1] + landed(slot)).astype(BF)
        up_ref[...] = landed(slot + 64)
        slot = (position ^ 4) * 8 + s[ROW]
        pair_ref[1] = (y1_ref[:B, :].astype(F32) + landed(slot)).astype(BF)

    pair, update = small(
        extend_mid, [((2, B, C), BF), ((B, C), F32)], scal, children, theirs, rhs, from_y1
    )

    def gather_mid(s, refs, extra):
        for k in range(4):
            for j in range(2):
                yield ((s[Y] & 1) ^ j) * 4 + (s[X] ^ k), refs[k][j]

    own, others = forward(w_mid, scal, gather_x(pair), gather_mid)
    y_mid = reduce_row(own, others)
    half = y_mid.astype(BF)

    def join(s, a_ref, b_ref, out_ref):
        out_ref[0] = a_ref[...]
        out_ref[1] = b_ref[...]

    (pair,) = small(join, [((2, B, C), BF)], scal, half, swap(half, "leaf", 4))
    own, others = forward(b_mid, scal, gather_x(pair), gather_mid)

    def pack(s, up_ref, total_ref, rhs_ref, full_ref, out_ref):
        full = up_ref[...] - total_ref[...]
        full_ref[...] = full
        out_ref[:B] = full.astype(BF)
        out_ref[B : 2 * B] = rhs_ref[0].astype(BF)
        out_ref[2 * B :] = jnp.full((16, C), s[T0].astype(F32), F32).astype(BF)

    children, sent = small(
        pack, [((B, C), F32), ((2 * B + 16, C), BF)], scal, update, reduce_row(own, others), rhs
    )

    def flip(s, low_ref, mid_ref, low_out, mid_out):
        low_out[...] = low_ref[...].T
        mid_out[...] = mid_ref[...].T

    turned_low, turned_mid = small(flip, [((C, B), F32)] * 2, scal, y_low, y_mid)

    moved = [swap(sent, "leaf", 4 * k) for k in (1, 2, 3)]

    def extend_top(s, own_ref, m1, m2, m3, rhs_ref, out_ref):
        others = (m1, m2, m3)
        child = [own_ref[...]] + [m[:B, :].astype(F32) for m in others]
        base = [rhs_ref[0]] + [m[B : 2 * B, :].astype(F32) for m in others]
        goal = [jnp.full((1, C), s[T0].astype(F32), F32)] + [
            m[2 * B :, :].astype(F32)[:1] for m in others
        ]
        for k in range(4):
            slot = ((s[Y] ^ k) * 4 + s[X]) * 8 + s[ROW]
            out_ref[k] = (
                base[k]
                + same(goal[k], slot) * child[k]
                + same(goal[k ^ 2], slot) * child[k ^ 2]
            ).astype(BF)

    (column,) = small(
        extend_top, [((4, B, C), BF)], scal, children, *moved, rhs
    )

    def gather_top(s, refs, extra):
        for k in range(4):
            for j in range(4):
                yield (s[Y] ^ j) * 4 + (s[X] ^ k), refs[k][j]

    own, others = forward(w_top, scal, gather_x(column), gather_top)

    def turn(s, total_ref, out_ref):
        out_ref[...] = total_ref[...].T.astype(BF)

    (half,) = small(turn, [((C, B), BF)], scal, reduce_row(own, others))
    b_mid = relay(lax.optimization_barrier((couple_mid, half))[0])
    pieces = gather_row(half)
    got = [swap(transposed(w_top, scal, pieces, only=k)[0], "leaf", k) for k in (2, 1, 3)]
    (own,) = transposed(w_top, scal, pieces, only=0)

    def total(planes):
        return own[planes] + sum(g[planes].astype(F32) for g in got)

    pair, cross = total(slice(0, 2)), total(slice(2, 4)).astype(BF)
    from_1, from_3 = swap(cross, "leaf", 4).astype(F32), swap(cross, "leaf", 12).astype(F32)
    from_2 = swap(pair.astype(BF), "leaf", 8).astype(F32)
    x_top = pair[0] + from_2[1] + from_1[0] + from_3[1]
    x_other = pair[1] + from_2[0] + from_1[1] + from_3[0]
    down_mid = jnp.where(block_map[0, 0] == leaf * 8 + row, x_top, x_other)
    half = down_mid.astype(BF)

    down_half = half
    w_mid = relay(lax.optimization_barrier((inv_mid, half))[0])
    parts = transposed(b_mid, scal, gather_row(half))
    got = [swap(parts[k], "leaf", k) for k in STEPS]
    full, cross = [parts[0][j] + sum(g[j].astype(F32) for g in got) for j in range(2)]
    coupled = full + swap(cross.astype(BF), "leaf", 4).astype(F32)
    half = (turned_mid - coupled).astype(BF)
    parts = transposed(w_mid, scal, gather_row(half))
    got = [swap(parts[k], "leaf", k) for k in STEPS]

    def pair_mid(s, own_ref, a, b, c, down_ref, full_ref, out_ref):
        for j in range(2):
            total = own_ref[j] + a[j].astype(F32) + b[j].astype(F32) + c[j].astype(F32)
            full_ref[j] = total
            out_ref[1 - j] = total.astype(BF)
        out_ref[2] = down_ref[...]

    full, sent = small(
        pair_mid, [((2, C, B), F32), ((3, C, B), BF)], scal, parts[0], *got, down_half
    )

    def choose(s, target, base, blocks):
        down = None
        goal = jnp.full((1, B), target.astype(F32), F32)
        for slot, block in zip(base, blocks):
            term = block * same(goal, slot)
            down = term if down is None else down + term
        return down

    def end_mid(s, full_ref, got_ref, down_ref, x_ref, out_ref, half_ref):
        own = full_ref[0] + got_ref[0].astype(F32)
        other = full_ref[1] + got_ref[1].astype(F32)
        x_ref[...] = own
        position = (s[Y] & 1) * 4 + s[X]
        slot, far = position * 8 + s[ROW], (position ^ 4) * 8 + s[ROW]
        down = choose(
            s,
            s[T1],
            (slot, slot + 64, far, far + 64),
            (own, down_ref[...], other, got_ref[2].astype(F32)),
        )
        out_ref[...] = down
        half_ref[...] = down.astype(BF)

    x_mid, down_low, half = small(
        end_mid,
        [((C, B), F32), ((C, B), F32), ((C, B), BF)],
        scal,
        full,
        swap(sent, "leaf", 4),
        down_mid,
    )

    down_half = half
    parts = transposed(b_low, scal, gather_row(half))
    got = [swap(parts[k], "leaf", k) for k in STEPS]

    coupled = parts[0][0] + sum(g[0].astype(F32) for g in got)
    half = (turned_low - coupled).astype(BF)
    parts = transposed(w_low, scal, gather_row(half), down_half)
    got = [swap(parts[k], "leaf", k) for k in STEPS]

    def end_low(s, own_ref, a, b, c, down_ref, top_ref, mid_ref, sol_ref, leaf_ref):
        own, other = [
            own_ref[j] + a[j].astype(F32) + b[j].astype(F32) + c[j].astype(F32) for j in range(2)
        ]
        sol_ref[0] = top_ref[...].T
        sol_ref[1] = mid_ref[...].T
        sol_ref[2] = own.T
        slot, far = s[X] * 8 + s[ROW], (s[X] ^ 2) * 8 + s[ROW]
        leaf_ref[...] = choose(
            s,
            s[T2],
            (slot, slot + 32, far, far + 32),
            (own, down_ref[...], other, c[2].astype(F32)),
        ).T

    solved, leaf_solution = small(
        end_low,
        [((3, B, C), F32), ((B, C), F32)],
        scal,
        parts[0],
        *got,
        down_low,
        x_top,
        x_mid,
    )
    return (solved, leaf_solution)


def solution(mesh):
    return jax.shard_map(
        shards,
        mesh=mesh,
        in_specs=(
            P(("leaf", "row"), None),
            P(None, ("leaf", "row"), None),
            P(None, "leaf", None, "row", None),
            P(None, "leaf", None, "row", None),
            P(None, "leaf", None, "row", None),
            P(None, "leaf", None, "row", None),
            P(None, "leaf", None, "row", None),
            P(None, ("leaf", "row")),
        ),
        out_specs=(P(None, ("leaf", "row"), None), P(("leaf", "row"), None)),
        check_vma=False,
    )
```

```python
import functools

import jax
import jax.numpy as jnp
from jax import lax
from jax.experimental import pallas as pl
from jax.experimental.pallas import tpu as pltpu
from jax.sharding import PartitionSpec as P

BF = jnp.bfloat16
F32 = jnp.float32
B = 128
C = 256
STEPS = (1, 3, 2)
X, Y, Z, CORE, ROW, T0, T1, T2 = range(8)
SMALL = 8 << 20


def swap(value, axis, mask):
    count = lax.axis_size(axis)
    return lax.ppermute(value, axis, [(i, i ^ mask) for i in range(count)])


def small(body, outs, scal, *ins):
    return pl.pallas_call(
        body,
        out_shape=[jax.ShapeDtypeStruct(*o) for o in outs],
        in_specs=[pl.BlockSpec(memory_space=pltpu.SMEM)]
        + [pl.BlockSpec(memory_space=pltpu.VMEM)] * len(ins),
        out_specs=[pl.BlockSpec(memory_space=pltpu.VMEM)] * len(outs),
        compiler_params=pltpu.CompilerParams(vmem_limit_bytes=SMALL),
        cost_estimate=pl.CostEstimate(flops=1 << 18, bytes_accessed=1 << 19, transcendentals=0),
    )(scal, *ins)


def relay_body(groups, real_ref, imag_ref, out_ref):
    span = C // groups
    shift = span.bit_length() - 1
    target = lax.broadcasted_iota(jnp.int32, (C, C), 0)
    source = lax.broadcasted_iota(jnp.int32, (C, C), 1)
    place = (source == (target & span - 1) * groups + (target >> shift)).astype(BF)

    for chunk in range(B * groups // C):
        rows = slice(chunk * C, (chunk + 1) * C)
        both = jnp.concatenate([real_ref[rows, :], imag_ref[rows, :]], axis=1)
        moved = jnp.dot(place, both, preferred_element_type=F32).astype(BF)
        for p in range(groups):
            out_ref[chunk * span : (chunk + 1) * span, p * C : (p + 1) * C] = moved[
                p * span : (p + 1) * span
            ]


def relay(weights):
    _, rows, groups, _, width = weights.shape
    flat = weights.reshape(2 * rows * groups, width)
    tiles = rows // B
    return pl.pallas_call(
        functools.partial(relay_body, groups),
        grid=(tiles,),
        out_shape=jax.ShapeDtypeStruct((rows, groups * C), BF),
        in_specs=[
            pl.BlockSpec((B * groups, B), lambda t: (t, 0)),
            pl.BlockSpec((B * groups, B), lambda t: (t + tiles, 0)),
        ],
        out_specs=pl.BlockSpec((B, groups * C), lambda t: (t, 0)),
        compiler_params=pltpu.CompilerParams(vmem_limit_bytes=2 * SMALL),
        cost_estimate=pl.CostEstimate(
            flops=4 * rows * groups * C * B, bytes_accessed=8 * rows * groups * B, transcendentals=0
        ),
    )(flat, flat)


def call(body, outs, scal, ins, scratch, flops):
    limit = 2 * ins[0].size + (12 << 20)
    return pl.pallas_call(
        body,
        out_shape=[jax.ShapeDtypeStruct(*o) for o in outs],
        in_specs=[pl.BlockSpec(memory_space=pltpu.SMEM)]
        + [pl.BlockSpec(memory_space=pltpu.VMEM)] * len(ins),
        out_specs=[pl.BlockSpec(memory_space=pltpu.VMEM)] * len(outs),
        scratch_shapes=scratch,
        compiler_params=pltpu.CompilerParams(vmem_limit_bytes=limit),
        cost_estimate=pl.CostEstimate(flops=flops, bytes_accessed=1 << 20, transcendentals=0),
    )(scal, *ins)


def forward(weights, scal, ins, gather, extras=()):
    rows, depth = weights.shape
    count = len(ins)

    def body(s, w_ref, *refs):
        in_refs, out_refs, vec = refs[:count], refs[count:-1], refs[-1]
        def put(index, block):
            start = pl.multiple_of(index * C, C)
            block = block.astype(F32)
            vec[pl.ds(start, B), :] = block.astype(BF)
            vec[pl.ds(start + B, B), :] = jnp.concatenate(
                [-block[:, B:], block[:, :B]], axis=1
            ).astype(BF)

        gather(s, in_refs, out_refs[2:], put)
        swapped = s[CORE] == 1

        @pl.loop(0, 4)
        def _(k):
            start = pl.multiple_of((s[Z] ^ k) * C, C)
            prod = jnp.dot(w_ref[pl.ds(start, C), :], vec[...], preferred_element_type=F32)
            upper, lower = prod[:B], prod[B:]
            out_refs[0][k] = jnp.where(swapped, lower, upper)
            out_refs[1][k] = jnp.where(swapped, upper, lower).astype(BF)

    outs = [((4, B, C), F32), ((4, B, C), BF)] + list(extras)
    return call(
        body, outs, scal, [weights, *ins], [pltpu.VMEM((depth, C), BF)], 2 * rows * depth * C
    )


def transposed(weights, scal, pieces, paired=None, only=None):
    rows, depth = weights.shape
    tiles = depth // (4 * C)
    ins = list(pieces.values()) + ([] if paired is None else [paired])
    keys = list(pieces)
    count = len(ins)
    mask = tiles - 1
    used = count + (4 if only is None else 1)

    def body(s, w_ref, *refs):
        in_refs, out_refs, scratch = refs[:count], refs[count:used], refs[used:]
        vec = scratch[0]
        for (zz, j), ref in zip(keys, in_refs):
            slot = 2 * (s[Z] ^ zz) + (s[CORE] ^ j)
            vec[:, pl.ds(pl.multiple_of(slot * B, B), B)] = ref[...]

        def block(position):
            part = jnp.dot(
                vec[...],
                w_ref[:, pl.ds(pl.multiple_of(position * C, C), C)],
                preferred_element_type=F32,
            )
            return jnp.concatenate(
                [part[:B, :B] - part[B:, B:], part[B:, :B] + part[:B, B:]], axis=0
            )

        if only is not None:

            @pl.loop(0, 4)
            def _(plane):
                j = (plane & 1) * 2 + (plane >> 1)
                value = block((s[Y] ^ j) * 4 + (s[X] ^ only))
                out_refs[0][plane] = value.astype(out_refs[0].dtype)

            return
        acc = scratch[1]

        @pl.loop(0, 4 * tiles, unroll=tiles)
        def _(step):
            k, j = step & 3, step >> 2
            acc[k, j] = block(((s[Y] & mask) ^ j) * 4 + (s[X] ^ k))

        for k in range(4):
            kind = out_refs[k].dtype
            out_refs[k][:tiles] = acc[k].astype(kind)
            if paired is not None:
                out_refs[k][1] = acc[k ^ 2, 0].astype(kind)
        if paired is not None:
            out_refs[2][2] = in_refs[-1][...]

    scratch_shapes = [pltpu.VMEM((C, rows), BF)]
    if only is not None:
        outs = [((4, C, B), BF if only else F32)]
    else:
        scratch_shapes.append(pltpu.VMEM((4, tiles, C, B), F32))
        planes = [1, 1, 1, 1] if paired is None else [2, 2, 3, 2]
        outs = [((tiles * planes[k], C, B), BF if k else F32) for k in range(4)]
    return call(
        body, outs, scal, [weights, *ins], scratch_shapes, 2 * rows * depth * C
    )


def same(goal, slot):
    return (goal == slot.astype(F32)).astype(F32)


def shards(leaf_update, rhs, inv_top, inv_mid, inv_low, couple_mid, couple_low, block_map):
    leaf = lax.axis_index("leaf")
    row = lax.axis_index("row")
    scal = jnp.concatenate(
        [jnp.stack([leaf & 3, leaf >> 2, row >> 1, row & 1, row]).astype(jnp.int32), block_map[:, 0]]
    )

    def reduce_row(own, other):
        other = swap(other, "row", 1)
        parts = {k: own[k] + other[k].astype(F32) for k in range(4)}
        total = parts[0]
        for k in STEPS:
            total = total + swap(parts[k].astype(BF), "row", 2 * k).astype(F32)
        return total

    def gather_row(own):
        pieces = {(0, 0): own}
        for k in STEPS:
            pieces[(k, 0)] = swap(own, "row", 2 * k)
        for k in (0,) + STEPS:
            pieces[(k, 1)] = swap(pieces[(k, 0)], "row", 1)
        return pieces

    def gather_x(value):
        return [value] + [swap(value, "leaf", k) for k in (1, 2, 3)]

    def send(map_ref, leaf_ref, rhs_ref, low_ref, leaf_vmem, rhs_vmem, sems):
        first = pltpu.make_async_copy(leaf_ref, leaf_vmem, sems.at[0])
        second = pltpu.make_async_copy(rhs_ref.at[2], rhs_vmem, sems.at[1])
        first.start()
        second.start()
        low_ref[2 * B :] = jnp.full((16, C), map_ref[2, 0].astype(F32), F32).astype(BF)
        first.wait()
        low_ref[:B] = leaf_vmem[...].astype(BF)
        second.wait()
        low_ref[B : 2 * B] = rhs_vmem[...].astype(BF)

    low = pl.pallas_call(
        send,
        out_shape=jax.ShapeDtypeStruct((2 * B + 16, C), BF),
        in_specs=[
            pl.BlockSpec(memory_space=pltpu.SMEM),
            pl.BlockSpec(memory_space=pl.ANY),
            pl.BlockSpec(memory_space=pl.ANY),
        ],
        out_specs=pl.BlockSpec(memory_space=pltpu.VMEM),
        scratch_shapes=[
            pltpu.VMEM((B, C), F32),
            pltpu.VMEM((B, C), F32),
            pltpu.SemaphoreType.DMA((2,)),
        ],
        compiler_params=pltpu.CompilerParams(vmem_limit_bytes=SMALL),
    )(block_map, leaf_update, rhs)
    got = gather_x(low)
    w_low, b_low, w_mid, b_mid, w_top = [
        relay(w) for w in (inv_low, couple_low, inv_mid, couple_mid, inv_top)
    ]

    def gather_low(s, refs, extra, put):
        goal = [r[2 * B : 2 * B + 16, :].astype(F32)[:1] for r in refs[:4]]
        child = [r[:B, :].astype(F32) for r in refs[:4]]
        slot = (s[X] + 4) * 8 + s[ROW]
        update = same(goal[0], slot) * child[0] + same(goal[2], slot) * child[2]
        extra[0][...] = update
        message = extra[1]
        rhs_ref = refs[4]
        message[:B] = rhs_ref[1].astype(BF)
        message[B : 2 * B] = rhs_ref[0].astype(BF)
        message[2 * B : 2 * B + 16] = jnp.full((16, C), s[T1].astype(F32), F32).astype(BF)
        message[2 * B + 16 : 2 * B + 32] = jnp.full((16, C), s[T0].astype(F32), F32).astype(BF)
        extra[2][:B] = rhs_ref[0].astype(BF)
        extra[2][B:] = jnp.full((16, C), s[T0].astype(F32), F32).astype(BF)
        for k in range(4):
            slot = (s[X] ^ k) * 8 + s[ROW]
            put(
                s[X] ^ k,
                refs[k][B : 2 * B, :].astype(F32)
                + same(goal[k], slot) * child[k]
                + same(goal[k ^ 2], slot) * child[k ^ 2],
            )

    own, others, update, to_y1, to_y3 = forward(
        w_low,
        scal,
        [*got, rhs],
        gather_low,
        extras=[((B, C), F32), ((2 * B + 32, C), BF), ((B + 16, C), BF)],
    )
    from_y1 = swap(to_y1, "leaf", 4)
    from_y3 = swap(to_y3, "leaf", 12)
    from_y2 = swap(to_y3, "leaf", 8)
    y_low = reduce_row(own, others)

    def gather_plain(s, refs, extra, put):
        for k in range(4):
            put(s[X] ^ k, refs[k][...])

    own, others = forward(b_low, scal, gather_x(y_low.astype(BF)), gather_plain)
    children = update - reduce_row(own, others)

    theirs = swap(children.astype(BF), "leaf", 4)

    def extend_mid(s, own_ref, other_ref, rhs_ref, y1_ref, pair_ref, up_ref):
        position = (s[Y] & 1) * 4 + s[X]
        goal_own = jnp.full((1, C), s[T1].astype(F32), F32)
        goal_other = y1_ref[2 * B : 2 * B + 16, :].astype(F32)[:1]

        def landed(slot):
            return same(goal_own, slot) * own_ref[...] + same(goal_other, slot) * other_ref[
                ...
            ].astype(F32)

        slot = position * 8 + s[ROW]
        pair_ref[0] = (rhs_ref[1] + landed(slot)).astype(BF)
        up_ref[...] = landed(slot + 64)
        slot = (position ^ 4) * 8 + s[ROW]
        pair_ref[1] = (y1_ref[:B, :].astype(F32) + landed(slot)).astype(BF)

    pair, update = small(
        extend_mid, [((2, B, C), BF), ((B, C), F32)], scal, children, theirs, rhs, from_y1
    )

    def gather_mid(s, refs, extra, put):
        for k in range(4):
            for j in range(2):
                put(((s[Y] & 1) ^ j) * 4 + (s[X] ^ k), refs[k][j])

    own, others = forward(w_mid, scal, gather_x(pair), gather_mid)
    y_mid = reduce_row(own, others)
    half = y_mid.astype(BF)

    def join(s, a_ref, b_ref, out_ref):
        out_ref[0] = a_ref[...]
        out_ref[1] = b_ref[...]

    (pair,) = small(join, [((2, B, C), BF)], scal, half, swap(half, "leaf", 4))
    own, others = forward(b_mid, scal, gather_x(pair), gather_mid)
    children = update - reduce_row(own, others)
    half = children.astype(BF)

    def flip(s, low_ref, mid_ref, low_out, mid_out):
        low_out[...] = low_ref[...].T
        mid_out[...] = mid_ref[...].T

    turned_low, turned_mid = small(flip, [((C, B), F32)] * 2, scal, y_low, y_mid)

    moved = [swap(half, "leaf", 4 * k) for k in STEPS]

    def extend_top(s, own_ref, m1, m3, m2, rhs_ref, y1_ref, y3_ref, y2_ref, out_ref):
        child = [own_ref[...], m1[...].astype(F32), m2[...].astype(F32), m3[...].astype(F32)]
        base = [rhs_ref[0], y1_ref[B : 2 * B, :], y2_ref[:B, :], y3_ref[:B, :]]
        goal = [
            jnp.full((1, C), s[T0].astype(F32), F32),
            y1_ref[2 * B + 16 : 2 * B + 32, :].astype(F32)[:1],
            y2_ref[B : B + 16, :].astype(F32)[:1],
            y3_ref[B : B + 16, :].astype(F32)[:1],
        ]
        for k in range(4):
            slot = ((s[Y] ^ k) * 4 + s[X]) * 8 + s[ROW]
            out_ref[k] = (
                base[k].astype(F32)
                + same(goal[k], slot) * child[k]
                + same(goal[k ^ 2], slot) * child[k ^ 2]
            ).astype(BF)

    (column,) = small(
        extend_top, [((4, B, C), BF)], scal, children, *moved, rhs, from_y1, from_y3, from_y2
    )

    def gather_top(s, refs, extra, put):
        for k in range(4):
            pl.loop(0, 4)(lambda j, k=k: put((s[Y] ^ j) * 4 + (s[X] ^ k), refs[k][j]))

    own, others = forward(w_top, scal, gather_x(column), gather_top)

    def turn(s, total_ref, out_ref):
        out_ref[...] = total_ref[...].T.astype(BF)

    (half,) = small(turn, [((C, B), BF)], scal, reduce_row(own, others))
    pieces = gather_row(half)
    got = [swap(transposed(w_top, scal, pieces, only=k)[0], "leaf", k) for k in (2, 1, 3)]
    (own,) = transposed(w_top, scal, pieces, only=0)
    b_mid = relay(lax.optimization_barrier((couple_mid, half))[0])
    *got, own, b_mid = lax.optimization_barrier((*got, own, b_mid))

    def total(planes):
        return own[planes] + sum(g[planes].astype(F32) for g in got)

    pair, cross = total(slice(0, 2)), total(slice(2, 4)).astype(BF)
    from_1, from_3 = swap(cross, "leaf", 4), swap(cross, "leaf", 12)
    from_2 = swap(pair.astype(BF), "leaf", 8)
    w_mid = relay(lax.optimization_barrier((inv_mid, half))[0])
    from_1, from_3, from_2, w_mid = lax.optimization_barrier((from_1, from_3, from_2, w_mid))
    from_1, from_3, from_2 = from_1.astype(F32), from_3.astype(F32), from_2.astype(F32)
    x_top = pair[0] + from_2[1] + from_1[0] + from_3[1]
    x_other = pair[1] + from_2[0] + from_1[1] + from_3[0]
    down_mid = jnp.where(block_map[0, 0] == leaf * 8 + row, x_top, x_other)
    half = down_mid.astype(BF)

    down_half = half
    parts = transposed(b_mid, scal, gather_row(half))
    got = [swap(parts[k], "leaf", k) for k in STEPS]
    full, cross = [parts[0][j] + sum(g[j].astype(F32) for g in got) for j in range(2)]
    coupled = full + swap(cross.astype(BF), "leaf", 4).astype(F32)
    half = (turned_mid - coupled).astype(BF)
    parts = transposed(w_mid, scal, gather_row(half))
    got = [swap(parts[k], "leaf", k) for k in STEPS]

    def pair_mid(s, own_ref, a, b, c, down_ref, full_ref, out_ref):
        for j in range(2):
            total = own_ref[j] + a[j].astype(F32) + b[j].astype(F32) + c[j].astype(F32)
            full_ref[j] = total
            out_ref[1 - j] = total.astype(BF)
        out_ref[2] = down_ref[...]

    full, sent = small(
        pair_mid, [((2, C, B), F32), ((3, C, B), BF)], scal, parts[0], *got, down_half
    )

    def choose(s, target, base, blocks):
        down = None
        goal = jnp.full((1, B), target.astype(F32), F32)
        for slot, block in zip(base, blocks):
            term = block * same(goal, slot)
            down = term if down is None else down + term
        return down

    def end_mid(s, full_ref, got_ref, down_ref, x_ref, out_ref, half_ref):
        own = full_ref[0] + got_ref[0].astype(F32)
        other = full_ref[1] + got_ref[1].astype(F32)
        x_ref[...] = own
        position = (s[Y] & 1) * 4 + s[X]
        slot, far = position * 8 + s[ROW], (position ^ 4) * 8 + s[ROW]
        down = choose(
            s,
            s[T1],
            (slot, slot + 64, far, far + 64),
            (own, down_ref[...], other, got_ref[2].astype(F32)),
        )
        out_ref[...] = down
        half_ref[...] = down.astype(BF)

    x_mid, down_low, half = small(
        end_mid,
        [((C, B), F32), ((C, B), F32), ((C, B), BF)],
        scal,
        full,
        swap(sent, "leaf", 4),
        down_mid,
    )

    down_half = half
    parts = transposed(b_low, scal, gather_row(half))
    got = [swap(parts[k], "leaf", k) for k in STEPS]

    coupled = parts[0][0] + sum(g[0].astype(F32) for g in got)
    half = (turned_low - coupled).astype(BF)
    parts = transposed(w_low, scal, gather_row(half), down_half)
    got = [swap(parts[k], "leaf", k) for k in STEPS]

    def end_low(s, own_ref, a, b, c, down_ref, top_ref, mid_ref, sol_ref, leaf_ref):
        own, other = [
            own_ref[j] + a[j].astype(F32) + b[j].astype(F32) + c[j].astype(F32) for j in range(2)
        ]
        sol_ref[0] = top_ref[...].T
        sol_ref[1] = mid_ref[...].T
        sol_ref[2] = own.T
        slot, far = s[X] * 8 + s[ROW], (s[X] ^ 2) * 8 + s[ROW]
        leaf_ref[...] = choose(
            s,
            s[T2],
            (slot, slot + 32, far, far + 32),
            (own, down_ref[...], other, c[2].astype(F32)),
        ).T

    solved, leaf_solution = small(
        end_low,
        [((3, B, C), F32), ((B, C), F32)],
        scal,
        parts[0],
        *got,
        down_low,
        x_top,
        x_mid,
    )
    return (solved, leaf_solution)


def solution(mesh):
    return jax.shard_map(
        shards,
        mesh=mesh,
        in_specs=(
            P(("leaf", "row"), None),
            P(None, ("leaf", "row"), None),
            P(None, "leaf", None, "row", None),
            P(None, "leaf", None, "row", None),
            P(None, "leaf", None, "row", None),
            P(None, "leaf", None, "row", None),
            P(None, "leaf", None, "row", None),
            P(None, ("leaf", "row")),
        ),
        out_specs=(P(None, ("leaf", "row"), None), P(("leaf", "row"), None)),
        check_vma=False,
    )
```

```python
import functools

import jax
import jax.numpy as jnp
from jax import lax
from jax.experimental import pallas as pl
from jax.experimental.pallas import tpu as pltpu
from jax.sharding import PartitionSpec as P

BF = jnp.bfloat16
F32 = jnp.float32
B = 128
C = 256
STEPS = (1, 3, 2)
X, Y, Z, CORE, ROW, T0, T1, T2 = range(8)
SMALL = 8 << 20


def swap(value, axis, mask):
    count = lax.axis_size(axis)
    return lax.ppermute(value, axis, [(i, i ^ mask) for i in range(count)])


def small(body, outs, scal, *ins):
    return pl.pallas_call(
        body,
        out_shape=[jax.ShapeDtypeStruct(*o) for o in outs],
        in_specs=[pl.BlockSpec(memory_space=pltpu.SMEM)]
        + [pl.BlockSpec(memory_space=pltpu.VMEM)] * len(ins),
        out_specs=[pl.BlockSpec(memory_space=pltpu.VMEM)] * len(outs),
        compiler_params=pltpu.CompilerParams(vmem_limit_bytes=SMALL),
        cost_estimate=pl.CostEstimate(flops=1 << 18, bytes_accessed=1 << 19, transcendentals=0),
    )(scal, *ins)


def relay_body(groups, real_ref, imag_ref, out_ref):
    span = C // groups
    shift = span.bit_length() - 1
    target = lax.broadcasted_iota(jnp.int32, (C, C), 0)
    source = lax.broadcasted_iota(jnp.int32, (C, C), 1)
    place = (source == (target & span - 1) * groups + (target >> shift)).astype(BF)

    for chunk in range(B * groups // C):
        rows = slice(chunk * C, (chunk + 1) * C)
        both = jnp.concatenate([real_ref[rows, :], imag_ref[rows, :]], axis=1)
        moved = jnp.dot(place, both, preferred_element_type=F32).astype(BF)
        for p in range(groups):
            out_ref[chunk * span : (chunk + 1) * span, p * C : (p + 1) * C] = moved[
                p * span : (p + 1) * span
            ]


def relay(weights):
    _, rows, groups, _, width = weights.shape
    flat = weights.reshape(2 * rows * groups, width)
    tiles = rows // B
    return pl.pallas_call(
        functools.partial(relay_body, groups),
        grid=(tiles,),
        out_shape=jax.ShapeDtypeStruct((rows, groups * C), BF),
        in_specs=[
            pl.BlockSpec((B * groups, B), lambda t: (t, 0)),
            pl.BlockSpec((B * groups, B), lambda t: (t + tiles, 0)),
        ],
        out_specs=pl.BlockSpec((B, groups * C), lambda t: (t, 0)),
        compiler_params=pltpu.CompilerParams(vmem_limit_bytes=2 * SMALL),
        cost_estimate=pl.CostEstimate(
            flops=4 * rows * groups * C * B, bytes_accessed=8 * rows * groups * B, transcendentals=0
        ),
    )(flat, flat)


def call(body, outs, scal, ins, scratch, flops):
    limit = 2 * ins[0].size + (12 << 20)
    return pl.pallas_call(
        body,
        out_shape=[jax.ShapeDtypeStruct(*o) for o in outs],
        in_specs=[pl.BlockSpec(memory_space=pltpu.SMEM)]
        + [pl.BlockSpec(memory_space=pltpu.VMEM)] * len(ins),
        out_specs=[pl.BlockSpec(memory_space=pltpu.VMEM)] * len(outs),
        scratch_shapes=scratch,
        compiler_params=pltpu.CompilerParams(vmem_limit_bytes=limit),
        cost_estimate=pl.CostEstimate(flops=flops, bytes_accessed=1 << 20, transcendentals=0),
    )(scal, *ins)


def forward(weights, scal, ins, gather, extras=()):
    rows, depth = weights.shape
    count = len(ins)

    def body(s, w_ref, *refs):
        in_refs, out_refs, vec = refs[:count], refs[count:-1], refs[-1]
        def put(index, block):
            start = pl.multiple_of(index * C, C)
            block = block.astype(F32)
            vec[pl.ds(start, B), :] = block.astype(BF)
            vec[pl.ds(start + B, B), :] = jnp.concatenate(
                [-block[:, B:], block[:, :B]], axis=1
            ).astype(BF)

        gather(s, in_refs, out_refs[2:], put)
        swapped = s[CORE] == 1

        @pl.loop(0, 4)
        def _(k):
            start = pl.multiple_of((s[Z] ^ k) * C, C)
            prod = jnp.dot(w_ref[pl.ds(start, C), :], vec[...], preferred_element_type=F32)
            upper, lower = prod[:B], prod[B:]
            out_refs[0][k] = jnp.where(swapped, lower, upper)
            out_refs[1][k] = jnp.where(swapped, upper, lower).astype(BF)

    outs = [((4, B, C), F32), ((4, B, C), BF)] + list(extras)
    return call(
        body, outs, scal, [weights, *ins], [pltpu.VMEM((depth, C), BF)], 2 * rows * depth * C
    )


def transposed(weights, scal, pieces, paired=None, only=None):
    rows, depth = weights.shape
    tiles = depth // (4 * C)
    ins = list(pieces.values()) + ([] if paired is None else [paired])
    keys = list(pieces)
    count = len(ins)
    mask = tiles - 1
    used = count + (4 if only is None else 1)

    def body(s, w_ref, *refs):
        in_refs, out_refs, scratch = refs[:count], refs[count:used], refs[used:]
        vec = scratch[0]
        for (zz, j), ref in zip(keys, in_refs):
            slot = 2 * (s[Z] ^ zz) + (s[CORE] ^ j)
            vec[:, pl.ds(pl.multiple_of(slot * B, B), B)] = ref[...]

        def block(position):
            part = jnp.dot(
                vec[...],
                w_ref[:, pl.ds(pl.multiple_of(position * C, C), C)],
                preferred_element_type=F32,
            )
            return jnp.concatenate(
                [part[:B, :B] - part[B:, B:], part[B:, :B] + part[:B, B:]], axis=0
            )

        if only is not None:

            @pl.loop(0, 4)
            def _(plane):
                j = (plane & 1) * 2 + (plane >> 1)
                value = block((s[Y] ^ j) * 4 + (s[X] ^ only))
                out_refs[0][plane] = value.astype(out_refs[0].dtype)

            return
        acc = scratch[1]

        @pl.loop(0, 4 * tiles, unroll=4)
        def _(step):
            k, j = step & 3, step >> 2
            acc[k, j] = block(((s[Y] & mask) ^ j) * 4 + (s[X] ^ k))

        for k in range(4):
            kind = out_refs[k].dtype
            out_refs[k][:tiles] = acc[k].astype(kind)
            if paired is not None:
                out_refs[k][1] = acc[k ^ 2, 0].astype(kind)
        if paired is not None:
            out_refs[2][2] = in_refs[-1][...]

    scratch_shapes = [pltpu.VMEM((C, rows), BF)]
    if only is not None:
        outs = [((4, C, B), BF if only else F32)]
    else:
        scratch_shapes.append(pltpu.VMEM((4, tiles, C, B), F32))
        planes = [1, 1, 1, 1] if paired is None else [2, 2, 3, 2]
        outs = [((tiles * planes[k], C, B), BF if k else F32) for k in range(4)]
    return call(
        body, outs, scal, [weights, *ins], scratch_shapes, 2 * rows * depth * C
    )


def same(goal, slot):
    return (goal == slot.astype(F32)).astype(F32)


def shards(leaf_update, rhs, inv_top, inv_mid, inv_low, couple_mid, couple_low, block_map):
    leaf = lax.axis_index("leaf")
    row = lax.axis_index("row")
    scal = jnp.concatenate(
        [jnp.stack([leaf & 3, leaf >> 2, row >> 1, row & 1, row]).astype(jnp.int32), block_map[:, 0]]
    )

    def reduce_row(own, other):
        other = swap(other, "row", 1)
        parts = {k: own[k] + other[k].astype(F32) for k in range(4)}
        total = parts[0]
        for k in STEPS:
            total = total + swap(parts[k].astype(BF), "row", 2 * k).astype(F32)
        return total

    def gather_row(own):
        pieces = {(0, 0): own}
        for k in STEPS:
            pieces[(k, 0)] = swap(own, "row", 2 * k)
        for k in (0,) + STEPS:
            pieces[(k, 1)] = swap(pieces[(k, 0)], "row", 1)
        return pieces

    def gather_x(value):
        return [value] + [swap(value, "leaf", k) for k in (1, 2, 3)]

    def send(map_ref, leaf_ref, rhs_ref, low_ref, leaf_vmem, rhs_vmem, sems):
        first = pltpu.make_async_copy(leaf_ref, leaf_vmem, sems.at[0])
        second = pltpu.make_async_copy(rhs_ref.at[2], rhs_vmem, sems.at[1])
        first.start()
        second.start()
        low_ref[2 * B :] = jnp.full((16, C), map_ref[2, 0].astype(F32), F32).astype(BF)
        first.wait()
        low_ref[:B] = leaf_vmem[...].astype(BF)
        second.wait()
        low_ref[B : 2 * B] = rhs_vmem[...].astype(BF)

    low = pl.pallas_call(
        send,
        out_shape=jax.ShapeDtypeStruct((2 * B + 16, C), BF),
        in_specs=[
            pl.BlockSpec(memory_space=pltpu.SMEM),
            pl.BlockSpec(memory_space=pl.ANY),
            pl.BlockSpec(memory_space=pl.ANY),
        ],
        out_specs=pl.BlockSpec(memory_space=pltpu.VMEM),
        scratch_shapes=[
            pltpu.VMEM((B, C), F32),
            pltpu.VMEM((B, C), F32),
            pltpu.SemaphoreType.DMA((2,)),
        ],
        compiler_params=pltpu.CompilerParams(vmem_limit_bytes=SMALL),
    )(block_map, leaf_update, rhs)
    got = gather_x(low)
    w_low, b_low, w_mid, b_mid, w_top = [
        relay(w) for w in (inv_low, couple_low, inv_mid, couple_mid, inv_top)
    ]

    def gather_low(s, refs, extra, put):
        goal = [r[2 * B : 2 * B + 16, :].astype(F32)[:1] for r in refs[:4]]
        child = [r[:B, :].astype(F32) for r in refs[:4]]
        slot = (s[X] + 4) * 8 + s[ROW]
        update = same(goal[0], slot) * child[0] + same(goal[2], slot) * child[2]
        extra[0][...] = update
        message = extra[1]
        rhs_ref = refs[4]
        message[:B] = rhs_ref[1].astype(BF)
        message[B : 2 * B] = rhs_ref[0].astype(BF)
        message[2 * B : 2 * B + 16] = jnp.full((16, C), s[T1].astype(F32), F32).astype(BF)
        message[2 * B + 16 : 2 * B + 32] = jnp.full((16, C), s[T0].astype(F32), F32).astype(BF)
        extra[2][:B] = rhs_ref[0].astype(BF)
        extra[2][B:] = jnp.full((16, C), s[T0].astype(F32), F32).astype(BF)
        for k in range(4):
            slot = (s[X] ^ k) * 8 + s[ROW]
            put(
                s[X] ^ k,
                refs[k][B : 2 * B, :].astype(F32)
                + same(goal[k], slot) * child[k]
                + same(goal[k ^ 2], slot) * child[k ^ 2],
            )

    own, others, update, to_y1, to_y3 = forward(
        w_low,
        scal,
        [*got, rhs],
        gather_low,
        extras=[((B, C), F32), ((2 * B + 32, C), BF), ((B + 16, C), BF)],
    )
    from_y1 = swap(to_y1, "leaf", 4)
    from_y3 = swap(to_y3, "leaf", 12)
    from_y2 = swap(to_y3, "leaf", 8)
    y_low = reduce_row(own, others)

    def gather_plain(s, refs, extra, put):
        for k in range(4):
            put(s[X] ^ k, refs[k][...])

    own, others = forward(b_low, scal, gather_x(y_low.astype(BF)), gather_plain)
    children = update - reduce_row(own, others)

    theirs = swap(children.astype(BF), "leaf", 4)

    def extend_mid(s, own_ref, other_ref, rhs_ref, y1_ref, pair_ref, up_ref):
        position = (s[Y] & 1) * 4 + s[X]
        goal_own = jnp.full((1, C), s[T1].astype(F32), F32)
        goal_other = y1_ref[2 * B : 2 * B + 16, :].astype(F32)[:1]

        def landed(slot):
            return same(goal_own, slot) * own_ref[...] + same(goal_other, slot) * other_ref[
                ...
            ].astype(F32)

        slot = position * 8 + s[ROW]
        pair_ref[0] = (rhs_ref[1] + landed(slot)).astype(BF)
        up_ref[...] = landed(slot + 64)
        slot = (position ^ 4) * 8 + s[ROW]
        pair_ref[1] = (y1_ref[:B, :].astype(F32) + landed(slot)).astype(BF)

    pair, update = small(
        extend_mid, [((2, B, C), BF), ((B, C), F32)], scal, children, theirs, rhs, from_y1
    )

    def gather_mid(s, refs, extra, put):
        for k in range(4):
            for j in range(2):
                put(((s[Y] & 1) ^ j) * 4 + (s[X] ^ k), refs[k][j])

    own, others = forward(w_mid, scal, gather_x(pair), gather_mid)
    y_mid = reduce_row(own, others)
    half = y_mid.astype(BF)

    def join(s, a_ref, b_ref, out_ref):
        out_ref[0] = a_ref[...]
        out_ref[1] = b_ref[...]

    (pair,) = small(join, [((2, B, C), BF)], scal, half, swap(half, "leaf", 4))
    own, others = forward(b_mid, scal, gather_x(pair), gather_mid)
    children = update - reduce_row(own, others)
    half = children.astype(BF)

    def flip(s, low_ref, mid_ref, low_out, mid_out):
        low_out[...] = low_ref[...].T
        mid_out[...] = mid_ref[...].T

    turned_low, turned_mid = small(flip, [((C, B), F32)] * 2, scal, y_low, y_mid)

    moved = [swap(half, "leaf", 4 * k) for k in STEPS]

    def extend_top(s, own_ref, m1, m3, m2, rhs_ref, y1_ref, y3_ref, y2_ref, out_ref):
        child = [own_ref[...], m1[...].astype(F32), m2[...].astype(F32), m3[...].astype(F32)]
        base = [rhs_ref[0], y1_ref[B : 2 * B, :], y2_ref[:B, :], y3_ref[:B, :]]
        goal = [
            jnp.full((1, C), s[T0].astype(F32), F32),
            y1_ref[2 * B + 16 : 2 * B + 32, :].astype(F32)[:1],
            y2_ref[B : B + 16, :].astype(F32)[:1],
            y3_ref[B : B + 16, :].astype(F32)[:1],
        ]
        for k in range(4):
            slot = ((s[Y] ^ k) * 4 + s[X]) * 8 + s[ROW]
            out_ref[k] = (
                base[k].astype(F32)
                + same(goal[k], slot) * child[k]
                + same(goal[k ^ 2], slot) * child[k ^ 2]
            ).astype(BF)

    (column,) = small(
        extend_top, [((4, B, C), BF)], scal, children, *moved, rhs, from_y1, from_y3, from_y2
    )

    def gather_top(s, refs, extra, put):
        for k in range(4):
            pl.loop(0, 4)(lambda j, k=k: put((s[Y] ^ j) * 4 + (s[X] ^ k), refs[k][j]))

    own, others = forward(w_top, scal, gather_x(column), gather_top)

    def turn(s, total_ref, out_ref):
        out_ref[...] = total_ref[...].T.astype(BF)

    (half,) = small(turn, [((C, B), BF)], scal, reduce_row(own, others))
    pieces = gather_row(half)
    got = [swap(transposed(w_top, scal, pieces, only=k)[0], "leaf", k) for k in (2, 1, 3)]
    (own,) = transposed(w_top, scal, pieces, only=0)
    b_mid = relay(lax.optimization_barrier((couple_mid, half))[0])
    *got, own, b_mid = lax.optimization_barrier((*got, own, b_mid))

    def total(planes):
        return own[planes] + sum(g[planes].astype(F32) for g in got)

    pair, cross = total(slice(0, 2)), total(slice(2, 4)).astype(BF)
    from_1, from_3 = swap(cross, "leaf", 4), swap(cross, "leaf", 12)
    from_2 = swap(pair.astype(BF), "leaf", 8)
    w_mid = relay(lax.optimization_barrier((inv_mid, half))[0])
    from_1, from_3, from_2, w_mid = lax.optimization_barrier((from_1, from_3, from_2, w_mid))
    from_1, from_3, from_2 = from_1.astype(F32), from_3.astype(F32), from_2.astype(F32)
    x_top = pair[0] + from_2[1] + from_1[0] + from_3[1]
    x_other = pair[1] + from_2[0] + from_1[1] + from_3[0]
    down_mid = jnp.where(block_map[0, 0] == leaf * 8 + row, x_top, x_other)
    half = down_mid.astype(BF)

    down_half = half
    parts = transposed(b_mid, scal, gather_row(half))
    got = [swap(parts[k], "leaf", k) for k in STEPS]
    full, cross = [parts[0][j] + sum(g[j].astype(F32) for g in got) for j in range(2)]
    coupled = full + swap(cross.astype(BF), "leaf", 4).astype(F32)
    half = (turned_mid - coupled).astype(BF)
    parts = transposed(w_mid, scal, gather_row(half))
    got = [swap(parts[k], "leaf", k) for k in STEPS]

    def pair_mid(s, own_ref, a, b, c, down_ref, full_ref, out_ref):
        for j in range(2):
            total = own_ref[j] + a[j].astype(F32) + b[j].astype(F32) + c[j].astype(F32)
            full_ref[j] = total
            out_ref[1 - j] = total.astype(BF)
        out_ref[2] = down_ref[...]

    full, sent = small(
        pair_mid, [((2, C, B), F32), ((3, C, B), BF)], scal, parts[0], *got, down_half
    )

    def choose(s, target, base, blocks):
        down = None
        goal = jnp.full((1, B), target.astype(F32), F32)
        for slot, block in zip(base, blocks):
            term = block * same(goal, slot)
            down = term if down is None else down + term
        return down

    def end_mid(s, full_ref, got_ref, down_ref, x_ref, out_ref, half_ref):
        own = full_ref[0] + got_ref[0].astype(F32)
        other = full_ref[1] + got_ref[1].astype(F32)
        x_ref[...] = own
        position = (s[Y] & 1) * 4 + s[X]
        slot, far = position * 8 + s[ROW], (position ^ 4) * 8 + s[ROW]
        down = choose(
            s,
            s[T1],
            (slot, slot + 64, far, far + 64),
            (own, down_ref[...], other, got_ref[2].astype(F32)),
        )
        out_ref[...] = down
        half_ref[...] = down.astype(BF)

    x_mid, down_low, half = small(
        end_mid,
        [((C, B), F32), ((C, B), F32), ((C, B), BF)],
        scal,
        full,
        swap(sent, "leaf", 4),
        down_mid,
    )

    down_half = half
    parts = transposed(b_low, scal, gather_row(half))
    got = [swap(parts[k], "leaf", k) for k in STEPS]

    coupled = parts[0][0] + sum(g[0].astype(F32) for g in got)
    half = (turned_low - coupled).astype(BF)
    parts = transposed(w_low, scal, gather_row(half), down_half)
    got = [swap(parts[k], "leaf", k) for k in STEPS]

    def end_low(s, own_ref, a, b, c, down_ref, top_ref, mid_ref, sol_ref, leaf_ref):
        own, other = [
            own_ref[j] + a[j].astype(F32) + b[j].astype(F32) + c[j].astype(F32) for j in range(2)
        ]
        sol_ref[0] = top_ref[...].T
        sol_ref[1] = mid_ref[...].T
        sol_ref[2] = own.T
        slot, far = s[X] * 8 + s[ROW], (s[X] ^ 2) * 8 + s[ROW]
        leaf_ref[...] = choose(
            s,
            s[T2],
            (slot, slot + 32, far, far + 32),
            (own, down_ref[...], other, c[2].astype(F32)),
        ).T

    solved, leaf_solution = small(
        end_low,
        [((3, B, C), F32), ((B, C), F32)],
        scal,
        parts[0],
        *got,
        down_low,
        x_top,
        x_mid,
    )
    return (solved, leaf_solution)


def solution(mesh):
    return jax.shard_map(
        shards,
        mesh=mesh,
        in_specs=(
            P(("leaf", "row"), None),
            P(None, ("leaf", "row"), None),
            P(None, "leaf", None, "row", None),
            P(None, "leaf", None, "row", None),
            P(None, "leaf", None, "row", None),
            P(None, "leaf", None, "row", None),
            P(None, "leaf", None, "row", None),
            P(None, ("leaf", "row")),
        ),
        out_specs=(P(None, ("leaf", "row"), None), P(("leaf", "row"), None)),
        check_vma=False,
    )
```
